32 devices in a mesh: seq: 8 (over z, x), batch: 4 (over y, core).
Axes of the slice: x: 2, y: 2, z: 4, core: 2. Of those that a mesh axis runs over, the one named last changes fastest.
Arguments:
- inputs: bfloat16 [1024, 4, 2048], P('seq', 'batch'), may hold values from -6 to 6
- positions: int32 [1024, 4], P('seq', 'batch'), may hold values from 0 to 1023, as said below
- ln1_gain: float32 [2048], replicated, may hold values from 0.5 to 1.5
- ln1_bias: float32 [2048], replicated, may hold values from -1.75 to 1.75
- w_qkv: bfloat16 [2048, 6144], P('seq'), may hold values from -0.125 to 0.125
- qkv_bias: float32 [6144], replicated, may hold values from -1.75 to 1.75
- w_out: bfloat16 [2048, 2048], P('seq'), may hold values from -0.75 to 0.75
- ln2_gain: float32 [2048], replicated, may hold values from 0.5 to 1.5
- ln2_bias: float32 [2048], replicated, may hold values from -1.75 to 1.75
- w_gate: bfloat16 [2048, 5632], P(None, 'seq'), may hold values from -0.125 to 0.125
- w_up: bfloat16 [2048, 5632], P(None, 'seq'), may hold values from -0.125 to 0.125
- w_down: bfloat16 [5632, 2048], P('seq'), may hold values from -0.078125 to 0.078125
- cotangent: bfloat16 [1024, 4, 2048], P('seq', 'batch'), may hold values from -6 to 6
Outputs:
- output: bfloat16 [1024, 4, 2048], P('seq', 'batch')
- grad_input: float32 [1024, 4, 2048], P('seq', 'batch')
- grad_ln1_gain: float32 [2048], replicated
- grad_ln1_bias: float32 [2048], replicated
- grad_w_qkv: float32 [2048, 6144], P('seq')
- grad_qkv_bias: float32 [6144], replicated
- grad_w_out: float32 [2048, 2048], P('seq')
- grad_ln2_gain: float32 [2048], replicated
- grad_ln2_bias: float32 [2048], replicated
- grad_w_gate: float32 [2048, 5632], P(None, 'seq')
- grad_w_up: float32 [2048, 5632], P(None, 'seq')
- grad_w_down: float32 [5632, 2048], P('seq')
The draws below stay inside these ranges and needn't reach their ends.
Inputs may be any that keep to these rules, and one draw needn't show every extreme that they name: positions[t, r] is 0 where a document of packed row r begins (always at t = 0) and positions[t - 1, r] + 1 elsewhere.
All inputs are finite; a program needn't handle non-finite values.
Results may differ from the reference program's by a relative error of at most 0.019.
Values may be sent and summed in bfloat16 or wider, within the bound.
No kernel may reach another device: no remote copies, remote signals or barrier semaphores. Data moves between devices by JAX's collectives and lax.ppermute only.
A program may use at most 512 MiB of HBM per device.

```python
import jax
import jax.numpy as jnp
from jax import lax

D = 2048
HEADS = 32
FF = 5632
HEAD_DIM = 64
ROT = 16
ROW_TOK_DEV = 128
ROWS_DEV = 1
KEY_BLOCK = 512
LENGTH = 1024
ROWS = 4


def draw_positions(key, part):
    key = jax.random.fold_in(key, 11)
    subkeys = jax.random.split(key, 5)
    position_index = jnp.arange(LENGTH, dtype=jnp.int32)[:, None]
    breaks = (jax.random.randint(subkeys[0], (LENGTH, ROWS), 0, max(LENGTH // 4, 2)) == 0).astype(jnp.int32)
    chosen = jax.random.randint(subkeys[1], (), 0, ROWS_DEV)
    row_index = jnp.arange(ROWS, dtype=jnp.int32)[None, :]
    full_row = jax.random.randint(subkeys[4], (), 0, ROWS)
    whole = row_index == full_row
    spanning = (row_index % ROWS_DEV == chosen) | whole
    doc_begin = jax.random.randint(subkeys[2], (1, ROWS), 0, ROW_TOK_DEV)
    finish = jax.random.randint(subkeys[3], (1, ROWS), LENGTH - ROW_TOK_DEV + 1, LENGTH + 1)
    doc_begin = jnp.where(whole, 0, doc_begin)
    finish = jnp.where(whole, LENGTH, finish)
    inside = spanning & (position_index > doc_begin) & (position_index < finish)
    edge_flags = spanning & ((position_index == doc_begin) | (position_index == finish))
    breaks = jnp.where(inside, 0, breaks)
    breaks = jnp.where(edge_flags, 1, breaks)
    breaks = jnp.where(position_index == 0, 1, breaks)
    starts = lax.cummax(jnp.where(breaks == 1, position_index, 0), axis=0)
    return (position_index - starts).astype(jnp.int32)


def levels(key, dims, cuts, smallest, high):
    def one(dim, parts):
        heights = jax.random.uniform(jax.random.fold_in(jax.random.fold_in(key, 6), dim), (parts,), jnp.float32, smallest / len(cuts), high / len(cuts))
        return jnp.repeat(jnp.exp(heights), dims[dim] // parts).reshape((-1,) + (1,) * (len(dims) - dim - 1))

    gain = one(*cuts[0])
    for cut in cuts[1:]:
        gain = gain * one(*cut)
    return gain


def normal_values(rng, extent, spread, reach, shards=(), kind=jnp.bfloat16):
    factor_of = levels(rng, extent, shards, -0.22, 0.18) if shards else 1.0
    entries = jax.random.normal(rng, extent, jnp.float32) * spread * factor_of
    return jnp.minimum(jnp.maximum(entries, -reach), reach).astype(kind)


def setup_inputs(seed: int = 0) -> dict:
    streams_of = jax.random.split(jax.random.key(seed), 14)
    return {
        "inputs": normal_values(streams_of[0], (LENGTH, ROWS, D), 1.0, 6.0, ((0, 8), (1, 4))),
        "positions": draw_positions(jax.random.fold_in(streams_of[13], 71), 0),
        "ln1_gain": jnp.clip(1.0 + 0.1 * jax.random.normal(streams_of[2], (D,), jnp.float32), 0.5, 1.5),
        "ln1_bias": normal_values(streams_of[3], (D,), 0.3, 1.75, (), jnp.float32),
        "w_qkv": normal_values(streams_of[4], (D, 3 * D), D ** -0.5, 0.125, ((0, 8),)),
        "qkv_bias": normal_values(streams_of[5], (3 * D,), 0.3, 1.75, (), jnp.float32),
        "w_out": normal_values(streams_of[6], (D, D), (D // 32) ** -0.5, 0.75, ((0, 8),)),
        "ln2_gain": jnp.clip(1.0 + 0.1 * jax.random.normal(streams_of[7], (D,), jnp.float32), 0.5, 1.5),
        "ln2_bias": normal_values(streams_of[8], (D,), 0.3, 1.75, (), jnp.float32),
        "w_gate": normal_values(streams_of[9], (D, FF), D ** -0.5, 0.125, ((1, 8),)),
        "w_up": normal_values(streams_of[10], (D, FF), D ** -0.5, 0.125, ((1, 8),)),
        "w_down": normal_values(streams_of[11], (FF, D), FF ** -0.5, 0.078125, ((0, 8),)),
        "cotangent": normal_values(streams_of[12], (LENGTH, ROWS, D), 1.0, 6.0, ((0, 8), (1, 4))),
    }


top_precision = lax.Precision.HIGHEST
eps_norm = 1e-05
theta_base = 10000.0
masked_score = -1e+30

@jax.custom_vjp
def low(v):
    return lax.optimization_barrier(v.astype(jnp.bfloat16)).astype(jnp.float32)

@jax.custom_vjp
def low_back(v):
    return v

def low_keep(v):
    return (low(v), None)

def low_pass(kept, grad):
    return (grad,)

def back_keep(v):
    return (v, None)

def back_low(kept, grad):
    return (low(grad),)
low.defvjp(low_keep, low_pass)
low_back.defvjp(back_keep, back_low)

def layer_norm(values, gain_vector, shift_vector):
    mean_value = lax.optimization_barrier(jnp.mean(values, axis=-1, keepdims=True))
    centred = values - mean_value
    inverse = lax.rsqrt(lax.optimization_barrier(jnp.mean(centred * centred, axis=-1, keepdims=True)) + eps_norm)
    return centred * inverse * gain_vector + shift_vector

def rotate_heads(values, row_positions):
    half_dim = ROT // 2
    frequency = theta_base ** (-(jnp.arange(half_dim, dtype=jnp.float32) * 2.0 / ROT))
    angles = row_positions.astype(jnp.float32)[:, None] * frequency
    cosine_table = jnp.cos(angles)[:, None, :]
    sine_table = jnp.sin(angles)[:, None, :]
    first_half = values[..., :half_dim]
    second_half = values[..., half_dim:ROT]
    return jnp.concatenate([first_half * cosine_table - second_half * sine_table, second_half * cosine_table + first_half * sine_table, values[..., ROT:]], axis=-1)

def attend(queries, key_rows, value_rows, row_positions):
    length = queries.shape[0]
    blocks = length // KEY_BLOCK
    score_scale = HEAD_DIM ** (-0.5)
    key_place = jnp.arange(length, dtype=jnp.int32)
    first_place = key_place - row_positions.astype(jnp.int32)

    @jax.checkpoint
    def one_block(block_args):
        query_block, query_place, doc_first = block_args
        scores = low_back(jnp.einsum('qhd,khd->hqk', query_block, key_rows, precision=top_precision) * score_scale)
        visible = (key_place[None, :] <= query_place[:, None]) & (key_place[None, :] >= doc_first[:, None])
        scores = jnp.where(visible[None], scores, masked_score)
        row_max = lax.optimization_barrier(jnp.max(scores, axis=-1, keepdims=True))
        weights = jnp.exp(scores - row_max)
        probability = low(weights / lax.optimization_barrier(jnp.sum(weights, axis=-1, keepdims=True)))
        return jnp.einsum('hqk,khd->qhd', probability, value_rows, precision=top_precision)
    mixed_blocks = lax.map(one_block, (queries.reshape(blocks, KEY_BLOCK, HEADS, HEAD_DIM), key_place.reshape(blocks, KEY_BLOCK), first_place.reshape(blocks, KEY_BLOCK)))
    return mixed_blocks.reshape(length, HEADS, HEAD_DIM)

def forward_row(row_input, row_positions, ln1_gain, ln1_bias, w_qkv, qkv_bias, w_out, ln2_gain, ln2_bias, w_gate, w_up, w_down):
    length = row_input.shape[0]
    normed = low(layer_norm(row_input, ln1_gain, ln1_bias))
    joined = low_back(jnp.dot(normed, w_qkv, precision=top_precision) + qkv_bias)
    joined = joined.reshape(length, 3, HEADS, HEAD_DIM)
    queries = low(rotate_heads(joined[:, 0], row_positions))
    key_rows = low(rotate_heads(joined[:, 1], row_positions))
    value_rows = low(joined[:, 2])
    attended = attend(queries, key_rows, value_rows, row_positions)
    mixed = low(low_back(attended.reshape(length, D)))
    middle = row_input + low_back(jnp.dot(mixed, w_out, precision=top_precision))
    normed_two = low(layer_norm(middle, ln2_gain, ln2_bias))
    gate_proj = low_back(jnp.dot(normed_two, w_gate, precision=top_precision))
    up_proj = low_back(jnp.dot(normed_two, w_up, precision=top_precision))
    hidden = low(jax.nn.silu(gate_proj) * up_proj)
    return middle + jnp.dot(hidden, w_down, precision=top_precision)

def reference(inputs, positions, ln1_gain, ln1_bias, w_qkv, qkv_bias, w_out, ln2_gain, ln2_bias, w_gate, w_up, w_down, cotangent):
    weights_f32 = (ln1_gain.astype(jnp.float32), ln1_bias.astype(jnp.float32), w_qkv.astype(jnp.float32), qkv_bias.astype(jnp.float32), w_out.astype(jnp.float32), ln2_gain.astype(jnp.float32), ln2_bias.astype(jnp.float32), w_gate.astype(jnp.float32), w_up.astype(jnp.float32), w_down.astype(jnp.float32))
    row_inputs = jnp.moveaxis(inputs.astype(jnp.float32), 1, 0)
    row_places = jnp.moveaxis(positions, 1, 0)
    row_cotangents = jnp.moveaxis(cotangent.astype(jnp.float32), 1, 0)

    def one_row(summed, row_args):
        row_input, row_positions, row_cotangent = row_args

        def run(value_in, gain_one, bias_one, qkv_matrix, qkv_shift, out_matrix, gain_two, bias_two, gate_matrix, up_matrix, down_matrix):
            return forward_row(value_in, row_positions, gain_one, bias_one, qkv_matrix, qkv_shift, out_matrix, gain_two, bias_two, gate_matrix, up_matrix, down_matrix)
        row_output, pullback = jax.vjp(run, row_input, weights_f32[0], weights_f32[1], weights_f32[2], weights_f32[3], weights_f32[4], weights_f32[5], weights_f32[6], weights_f32[7], weights_f32[8], weights_f32[9])
        gradients = pullback(row_cotangent)
        summed = tuple((running + gradient for running, gradient in zip(summed, gradients[1:])))
        return (summed, (row_output, gradients[0]))
    zero_sums = tuple((jnp.zeros_like(weight) for weight in weights_f32))
    summed, (row_outputs, row_grads) = lax.scan(one_row, zero_sums, (row_inputs, row_places, row_cotangents))
    output = jnp.moveaxis(row_outputs, 0, 1).astype(jnp.bfloat16)
    grad_input = jnp.moveaxis(row_grads, 0, 1)
    return (output, grad_input, summed[0], summed[1], summed[2], summed[3], summed[4], summed[5], summed[6], summed[7], summed[8], summed[9])
```

```python
import functools

import jax
import jax.numpy as jnp
from jax import lax
from jax.experimental import pallas as pl
from jax.experimental.pallas import tpu as pltpu
from jax.sharding import PartitionSpec as P

HEADS = 32
HEAD_DIM = 64
ROT = 16
BLOCK = 128
TILE = 256

eps_norm = 1e-05
theta_base = 10000.0
masked_score = -1e30
bf16 = jnp.bfloat16
f32 = jnp.float32


def ring_order(n):
    return [0, 2, 4, 6, 7, 5, 3, 1] if n == 8 else list(range(n))


class Ring:
    def __init__(self, axis):
        self.axis = axis
        self.n = n = lax.axis_size(axis)
        order = ring_order(n)
        self.ahead = [(order[i], order[(i + 1) % n]) for i in range(n)]
        self.behind = [(b, a) for a, b in self.ahead]
        place = jnp.array([order.index(i) for i in range(n)], jnp.int32)
        offset = (place - place[lax.axis_index(axis)]) % n
        half = n // 2
        self.slot = jnp.where(
            offset == 0, 0, jnp.where(offset == half, n - 1, jnp.where(offset < half, 2 * offset, 2 * (n - offset) - 1))
        ).astype(jnp.int32)

    def up(self, v):
        return lax.ppermute(v, self.axis, self.ahead)

    def down(self, v):
        return lax.ppermute(v, self.axis, self.behind)

    def gather(self, v):
        half = v.shape[0] // 2
        blocks, first, second = [v], v, v
        for _ in range(1, self.n // 2):
            first, second = self.up(first), self.down(second)
            blocks += [first, second]
        return blocks + [jnp.concatenate([self.up(first[:half]), self.down(second[half:])])]

    def scatter(self, parts):
        far = parts[-1]().astype(bf16)
        half = far.shape[0] // 2
        first, second = self.up(far[:half]), self.down(far[half:])
        for d in range(self.n // 2 - 1, 0, -1):
            first, second = first.astype(f32), second.astype(f32)
            if d == self.n // 2 - 1:
                first = jnp.pad(first, ((0, half), (0, 0)))
                second = jnp.pad(second, ((half, 0), (0, 0)))
            first = self.up((parts[2 * d]() + first).astype(bf16))
            second = self.down((parts[2 * d - 1]() + second).astype(bf16))
        return parts[0]() + first.astype(f32) + second.astype(f32)


def swap(v, axis, bit):
    n = lax.axis_size(axis)
    return lax.ppermute(v, axis, [(i, i ^ bit) for i in range(n)])


def bits_of(n):
    return [1 << i for i in range(n.bit_length() - 1)]


def batch_scatter(v, axis="batch"):
    n = lax.axis_size(axis)
    me = lax.axis_index(axis)
    rest = v
    for bit in bits_of(n):
        pairs = rest.reshape((rest.shape[0] // 2, 2) + rest.shape[1:])
        mine = (me // bit) % 2
        keep = lax.dynamic_index_in_dim(pairs, mine, 1, keepdims=False)
        give = lax.dynamic_index_in_dim(pairs, 1 - mine, 1, keepdims=False)
        rest = keep.astype(f32) + swap(give.astype(bf16), axis, bit).astype(f32)
    return rest[0]


def batch_gather(v, axis="batch"):
    n = lax.axis_size(axis)
    me = lax.axis_index(axis)
    held = v[None]
    for bit in reversed(bits_of(n)):
        other = swap(held, axis, bit)
        low = (me // bit) % 2 == 0
        pair = jnp.stack([jnp.where(low, held, other), jnp.where(low, other, held)], 1)
        held = pair.reshape((-1,) + v.shape)
    return held


def sum_all(v, axes):
    for axis in axes:
        for bit in bits_of(lax.axis_size(axis)):
            v = v + swap(v, axis, bit)
    return v


def norm_parts(values, gain_vector, shift_vector):
    mean_value = jnp.mean(values, axis=-1, keepdims=True)
    centred = values - mean_value
    inverse = lax.rsqrt(jnp.mean(centred * centred, axis=-1, keepdims=True) + eps_norm)
    unit_value = centred * inverse
    return (unit_value * gain_vector + shift_vector, unit_value, inverse)


def norm_back(gradient, unit_value, inverse, gain_vector):
    scaled = gradient * gain_vector
    return inverse * (
        scaled
        - jnp.mean(scaled, axis=-1, keepdims=True)
        - unit_value * jnp.mean(scaled * unit_value, axis=-1, keepdims=True)
    )


def dot(a, b):
    return jnp.dot(a, b, preferred_element_type=f32)


def dot_rows(a, b):
    return lax.dot_general(a, b, (((0,), (0,)), ((), ())), preferred_element_type=f32)


def dot_last(a, b):
    return lax.dot_general(a, b, (((1,), (1,)), ((), ())), preferred_element_type=f32)


def rotary_tables(positions, width):
    half = ROT // 2
    frequency = theta_base ** (-(jnp.arange(half, dtype=f32) * 2.0 / ROT))
    angles = positions.astype(f32)[:, None] * frequency
    cosine, sine = jnp.cos(angles), jnp.sin(angles)
    rest = jnp.zeros((positions.shape[0], HEAD_DIM - ROT), f32)
    own = jnp.concatenate([cosine, cosine, rest + 1.0], 1)
    other = jnp.concatenate([-sine, sine, rest], 1)
    return jnp.tile(own, (1, width // HEAD_DIM)), jnp.tile(other, (1, width // HEAD_DIM))


def rotate_lanes(x, own, other):
    half = ROT // 2
    width = x.shape[1]
    lane = lax.broadcasted_iota(jnp.int32, x.shape, 1) % HEAD_DIM
    partner = jnp.where(lane < half, pltpu.roll(x, width - half, 1), pltpu.roll(x, half, 1))
    return x * own + partner * other


def visible_to(first_ref, start, keys, tile):
    key = lax.broadcasted_iota(jnp.int32, (keys, tile), 0)
    query = lax.broadcasted_iota(jnp.int32, (keys, tile), 1) + start
    return (key <= query) & (key >= first_ref[0:1, start : start + tile])


def head_rows(x, h):
    if x.shape[0] == HEAD_DIM:
        return x
    row = lax.broadcasted_iota(jnp.int32, x.shape, 0) // HEAD_DIM
    return jnp.where(row == h, x, jnp.zeros_like(x))


def head_lanes(x, h):
    if x.shape[1] == HEAD_DIM:
        return x
    lane = lax.broadcasted_iota(jnp.int32, x.shape, 1) // HEAD_DIM
    return jnp.where(lane == h, x, jnp.zeros_like(x))


def attend_kernel(slot_ref, joined_ref, own_ref, other_ref, first_ref, qkv_ref, mixed_ref, lse_ref, q_t, v_t):
    length, width3 = joined_ref.shape
    width = width3 // 3
    heads = width // HEAD_DIM
    scale = HEAD_DIM ** (-0.5)
    for j in range(length // BLOCK):
        rows = pl.ds(pl.multiple_of(slot_ref[j] * BLOCK, BLOCK), BLOCK)
        here = slice(j * BLOCK, (j + 1) * BLOCK)
        x = joined_ref[rows, :]
        own, other = own_ref[here, :], other_ref[here, :]
        q = rotate_lanes(x[:, :width], own, other).astype(bf16)
        k = rotate_lanes(x[:, width : 2 * width], own, other).astype(bf16)
        v = x[:, 2 * width :].astype(bf16)
        qkv_ref[0, here, :] = q
        qkv_ref[1, here, :] = k
        qkv_ref[2, here, :] = v
        q_t[:, here] = (q.astype(f32) * scale).T.astype(bf16)
        v_t[:, here] = v.astype(f32).T.astype(bf16)
    lse_ref[...] = jnp.zeros_like(lse_ref)
    tile = min(TILE, length)
    for start in range(0, length, tile):
        keys = start + tile
        seen = visible_to(first_ref, start, keys, tile)
        queries = q_t[:, start : start + tile]
        outs = []
        for h in range(heads):
            scores = dot(qkv_ref[1, :keys, :], head_rows(queries, h))
            scores = jnp.where(seen, scores, masked_score)
            top = jnp.max(scores, axis=0, keepdims=True)
            weights = jnp.exp(scores - top)
            total = jnp.sum(weights, axis=0, keepdims=True)
            lse_ref[h : h + 1, start : start + tile] = top + jnp.log(total)
            prob = (weights * (1.0 / total)).astype(bf16)
            outs.append(dot(v_t[h * HEAD_DIM : (h + 1) * HEAD_DIM, :keys], prob))
        out = jnp.concatenate(outs, 0).T.astype(bf16)
        for i in range(tile // BLOCK):
            rows = pl.ds(pl.multiple_of(slot_ref[start // BLOCK + i] * BLOCK, BLOCK), BLOCK)
            mixed_ref[rows, :] = out[i * BLOCK : (i + 1) * BLOCK]


def attend_back_kernel(
    slot_ref, qkv_ref, mixed_ref, grad_ref, lse_ref, own_ref, other_ref, first_ref, out_ref,
    q_t, k_t, g_t, grads, delta, dk, dv,
):
    length, width = mixed_ref.shape
    heads = width // HEAD_DIM
    scale = HEAD_DIM ** (-0.5)
    for j in range(length // BLOCK):
        rows = pl.ds(pl.multiple_of(slot_ref[j] * BLOCK, BLOCK), BLOCK)
        here = slice(j * BLOCK, (j + 1) * BLOCK)
        g = grad_ref[rows, :]
        g_flip = g.astype(f32).T
        o_flip = mixed_ref[rows, :].astype(f32).T
        both = g_flip * o_flip
        for h in range(heads):
            delta[h : h + 1, here] = jnp.sum(both[h * HEAD_DIM : (h + 1) * HEAD_DIM], axis=0, keepdims=True)
        grads[here, :] = g
        g_t[:, here] = g_flip.astype(bf16)
        q_t[:, here] = (qkv_ref[0, here, :].astype(f32) * scale).T.astype(bf16)
        k_t[:, here] = qkv_ref[1, here, :].astype(f32).T.astype(bf16)
    dk[...] = jnp.zeros_like(dk)
    dv[...] = jnp.zeros_like(dv)
    tile = min(TILE, length)
    for start in range(0, length, tile):
        keys = start + tile
        here = slice(start, keys)
        seen = visible_to(first_ref, start, keys, tile)
        q_tile, g_tile = q_t[:, here], g_t[:, here]
        q_rows, g_rows = qkv_ref[0, here, :], grads[here, :]
        dq, dk_sum, dv_sum = [], dk[:keys, :], dv[:keys, :]
        for h in range(heads):
            scores = dot(qkv_ref[1, :keys, :], head_rows(q_tile, h))
            prob = jnp.where(seen, jnp.exp(scores - lse_ref[h : h + 1, here]), 0.0)
            grad_prob = dot(qkv_ref[2, :keys, :], head_rows(g_tile, h))
            grad_score = (prob * (grad_prob - delta[h : h + 1, here])).astype(bf16)
            dv_sum += dot(prob.astype(bf16), head_lanes(g_rows, h))
            dk_sum += dot(grad_score, head_lanes(q_rows, h))
            dq.append(dot(k_t[h * HEAD_DIM : (h + 1) * HEAD_DIM, :keys], grad_score))
        dk[:keys, :] = dk_sum
        dv[:keys, :] = dv_sum
        dq = jnp.concatenate(dq, 0).T * scale
        for i in range(tile // BLOCK):
            at = slice(i * BLOCK, (i + 1) * BLOCK)
            place = slice(start + i * BLOCK, start + (i + 1) * BLOCK)
            rows = pl.ds(pl.multiple_of(slot_ref[start // BLOCK + i] * BLOCK, BLOCK), BLOCK)
            turned = rotate_lanes(dq[at], own_ref[place, :], -other_ref[place, :])
            out_ref[rows, :width] = turned.astype(bf16)
    for j in range(length // BLOCK):
        rows = pl.ds(pl.multiple_of(slot_ref[j] * BLOCK, BLOCK), BLOCK)
        here = slice(j * BLOCK, (j + 1) * BLOCK)
        turned = rotate_lanes(dk[here, :] * scale, own_ref[here, :], -other_ref[here, :])
        out_ref[rows, width : 2 * width] = turned.astype(bf16)
        out_ref[rows, 2 * width :] = dv[here, :].astype(bf16)


def in_vmem(count):
    return [pl.BlockSpec(memory_space=pltpu.SMEM)] + [pl.BlockSpec(memory_space=pltpu.VMEM)] * count


def attend(slot, joined, own, other, first):
    length, width3 = joined.shape
    width = width3 // 3
    rows = max(8, width // HEAD_DIM)
    return pl.pallas_call(
        attend_kernel,
        out_shape=(
            jax.ShapeDtypeStruct((3, length, width), bf16),
            jax.ShapeDtypeStruct((length, width), bf16),
            jax.ShapeDtypeStruct((rows, length), f32),
        ),
        in_specs=in_vmem(4),
        out_specs=(pl.BlockSpec(memory_space=pltpu.VMEM),) * 3,
        scratch_shapes=[pltpu.VMEM((width, length), bf16), pltpu.VMEM((width, length), bf16)],
        compiler_params=pltpu.CompilerParams(vmem_limit_bytes=48 * 2**20),
        name="attend",
    )(slot, joined, own, other, first)


def attend_back(slot, qkv, mixed, grad, lse, own, other, first):
    length, width = mixed.shape
    rows = lse.shape[0]
    return pl.pallas_call(
        attend_back_kernel,
        out_shape=jax.ShapeDtypeStruct((length, 3 * width), bf16),
        in_specs=in_vmem(7),
        out_specs=pl.BlockSpec(memory_space=pltpu.VMEM),
        scratch_shapes=[
            pltpu.VMEM((width, length), bf16),
            pltpu.VMEM((width, length), bf16),
            pltpu.VMEM((width, length), bf16),
            pltpu.VMEM((length, width), bf16),
            pltpu.VMEM((rows, length), f32),
            pltpu.VMEM((length, width), f32),
            pltpu.VMEM((length, width), f32),
        ],
        compiler_params=pltpu.CompilerParams(vmem_limit_bytes=48 * 2**20),
        name="attend_back",
    )(slot, qkv, mixed, grad, lse, own, other, first)


def on_device(
    inputs, positions, ln1_gain, ln1_bias, w_qkv, qkv_bias, w_out, ln2_gain, ln2_bias, w_gate, w_up, w_down, cotangent
):
    n, rows = lax.axis_size("seq"), lax.axis_size("batch")
    me, my_row = lax.axis_index("seq"), lax.axis_index("batch")
    ring = Ring("seq")
    tokens, model = inputs.shape[0], inputs.shape[2]
    length = tokens * n
    width = model // n
    depth = w_qkv.shape[0]
    x = inputs.reshape(tokens, model).astype(f32)
    cot = cotangent.reshape(tokens, model)

    share = depth // rows
    mine = lax.dynamic_slice_in_dim(w_qkv, my_row * share, share, 0).reshape(share, 3, n, width)
    mine = mine.transpose(2, 0, 1, 3).reshape(n, share, 3 * width)
    fetched = lax.all_to_all(mine, "seq", split_axis=0, concat_axis=0, tiled=True)
    w_heads = batch_gather(fetched).transpose(1, 0, 2, 3).reshape(model, 3 * width)
    bias_heads = lax.dynamic_index_in_dim(qkv_bias.reshape(3, n, width), me, 1, keepdims=False).reshape(3 * width)

    places = lax.all_gather(positions.reshape(tokens), "seq", axis=0, tiled=True)
    own, other = rotary_tables(places, width)
    first = (jnp.arange(length, dtype=jnp.int32) - places)[None]

    normed, unit_one, inverse_one = norm_parts(x, ln1_gain, ln1_bias)
    normed_blocks = ring.gather(normed.astype(bf16))
    joined = jnp.concatenate([dot(b, w_heads) + bias_heads for b in normed_blocks])
    qkv, mixed, lse = attend(ring.slot, joined, own, other, first)

    def block(v, i):
        return v[i * tokens : (i + 1) * tokens]

    branch = ring.scatter([functools.partial(lambda i: dot(block(mixed, i), w_out), i) for i in range(n)])
    middle = x + branch
    normed_two, unit_two, inverse_two = norm_parts(middle, ln2_gain, ln2_bias)
    cot_blocks = ring.gather(cot)
    two_blocks = ring.gather(normed_two.astype(bf16))

    hidden, grad_gate, grad_up = [], [], []
    for b, c in zip(two_blocks, cot_blocks, strict=True):
        gate, up = dot(b, w_gate), dot(b, w_up)
        grad_hidden = dot_last(c, w_down)
        sigmoid = jax.nn.sigmoid(gate)
        silu = gate * sigmoid
        hidden.append((silu * up).astype(bf16))
        grad_gate.append((grad_hidden * up * sigmoid * (1.0 + gate * (1.0 - sigmoid))).astype(bf16))
        grad_up.append((grad_hidden * silu).astype(bf16))

    grad_two = ring.scatter(
        [
            functools.partial(lambda i: dot_last(grad_gate[i], w_gate) + dot_last(grad_up[i], w_up), i)
            for i in range(n)
        ]
    )
    out_sum = ring.scatter([functools.partial(lambda i: dot(hidden[i], w_down), i) for i in range(n)])
    output = (middle + out_sum).astype(bf16)

    all_two, all_cot = jnp.concatenate(two_blocks), jnp.concatenate(cot_blocks)
    grad_w_down = dot_rows(jnp.concatenate(hidden), all_cot).astype(bf16)
    grad_w_gate = dot_rows(all_two, jnp.concatenate(grad_gate)).astype(bf16)
    grad_w_up = dot_rows(all_two, jnp.concatenate(grad_up)).astype(bf16)

    def over_rows(v):
        parts = v.reshape((rows, v.shape[0] // rows) + v.shape[1:])
        return batch_gather(batch_scatter(parts).astype(bf16)).reshape(v.shape).astype(f32)

    grad_w_down, grad_w_gate, grad_w_up = over_rows(grad_w_down), over_rows(grad_w_gate), over_rows(grad_w_up)

    grad_middle = cot.astype(f32) + norm_back(grad_two, unit_two, inverse_two, ln2_gain)
    gain_two_grad = jnp.sum(grad_two * unit_two, axis=0)
    bias_two_grad = jnp.sum(grad_two, axis=0)
    branch_blocks = ring.gather(grad_middle.astype(bf16))
    grad_mixed = jnp.concatenate([dot_last(b, w_out).astype(bf16) for b in branch_blocks])
    grad_w_out = over_rows(dot_rows(mixed, jnp.concatenate(branch_blocks)).astype(bf16))

    grad_joined = attend_back(ring.slot, qkv, mixed, grad_mixed, lse, own, other, first)
    bias_heads_grad = jnp.sum(grad_joined.astype(f32), axis=0)
    grad_one = ring.scatter(
        [functools.partial(lambda i: dot_last(block(grad_joined, i), w_heads), i) for i in range(n)]
    )
    grad_input = grad_middle + norm_back(grad_one, unit_one, inverse_one, ln1_gain)
    gain_one_grad = jnp.sum(grad_one * unit_one, axis=0)
    bias_one_grad = jnp.sum(grad_one, axis=0)

    grad_w_heads = dot_rows(jnp.concatenate(normed_blocks), grad_joined).astype(bf16)
    parts = grad_w_heads.reshape(n, rows, share, 3 * width).transpose(1, 0, 2, 3)
    mine = batch_scatter(parts).astype(bf16)
    mine = lax.all_to_all(mine, "seq", split_axis=0, concat_axis=0, tiled=True)
    mine = mine.reshape(n, share, 3, width).transpose(1, 2, 0, 3).reshape(share, 3 * model)
    grad_w_qkv = batch_gather(mine).reshape(depth, 3 * model).astype(f32)

    bias_all = jnp.zeros((3, n, width), f32)
    bias_all = lax.dynamic_update_slice(bias_all, bias_heads_grad.reshape(3, 1, width), (0, me, 0)).reshape(-1)
    vectors = jnp.concatenate([gain_one_grad, bias_one_grad, gain_two_grad, bias_two_grad, bias_all]).reshape(-1, 128)
    vectors = sum_all(vectors, ("seq", "batch")).reshape(-1)
    gain_one_sum, bias_one_sum, gain_two_sum, bias_two_sum, qkv_bias_sum = jnp.split(
        vectors, [model, 2 * model, 3 * model, 4 * model]
    )
    return (
        output.reshape(tokens, 1, model),
        grad_input.reshape(tokens, 1, model),
        gain_one_sum,
        bias_one_sum,
        grad_w_qkv,
        qkv_bias_sum,
        grad_w_out,
        gain_two_sum,
        bias_two_sum,
        grad_w_gate,
        grad_w_up,
        grad_w_down,
    )


def solution(mesh):
    token, shard, column, whole = P("seq", "batch", None), P("seq", None), P(None, "seq"), P()
    in_specs = (
        token, P("seq", "batch"), whole, whole, shard, whole, shard, whole, whole, column, column, shard, token
    )
    out_specs = (token, token, whole, whole, shard, whole, shard, whole, whole, column, column, shard)
    return jax.shard_map(on_device, mesh=mesh, in_specs=in_specs, out_specs=out_specs, check_vma=False)
```

```python
import functools

import jax
import jax.numpy as jnp
import numpy as np
from jax import lax
from jax.experimental import pallas as pl
from jax.experimental.pallas import tpu as pltpu
from jax.sharding import PartitionSpec as P

HEADS = 32
HEAD_DIM = 64
ROT = 16
BLOCK = 128
TILE = 256

eps_norm = 1e-05
theta_base = 10000.0
masked_score = -1e30
bf16 = jnp.bfloat16
f32 = jnp.float32


def ring_order(n):
    return [0, 2, 4, 6, 7, 5, 3, 1] if n == 8 else list(range(n))


class Ring:
    def __init__(self, axis):
        self.axis = axis
        self.n = n = lax.axis_size(axis)
        order = ring_order(n)
        self.ahead = [(order[i], order[(i + 1) % n]) for i in range(n)]
        self.behind = [(b, a) for a, b in self.ahead]
        half = n // 2
        table = np.zeros((n, 2 * n), np.int32)
        for i, device in enumerate(order):
            for slot in range(n):
                step = -((slot + 1) // 2) if slot % 2 and slot < n - 1 else slot // 2 if slot < n - 1 else half
                natural = order[(i + step) % n]
                table[device, natural], table[device, n + slot] = slot, natural
        self.table = jnp.asarray(table)

    def up(self, v):
        return lax.ppermute(v, self.axis, self.ahead)

    def down(self, v):
        return lax.ppermute(v, self.axis, self.behind)


class Gather:
    def __init__(self, ring, line, v):
        self.ring, self.line, self.d = ring, line, 1
        self.half = v.shape[0] // 2
        self.blocks = [v]
        self.flying = ring.up(v), ring.down(v)

    def step(self):
        got = self.line(lambda *v: v, *self.flying)
        self.blocks += got
        self.d += 1
        last = self.ring.n // 2
        if self.d < last:
            self.flying = self.ring.up(got[0]), self.ring.down(got[1])
        elif self.d == last:
            top, bottom = halves(*got)
            self.flying = self.ring.up(top), self.ring.down(bottom)
        return got


class Line:
    def __init__(self):
        self.last = ()

    def __call__(self, work, *given):
        given, _ = lax.optimization_barrier((given, self.last))
        out = work(*given)
        self.last = out
        return out


def swap(v, axis, bit):
    n = lax.axis_size(axis)
    return lax.ppermute(v, axis, [(i, i ^ bit) for i in range(n)])


def bits_of(n):
    return [1 << i for i in range(n.bit_length() - 1)]


def after(v, *others):
    return lax.optimization_barrier((v, *others))[0]


class Places:
    def __init__(self, model):
        u = functools.partial(jnp.asarray, dtype=jnp.uint32)
        seq, batch = lax.axis_index("seq").astype(jnp.uint32), lax.axis_index("batch").astype(jnp.uint32)
        core, y = batch % u(2), batch // u(2)
        self.seq = seq
        self.quarter = [batch ^ u(k) for k in range(4)]
        self.order = [(q % u(2)) * u(2) + q // u(2) for q in self.quarter]
        self.starts = {
            (name, size): which * u(size)
            for name, which in (("core", core), ("across", u(1) - core), ("y", y), ("other", u(1) - y))
            for size in (model // 2, model // 4)
        }
        for name in ("y", "other"):
            self.starts["mine " + name, model // 4] = (
                self.starts["core", model // 2] + self.starts[name, model // 4]
            )
        self.column_place = jnp.stack([(core * u(2) + y) ^ u(k) for k in range(4)]).astype(jnp.int32)
        self.row_place = jnp.stack([batch ^ u(k) for k in (0, 2, 1, 3)]).astype(jnp.int32)
        peers = [seq ^ u(k) for k in range(lax.axis_size("seq"))]
        self.peers = jnp.stack([batch, *peers]).astype(jnp.int32)

    def scalars(self):
        return [self.seq, *self.quarter, *self.order, *self.starts.values(), self.column_place, self.row_place, self.peers]

    def tied(self, scalars):
        self.seq, self.quarter, self.order = scalars[0], scalars[1:5], scalars[5:9]
        self.starts = dict(zip(self.starts, scalars[9:-3], strict=True))
        self.column_place, self.row_place, self.peers = scalars[-3:]

    def side(self, v, which, parts=2):
        size = v.shape[1] // parts
        return lax.dynamic_slice(v, (jnp.uint32(0), self.starts[which, size]), (v.shape[0], size))


def pick(v, index, axis):
    starts = [jnp.uint32(0)] * v.ndim
    starts[axis] = index
    sizes = list(v.shape)
    sizes[axis] = 1
    return lax.squeeze(lax.dynamic_slice(v, starts, sizes), (axis,))


def norm_parts(values, gain_vector, shift_vector):
    mean_value = jnp.mean(values, axis=-1, keepdims=True)
    centred = values - mean_value
    inverse = lax.rsqrt(jnp.mean(centred * centred, axis=-1, keepdims=True) + eps_norm)
    unit_value = centred * inverse
    return (unit_value * gain_vector + shift_vector, unit_value, inverse)


def norm_back(gradient, unit_value, inverse, gain_vector):
    scaled = gradient * gain_vector
    return inverse * (
        scaled
        - jnp.mean(scaled, axis=-1, keepdims=True)
        - unit_value * jnp.mean(scaled * unit_value, axis=-1, keepdims=True)
    )


def dot(a, b):
    return jnp.dot(a, b, preferred_element_type=f32)


def dot_rows(a, b):
    return lax.dot_general(a, b, (((0,), (0,)), ((), ())), preferred_element_type=f32)


def dot_last(a, b):
    return lax.dot_general(a, b, (((1,), (1,)), ((), ())), preferred_element_type=f32)


def rotary_waves(positions):
    half = ROT // 2
    frequency = theta_base ** (-(jnp.arange(half, dtype=f32) * 2.0 / ROT))
    angles = frequency[:, None] * positions
    return jnp.concatenate([jnp.cos(angles), jnp.sin(angles)], 0)


def fill_table(table_ref, waves_ref):
    half = ROT // 2
    for start in range(0, table_ref.shape[0], BLOCK):
        here = slice(start, start + BLOCK)
        cosine, sine = waves_ref[:half, here], waves_ref[half:, here]
        rest = jnp.zeros((HEAD_DIM - ROT, BLOCK), f32)
        table_ref[here, :] = jnp.concatenate([cosine, cosine, rest + 1.0, -sine, sine, rest], 0).T


def spread_table(table, width):
    own, other = table[:, :HEAD_DIM], table[:, HEAD_DIM:]
    return (jnp.concatenate([v] * (width // HEAD_DIM), 1) for v in (own, other))


def rotate_lanes(x, own, other):
    half = ROT // 2
    width = x.shape[1]
    lane = lax.broadcasted_iota(jnp.int32, x.shape, 1) % HEAD_DIM
    partner = jnp.where(lane < half, pltpu.roll(x, width - half, 1), pltpu.roll(x, half, 1))
    return x * own + partner * other


def visible_to(first_ref, start, keys, tile):
    key = lax.broadcasted_iota(jnp.int32, (keys, tile), 0)
    query = lax.broadcasted_iota(jnp.int32, (keys, tile), 1) + start
    return (key <= query) & (key >= first_ref[0:1, start : start + tile])


def head_rows(x, h):
    if x.shape[0] == HEAD_DIM:
        return x
    row = lax.broadcasted_iota(jnp.int32, x.shape, 0) // HEAD_DIM
    return jnp.where(row == h, x, jnp.zeros_like(x))


def head_lanes(x, h):
    if x.shape[1] == HEAD_DIM:
        return x
    lane = lax.broadcasted_iota(jnp.int32, x.shape, 1) // HEAD_DIM
    return jnp.where(lane == h, x, jnp.zeros_like(x))


def row_list(refs):
    return jnp.concatenate([ref[...] for ref in refs], 0)


def at_block(ref, index):
    return pl.ds(pl.multiple_of(ref[index] * BLOCK, BLOCK), BLOCK)


def grouped(refs, rows):
    groups, held, count = [], [], 0
    for ref in refs:
        held.append(ref)
        count += ref.shape[0]
        if count == rows:
            groups.append(held)
            held, count = [], 0
    return groups


def attend_kernel(blocks, maps_ref, *refs):
    block_refs, refs = refs[:blocks], refs[blocks:]
    piece_refs, refs = refs[:4], refs[4:]
    bias_ref, waves_ref, first_ref, all_ref, qkv_ref, mixed_ref, lse_ref, q_t, v_t, table_ref = refs
    fill_table(table_ref, waves_ref)
    length, width = mixed_ref.shape
    heads = width // HEAD_DIM
    blocks = length // BLOCK
    scale = HEAD_DIM ** (-0.5)
    tile = min(TILE, length)
    depth = piece_refs[0].shape[0]
    for i, group in enumerate(grouped(block_refs, tile)):
        rows = row_list(group)
        all_ref[i * tile : (i + 1) * tile, :] = rows
        x = bias_ref[...] + sum(dot(rows[:, g * depth : (g + 1) * depth], p[...]) for g, p in enumerate(piece_refs))
        for k in range(tile // BLOCK):
            here = at_block(maps_ref, blocks + i * (tile // BLOCK) + k)
            part = x[k * BLOCK : (k + 1) * BLOCK]
            own, other = spread_table(table_ref[here, :], width)
            q = rotate_lanes(part[:, :width], own, other).astype(bf16)
            v = part[:, 2 * width :].astype(bf16)
            qkv_ref[0, here, :] = q
            qkv_ref[1, here, :] = rotate_lanes(part[:, width : 2 * width], own, other).astype(bf16)
            qkv_ref[2, here, :] = v
            q_t[:, here] = (q.astype(f32) * scale).T.astype(bf16)
            v_t[:, here] = v.astype(f32).T.astype(bf16)
    lse_ref[...] = jnp.zeros_like(lse_ref)
    for start in range(0, length, tile):
        keys = start + tile
        seen = visible_to(first_ref, start, keys, tile)
        queries = q_t[:, start : start + tile]
        outs = []
        for h in range(heads):
            scores = dot(qkv_ref[1, :keys, :], head_rows(queries, h))
            scores = jnp.where(seen, scores, masked_score)
            top = jnp.max(scores, axis=0, keepdims=True)
            weights = jnp.exp(scores - top)
            total = jnp.sum(weights, axis=0, keepdims=True)
            lse_ref[h : h + 1, start : start + tile] = top + jnp.log(total)
            prob = (weights * (1.0 / total)).astype(bf16)
            outs.append(dot(v_t[h * HEAD_DIM : (h + 1) * HEAD_DIM, :keys], prob))
        out = jnp.concatenate(outs, 0).T.astype(bf16)
        for i in range(tile // BLOCK):
            mixed_ref[at_block(maps_ref, start // BLOCK + i), :] = out[i * BLOCK : (i + 1) * BLOCK]


def attend_back_kernel(blocks, maps_ref, *refs):
    block_refs, refs = refs[:blocks], refs[blocks:]
    w_ref, qkv_ref, mixed_ref, lse_ref, waves_ref, first_ref, out_ref, outer_ref = refs[:8]
    q_t, k_t, g_t, grads, delta, dk, dv, table_ref = refs[8:]
    fill_table(table_ref, waves_ref)
    length, width = mixed_ref.shape
    blocks = length // BLOCK
    heads = width // HEAD_DIM
    scale = HEAD_DIM ** (-0.5)
    tile = min(TILE, length)
    for i, group in enumerate(grouped(block_refs, tile)):
        rows = dot_last(row_list(group), w_ref[...]).astype(bf16)
        for k in range(tile // BLOCK):
            s = i * (tile // BLOCK) + k
            here = at_block(maps_ref, blocks + s)
            g = rows[k * BLOCK : (k + 1) * BLOCK]
            g_flip = g.astype(f32).T
            both = g_flip * mixed_ref[s * BLOCK : (s + 1) * BLOCK, :].astype(f32).T
            for h in range(heads):
                delta[h : h + 1, here] = jnp.sum(both[h * HEAD_DIM : (h + 1) * HEAD_DIM], axis=0, keepdims=True)
            grads[here, :] = g
            g_t[:, here] = g_flip.astype(bf16)
    for j in range(blocks):
        here = slice(j * BLOCK, (j + 1) * BLOCK)
        q_t[:, here] = (qkv_ref[0, here, :].astype(f32) * scale).T.astype(bf16)
        k_t[:, here] = qkv_ref[1, here, :].astype(f32).T.astype(bf16)
    dk[...] = jnp.zeros_like(dk)
    dv[...] = jnp.zeros_like(dv)
    for start in range(0, length, tile):
        keys = start + tile
        here = slice(start, keys)
        seen = visible_to(first_ref, start, keys, tile)
        q_tile, g_tile = q_t[:, here], g_t[:, here]
        q_rows, g_rows = qkv_ref[0, here, :], grads[here, :]
        dq, dk_sum, dv_sum = [], dk[:keys, :], dv[:keys, :]
        for h in range(heads):
            scores = dot(qkv_ref[1, :keys, :], head_rows(q_tile, h))
            prob = jnp.where(seen, jnp.exp(scores - lse_ref[h : h + 1, here]), 0.0)
            grad_prob = dot(qkv_ref[2, :keys, :], head_rows(g_tile, h))
            grad_score = (prob * (grad_prob - delta[h : h + 1, here])).astype(bf16)
            dv_sum += dot(prob.astype(bf16), head_lanes(g_rows, h))
            dk_sum += dot(grad_score, head_lanes(q_rows, h))
            dq.append(dot(k_t[h * HEAD_DIM : (h + 1) * HEAD_DIM, :keys], grad_score))
        dk[:keys, :] = dk_sum
        dv[:keys, :] = dv_sum
        dq = jnp.concatenate(dq, 0).T * scale
        for i in range(tile // BLOCK):
            at = slice(i * BLOCK, (i + 1) * BLOCK)
            place = slice(start + i * BLOCK, start + (i + 1) * BLOCK)
            own, other = spread_table(table_ref[place, :], width)
            turned = rotate_lanes(dq[at], own, -other)
            out_ref[at_block(maps_ref, start // BLOCK + i), :width] = turned.astype(bf16)
    for j in range(blocks):
        rows = at_block(maps_ref, j)
        here = slice(j * BLOCK, (j + 1) * BLOCK)
        own, other = spread_table(table_ref[here, :], width)
        turned = rotate_lanes(dk[here, :] * scale, own, -other)
        out_ref[rows, width : 2 * width] = turned.astype(bf16)
        out_ref[rows, 2 * width :] = dv[here, :].astype(bf16)
    for start in range(0, outer_ref.shape[1], 512):
        columns = slice(start, start + 512)
        outer_ref[:, columns] = sum(
            dot_rows(
                mixed_ref[i * tile : (i + 1) * tile, :], jnp.concatenate([ref[:, columns] for ref in group], 0)
            )
            for i, group in enumerate(grouped(block_refs, tile))
        )


def once(kernel, name, megabytes, out_shape, scratch, *given, maps=None):
    vmem = pl.BlockSpec(memory_space=pltpu.VMEM)
    many = isinstance(out_shape, (tuple, list))
    small = [] if maps is None else [maps]
    return pl.pallas_call(
        kernel,
        out_shape=out_shape,
        in_specs=[pl.BlockSpec(memory_space=pltpu.SMEM)] * len(small) + [vmem] * len(given),
        out_specs=[vmem] * len(out_shape) if many else vmem,
        scratch_shapes=scratch,
        compiler_params=pltpu.CompilerParams(vmem_limit_bytes=megabytes * 2**20),
        cost_estimate=BRIEF,
        name=name,
    )(*small, *given)


BRIEF = pl.CostEstimate(flops=1, bytes_accessed=1, transcendentals=0)


def attend(maps, blocks, pieces, bias, waves, first):
    length, width = waves.shape[1], pieces[0].shape[1] // 3
    return once(
        functools.partial(attend_kernel, len(blocks)),
        "attend",
        16 if length <= 1024 else 40,
        (
            jax.ShapeDtypeStruct((length, blocks[0].shape[1]), bf16),
            jax.ShapeDtypeStruct((3, length, width), bf16),
            jax.ShapeDtypeStruct((length, width), bf16),
            jax.ShapeDtypeStruct((max(8, width // HEAD_DIM), length), f32),
        ),
        [pltpu.VMEM((width, length), bf16), pltpu.VMEM((width, length), bf16), pltpu.VMEM((length, 2 * HEAD_DIM), f32)],
        *blocks,
        *pieces,
        bias,
        waves,
        first,
        maps=maps,
    )


def attend_back(maps, blocks, w_out, qkv, mixed, lse, waves, first):
    length, width = mixed.shape
    return once(
        functools.partial(attend_back_kernel, len(blocks)),
        "attend_back",
        16 if length <= 1024 else 40,
        (
            jax.ShapeDtypeStruct((length, 3 * width), bf16),
            jax.ShapeDtypeStruct((width, blocks[0].shape[1]), f32),
        ),
        [
            pltpu.VMEM((width, length), bf16),
            pltpu.VMEM((width, length), bf16),
            pltpu.VMEM((width, length), bf16),
            pltpu.VMEM((length, width), bf16),
            pltpu.VMEM((lse.shape[0], length), f32),
            pltpu.VMEM((length, width), f32),
            pltpu.VMEM((length, width), f32),
            pltpu.VMEM((length, 2 * HEAD_DIM), f32),
        ],
        *blocks,
        w_out,
        qkv,
        mixed,
        lse,
        waves,
        first,
        maps=maps,
    )


def exchange(blocks):
    return [blocks[0]] + [swap(v, "seq", k) for k, v in enumerate(blocks) if k]


def local(kernel, name, out_shape, smem, given, anywhere=0, scratch=()):
    vmem = pl.BlockSpec(memory_space=pltpu.VMEM)
    many = isinstance(out_shape, (tuple, list))
    return pl.pallas_call(
        kernel,
        out_shape=out_shape,
        in_specs=[pl.BlockSpec(memory_space=pltpu.SMEM)]
        + [pl.BlockSpec(memory_space=pl.ANY)] * anywhere
        + [vmem] * (len(given) - anywhere),
        out_specs=[vmem] * len(out_shape) if many else vmem,
        scratch_shapes=list(scratch),
        compiler_params=pltpu.CompilerParams(vmem_limit_bytes=6 * 2**20),
        cost_estimate=BRIEF,
        name=name,
    )(smem, *given)


def cut_kernel(peers_ref, w_ref, place_ref, *refs):
    outs, semaphores = refs[:-1], refs[-1]
    extra, width = place_ref.shape[0], place_ref.shape[1] // 3
    share, model = outs[0].shape[0] - extra, w_ref.shape[1] // 3
    rows = pl.ds(pl.multiple_of(peers_ref[0] * share, share), share)
    copies = []
    for k, out in enumerate(outs):
        for c in range(3):
            columns = pl.ds(pl.multiple_of(c * model + peers_ref[1 + k] * width, BLOCK), width)
            copies.append(
                pltpu.make_async_copy(
                    w_ref.at[rows, columns],
                    out.at[pl.ds(0, share), pl.ds(c * width, width)],
                    semaphores.at[3 * k + c],
                )
            )
            copies[-1].start()
    for out in outs:
        out[share:, :] = place_ref[...]
    for copy in copies:
        copy.wait()


def cut(at, w, place, n):
    extra, columns = place.shape
    share, width = w.shape[0] // 4, columns // 3
    if width % BLOCK:
        mine = pick(w.reshape(4, share, 3 * width * n), at.quarter[0], 0).reshape(share, 3, n, width)
        mine = [pick(mine, at.seq ^ jnp.uint32(k), 2).reshape(share, columns) for k in range(n)]
        return [jnp.concatenate([v, place]) for v in mine]
    out = jax.ShapeDtypeStruct((share + extra, columns), bf16)
    return local(cut_kernel, "cut", [out] * n, at.peers, (w, place), 1, [pltpu.SemaphoreType.DMA((3 * n,))])


def stack_kernel(peers_ref, *refs):
    ins, (piece_ref, place_ref) = refs[:-2], refs[-2:]
    share = piece_ref.shape[0] // len(ins)
    tokens = place_ref.shape[1] // len(ins)
    for k, ref in enumerate(ins):
        peer = peers_ref[1 + k]
        piece_ref[pl.ds(pl.multiple_of(peer * share, share), share), :] = ref[:share, :]
        place = ref[share:, :tokens].astype(f32)
        place_ref[:, pl.ds(pl.multiple_of(peer * tokens, tokens), tokens)] = place[0:1] * 64.0 + place[1:2]


def stacked(at, blocks, extra, tokens):
    n, (rows, columns) = len(blocks), blocks[0].shape
    shapes = [
        jax.ShapeDtypeStruct((n * (rows - extra), columns), bf16),
        jax.ShapeDtypeStruct((1, n * tokens), f32),
    ]
    return local(stack_kernel, "stacked", shapes, at.peers, blocks)


def in_plain_order(x, number, n):
    share = x.shape[1] // (4 * n)
    order = [(q % 2) * 2 + q // 2 for q in (number ^ j for j in range(4))]
    starts = [order[j] * n * share + s * share for s in range(n) for j in range(4)]
    return jnp.concatenate([x[:, start : start + share] for start in starts], 1)


def last_back_kernel(n, peers_ref, term_ref, first_ref, second_ref, unit_ref, inverse_ref, gain_ref, middle_ref, out_ref):
    total = term_ref[...] + first_ref[...].astype(f32) + second_ref[...].astype(f32)
    for number in range(4):

        @pl.when(peers_ref[0] == number)
        def _(number=number):
            out_ref[...] = in_plain_order(total, number, n)

    out_ref[...] = middle_ref[...] + norm_back(out_ref[...], unit_ref[...], inverse_ref[...], gain_ref[...])


def beside_kernel(in_ref, out_ref):
    n, _, columns = in_ref.shape
    width = columns // 3
    for k in range(n):
        for c in range(3):
            start = (c * n + k) * width
            out_ref[:, start : start + width] = in_ref[k, :, c * width : (c + 1) * width]


def beside(v):
    n, rows, columns = v.shape
    return once(beside_kernel, "beside", 6, jax.ShapeDtypeStruct((rows, n * columns), bf16), [], v)


def halves_kernel(first_ref, second_ref, top_ref, bottom_ref):
    half = top_ref.shape[0]
    top_ref[...] = first_ref[:half, :]
    bottom_ref[...] = second_ref[half:, :]


def halves(first, second):
    half = jax.ShapeDtypeStruct((first.shape[0] // 2, first.shape[1]), first.dtype)
    vmem = pl.BlockSpec(memory_space=pltpu.VMEM)
    return pl.pallas_call(
        halves_kernel,
        out_shape=(half, half),
        in_specs=[vmem] * 2,
        out_specs=(vmem,) * 2,
        compiler_params=pltpu.CompilerParams(vmem_limit_bytes=4 * 2**20),
        cost_estimate=BRIEF,
        name="halves",
    )(first, second)


def hidden_kernel(at, tokens, cots, held, *refs):
    token_refs, refs = refs[:tokens], refs[tokens:]
    cot_refs, refs = refs[:cots], refs[cots:]
    gate_ref, up_ref, down_ref, refs = refs[0], refs[1], refs[2], refs[3 + held :]
    results, scratch, semaphores = refs[:5], refs[5:10], refs[10]
    rows = scratch[0].shape[0]
    copies = [
        pltpu.make_async_copy(v, out.at[pl.ds(at * rows, rows), :], semaphores.at[i])
        for i, (v, out) in enumerate(zip(scratch, results, strict=True))
    ]
    two, cot, hidden, grad_gate, grad_up = scratch
    two[...] = row_list(token_refs)
    copies[0].start()
    cot[...] = row_list(cot_refs)
    copies[1].start()
    units = gate_ref.shape[0]
    for start in range(0, units, TILE):
        here = slice(start, min(start + TILE, units))
        gate, up = dot_last(two[...], gate_ref[here, :]), dot_last(two[...], up_ref[here, :])
        grad_hidden = dot_last(cot[...], down_ref[here, :])
        sigmoid = 1.0 / (1.0 + jnp.exp(-gate))
        silu = gate * sigmoid
        hidden[:, here] = (silu * up).astype(bf16)
        grad_gate[:, here] = (grad_hidden * up * sigmoid * (1.0 + gate * (1.0 - sigmoid))).astype(bf16)
        grad_up[:, here] = (grad_hidden * silu).astype(bf16)
    for copy in copies[2:]:
        copy.start()
    for copy in copies:
        copy.wait()


def hidden_pair(at, pairs, tokens, cots, gate_rows, up_rows, w_down, held):
    rows = sum(b.shape[0] for b in tokens)
    units, model = gate_rows.shape
    widths = (model, model, units, units, units)
    first = len(tokens) + len(cots) + 3
    hbm = pl.BlockSpec(memory_space=pltpu.HBM)
    return pl.pallas_call(
        functools.partial(hidden_kernel, at, len(tokens), len(cots), len(held)),
        out_shape=[jax.ShapeDtypeStruct((rows * pairs, w), bf16) for w in widths],
        in_specs=[pl.BlockSpec(memory_space=pltpu.VMEM)] * first + [hbm] * len(held),
        out_specs=[hbm] * 5,
        scratch_shapes=[pltpu.VMEM((rows, w), bf16) for w in widths] + [pltpu.SemaphoreType.DMA((5,))],
        input_output_aliases={first + i: i for i in range(len(held))},
        compiler_params=pltpu.CompilerParams(vmem_limit_bytes=12 * 2**20),
        cost_estimate=BRIEF,
        name="hidden_pair",
    )(*tokens, *cots, gate_rows, up_rows, w_down, *held)


def place_kernel(at_ref, *refs):
    out_ref = refs[-1]
    for i, ref in enumerate(refs[:-1]):

        @pl.when(pl.program_id(0) == i)
        def _(ref=ref):
            out_ref[...] = ref[...].astype(f32)


def placed(at, pieces, axis):
    shape = list(pieces[0].shape)
    total = list(shape)
    total[axis] *= len(pieces)
    return pl.pallas_call(
        place_kernel,
        out_shape=jax.ShapeDtypeStruct(tuple(total), f32),
        grid_spec=pltpu.PrefetchScalarGridSpec(
            num_scalar_prefetch=1,
            grid=(len(pieces),),
            in_specs=[pl.BlockSpec(tuple(shape), lambda i, at: (0, 0)) for _ in pieces],
            out_specs=pl.BlockSpec(tuple(shape), lambda i, at: (0, at[i]) if axis else (at[i], 0)),
        ),
        compiler_params=pltpu.CompilerParams(vmem_limit_bytes=16 * 2**20),
        cost_estimate=BRIEF,
        name="placed",
    )(at, *pieces)


def on_device(
    inputs, positions, ln1_gain, ln1_bias, w_qkv, qkv_bias, w_out, ln2_gain, ln2_bias, w_gate, w_up, w_down, cotangent
):
    n = lax.axis_size("seq")
    ring = Ring("seq")
    line = Line()
    tokens, model = inputs.shape[0], inputs.shape[2]
    length = tokens * n
    pairs = n // 2
    width = model // n
    depth = w_qkv.shape[0]
    share = depth // 4
    x = inputs.reshape(tokens, model).astype(f32)
    cot = cotangent.reshape(tokens, model)
    gate_rows, up_rows = w_gate.T, w_up.T
    others = (0, 2, 1, 3)
    at = Places(model)
    at.tied(line(lambda *v: v, *at.scalars()))

    def other_y(v):
        return swap(v, "batch", 2)

    def other_core(v):
        return swap(v, "batch", 1)

    place = positions.reshape(tokens)
    extra = 8
    place = jnp.stack([place // 64, place % 64]).astype(bf16)
    place = jnp.pad(place, ((0, extra - 2), (0, 3 * width - tokens)))
    fetched = exchange(line(lambda w, place: cut(at, w, place, n), w_qkv, place))
    bias_heads = line(lambda v: pick(v.reshape(3, n, width), at.seq, 1).reshape(1, 3 * width), qkv_bias)

    def first_norm(x):
        normed, unit, inverse = norm_parts(x, ln1_gain, ln1_bias)
        normed = normed.astype(bf16).reshape(tokens, n, 4, share)
        normed = [pick(normed, at.quarter[k], 2).reshape(tokens, -1) for k in others]
        return jnp.concatenate(normed, 1), unit, inverse

    normed, unit_one, inverse_one = line(first_norm, x)
    normed_blocks = Gather(ring, line, normed)

    piece, places = line(lambda *v: stacked(at, v, extra, tokens), *fetched)
    piece_y, piece_core = other_y(piece), other_core(piece)
    normed_blocks.step()

    def take(places, maps):
        maps = pick(maps, at.seq, 0)
        first = jnp.arange(length, dtype=jnp.int32)[None] - places.astype(jnp.int32)
        return maps, rotary_waves(places), first

    normed_blocks.step()
    ring.maps, waves, seen_from = line(take, places, ring.table)
    piece_core = line(lambda v: v, piece_core)
    for _ in range(pairs - 3):
        normed_blocks.step()
    piece_y = line(lambda v: v, piece_y)
    piece_both = other_core(piece_y)
    normed_blocks.step()
    cot_blocks = Gather(ring, line, cot)
    pieces = [piece, piece_y, piece_core, piece_both]
    all_normed, qkv, mixed, lse = line(
        lambda pieces: attend(ring.maps, normed_blocks.blocks, pieces, bias_heads, waves, seen_from), pieces
    )

    def block(v, i):
        return v[i * tokens : (i + 1) * tokens]

    class Scatter:
        def __init__(self, given, far, pair, own):
            self.given, self.pair, self.own = given, pair, own
            top, bottom = line(lambda *v: halves(*[far(*v).astype(bf16)] * 2), *given)
            self.first, self.second = ring.up(top), ring.down(bottom)
            self.d = pairs - 1
            self.term = line(lambda *v: pair(self.d, *v), *given)

        def step(self):
            half = tokens // 2

            def add(term, first, second):
                first, second = first.astype(f32), second.astype(f32)
                if self.d == pairs - 1:
                    first = jnp.pad(first, ((0, half), (0, 0)))
                    second = jnp.pad(second, ((half, 0), (0, 0)))
                return (term[tokens:] + first).astype(bf16), (term[:tokens] + second).astype(bf16)

            first, second = line(add, self.term, self.first, self.second)
            self.first, self.second = ring.up(first), ring.down(second)
            self.d -= 1
            self.term = line(lambda *v: self.pair(self.d, *v) if self.d else self.own(*v), *self.given)

        def parts(self):
            return self.term, self.first, self.second

        def finish(self):
            return line(lambda a, b, c: a + b.astype(f32) + c.astype(f32), *self.parts())

    def scattered(given, far, pair, own, fill, whole=True):
        going = Scatter(given, far, pair, own)
        for k in range(pairs):
            for work in fill[k] if k < len(fill) else ():
                work()
            if k < pairs - 1:
                going.step()
        return going.finish() if whole else going.parts()

    def pair_rows(v, d):
        return v[(2 * d - 1) * tokens : (2 * d + 1) * tokens]

    heads = {}

    def join_heads():
        heads["w"] = line(lambda *p: jnp.concatenate(p), *pieces)

    cot_step = cot_blocks.step
    branch = scattered(
        (mixed, w_out),
        lambda v, w: dot(block(v, n - 1), w),
        lambda d, v, w: dot(pair_rows(v, d), w),
        lambda v, w: dot(block(v, 0), w),
        [(cot_step,), (cot_step,), (cot_step,), (join_heads,)],
    )

    def second_norm(x, branch):
        middle = x + branch
        normed, unit, inverse = norm_parts(middle, ln2_gain, ln2_bias)
        return normed.astype(bf16), middle, unit, inverse

    normed_two, middle, unit_two, inverse_two = line(second_norm, x, branch)
    two_blocks = Gather(ring, line, normed_two)
    while len(cot_blocks.blocks) < n + 1:
        cot_blocks.step()
    held = []
    for d in range(1, pairs + 1):
        two_blocks.step()
        first, second = (v.blocks[2 * d - 1 : 2 * d + 1] for v in (two_blocks, cot_blocks))
        if d == pairs:
            first, second = [normed_two, *first], [cot, *second]
        held = line(
            lambda t, held, c=second, d=d: hidden_pair(d - 1, pairs, t, c, gate_rows, up_rows, w_down, held), first, held
        )
    all_two, all_cot, all_hidden, all_gate, all_up = held

    def last(v):
        return v[(n - 2) * tokens :]

    def ffn_rows(v, d):
        return v[2 * (d - 1) * tokens : 2 * d * tokens]

    def both(gate, up, gate_rows, up_rows):
        return dot(gate, gate_rows) + dot(up, up_rows)

    def quarter_one(units, rows, got):
        return (dot_rows(units, at.side(rows, "mine other", 4)) + at.side(got, "other").astype(f32)).astype(bf16)

    def quarter_two(units, rows, got, got_y):
        return (dot_rows(units, at.side(rows, "mine y", 4)) + at.side(got, "y").astype(f32) + got_y.astype(f32)).astype(bf16)

    class Reduced:
        def __init__(self, units, rows):
            self.units, self.rows = units, rows

        def one(self):
            self.got = other_core(line(lambda u, r: dot_rows(u, at.side(r, "across")).astype(bf16), self.units, self.rows))

        def two(self):
            self.got_y = other_y(line(quarter_one, self.units, self.rows, self.got))

        def three(self):
            piece = line(quarter_two, self.units, self.rows, self.got, self.got_y)
            self.pieces = [piece, other_y(piece), other_core(piece)]

        def four(self):
            self.pieces[1] = line(lambda v: v, self.pieces[1])
            self.pieces.append(other_core(self.pieces[1]))

        def five(self):
            self.out = line(lambda *p: placed(at.column_place, p, 1), *self.pieces)

    down, gate, up = Reduced(all_hidden, all_cot), Reduced(all_gate, all_two), Reduced(all_up, all_two)
    last_term = line(lambda g, u, *w: both(last(g), last(u), *w), all_gate, all_up, gate_rows, up_rows)
    grad_two = scattered(
        (last_term, all_gate, all_up, gate_rows, up_rows),
        lambda v, *_: v[tokens:],
        lambda d, _, g, u, *w: both(ffn_rows(g, d), ffn_rows(u, d), *w),
        lambda v, *_: v[:tokens],
        [(down.one, gate.one, down.two), (gate.two, up.one), (up.two, down.three), (gate.three,)],
    )

    def second_back(grad_two):
        grad_middle = cot.astype(f32) + norm_back(grad_two, unit_two, inverse_two, ln2_gain)
        return grad_middle, grad_middle.astype(bf16), jnp.sum(grad_two * unit_two, axis=0), jnp.sum(grad_two, axis=0)

    grad_middle, grad_branch, gain_two_grad, bias_two_grad = line(second_back, grad_two)

    branch_blocks = Gather(ring, line, grad_branch)
    going = {}

    def start_out():
        last_out = line(lambda h, w: dot(last(h), w), all_hidden, w_down)
        going["out"] = Scatter(
            (last_out, all_hidden, w_down),
            lambda v, *_: v[tokens:],
            lambda d, _, h, w: dot(ffn_rows(h, d), w),
            lambda v, *_: v[:tokens],
        )

    fill = [(up.three,), (down.four, start_out), (gate.four,), (lambda: going["out"].step(), up.four)]
    for k in range(pairs):
        for work in fill[k] if k < len(fill) else ():
            work()
        branch_blocks.step()
    out_sum = going["out"]
    out_sum.step()
    grad_joined, outer = line(
        lambda w: attend_back(ring.maps, branch_blocks.blocks, w, qkv, mixed, lse, waves, seen_from), w_out
    )

    grad_w_out = {}

    def out_one():
        grad_w_out["mine"], give = line(lambda v: (at.side(v, "core"), at.side(v, "across").astype(bf16)), outer)
        grad_w_out["got"] = other_core(give)

    def out_two():
        def work(v, got):
            v = v + got.astype(f32)
            return at.side(v, "y"), at.side(v, "other").astype(bf16)

        grad_w_out["mine"], give = line(work, grad_w_out["mine"], grad_w_out["got"])
        grad_w_out["got"] = other_y(give)

    def out_three():
        v = line(lambda v, got: (v + got.astype(f32)).astype(bf16), grad_w_out["mine"], grad_w_out["got"])
        grad_w_out["pieces"] = [v, other_y(v), other_core(v)]

    qkv_grad = {}

    def qkv_one():
        give = line(lambda a, b: dot_rows(a[:, model // 2 :], b).astype(bf16), all_normed, grad_joined)
        qkv_grad["give"], qkv_grad["got"] = give, other_core(give)

    def qkv_two():
        def work(a, b, got):
            own = dot_rows(a[:, model // 4 : model // 2], b)
            return (own + got[got.shape[0] // 2 :].astype(f32)).astype(bf16), own

        give, qkv_grad["local_y"] = line(work, all_normed, grad_joined, qkv_grad["got"])
        qkv_grad["got_y"] = other_y(give)

    def qkv_three():
        def work(a, b, got, got_y):
            own = dot_rows(a[:, : model // 4], b)
            return (own + got[: got.shape[0] // 2].astype(f32) + got_y.astype(f32)).astype(bf16), own

        piece, qkv_grad["local"] = line(work, all_normed, grad_joined, qkv_grad["got"], qkv_grad["got_y"])
        piece = piece.reshape(n, share, 3 * width)
        qkv_grad["back"] = lax.all_to_all(piece, "seq", split_axis=0, concat_axis=0, tiled=True)

    def to_rows():
        back = line(beside, qkv_grad["back"])
        qkv_grad["rows"], qkv_grad["back_y"], qkv_grad["back_core"] = back, other_y(back), other_core(back)

    def natural(v):
        v = v.reshape(-1, 4, n, share)
        v = [pick(v, at.order[j], 1) for j in range(4)]
        return jnp.stack(v, 2).reshape(-1, model)

    vectors = {}

    def sum_vectors():
        def work(joined, w, *local):
            bias = jnp.sum(joined.astype(f32), axis=0)
            w = w.astype(f32)
            shift = natural(jnp.sum(w * bias, axis=1))[0]
            rows = jnp.concatenate([v.astype(f32) for v in local])
            gain = (natural(jnp.sum(w * rows, axis=1))[0] - ln1_bias * shift) / ln1_gain
            bias_all = jnp.zeros((3, n, width), f32)
            bias_all = lax.dynamic_update_slice(bias_all, bias.reshape(3, 1, width), (jnp.uint32(0), at.seq, jnp.uint32(0))).reshape(-1)
            return jnp.concatenate([gain, shift, gain_two_grad, bias_two_grad, bias_all]).reshape(-1, 128)

        v = line(work, grad_joined, heads["w"], qkv_grad["local"], qkv_grad["local_y"], qkv_grad["give"])
        vectors["sum"] = v
        vectors["hops"] = [("batch", 1), *(("seq", bit) for bit in bits_of(n)), ("batch", 2)]
        vectors["other"] = swap(v, *vectors["hops"][0])

    def vector_step():
        v = line(lambda a, b: a + b, vectors["sum"], vectors["other"])
        vectors["sum"] = v
        vectors["hops"].pop(0)
        if vectors["hops"]:
            vectors["other"] = swap(v, *vectors["hops"][0])

    qkv_one()
    grad_one = scattered(
        (grad_joined, heads["w"]),
        lambda v, w: dot_last(block(v, n - 1), w),
        lambda d, v, w: dot_last(pair_rows(v, d), w),
        lambda v, w: dot_last(block(v, 0), w),
        [(qkv_two,), (qkv_three,), (down.five, gate.five, to_rows), (sum_vectors,)],
        whole=False,
    )

    def last_back(term, first, second):
        if share % HEAD_DIM:
            grad_one = natural(term + first.astype(f32) + second.astype(f32))
            return grad_middle + norm_back(grad_one, unit_one, inverse_one, ln1_gain)
        given = term, first, second, unit_one, inverse_one, ln1_gain[None], grad_middle
        out = jax.ShapeDtypeStruct((tokens, model), f32)
        return once(functools.partial(last_back_kernel, n), "last_back", 8, out, [], *given, maps=at.peers)

    grad_input = line(last_back, *grad_one)
    back_y = line(lambda v: v, qkv_grad["back_y"])
    back_both = other_core(back_y)
    out_one()
    vector_step()
    for _ in range(pairs - 3):
        out_sum.step()
    out_two()
    vector_step()
    up.five()
    out_three()
    vector_step()
    grad_w_qkv = line(
        lambda *p: placed(at.row_place, p, 0), qkv_grad["rows"], back_y, qkv_grad["back_core"], back_both
    )
    while vectors["hops"]:
        vector_step()
    output = line(lambda a, b: (a + b).astype(bf16), middle, out_sum.finish())
    v = grad_w_out["pieces"]
    v[1] = line(lambda v: v, v[1])
    v.append(other_core(v[1]))
    grad_w_out = line(lambda *p: placed(at.column_place, p, 1), *v)
    gain_one_sum, bias_one_sum, gain_two_sum, bias_two_sum, qkv_bias_sum = jnp.split(
        vectors["sum"].reshape(-1), [model, 2 * model, 3 * model, 4 * model]
    )

    return (
        output.reshape(tokens, 1, model),
        grad_input.reshape(tokens, 1, model),
        gain_one_sum,
        bias_one_sum,
        grad_w_qkv,
        qkv_bias_sum,
        grad_w_out,
        gain_two_sum,
        bias_two_sum,
        gate.out.T,
        up.out.T,
        down.out,
    )


def solution(mesh):
    token, shard, column, whole = P("seq", "batch", None), P("seq", None), P(None, "seq"), P()
    in_specs = (
        token, P("seq", "batch"), whole, whole, shard, whole, shard, whole, whole, column, column, shard, token
    )
    out_specs = (token, token, whole, whole, shard, whole, shard, whole, whole, column, column, shard)
    return jax.shard_map(on_device, mesh=mesh, in_specs=in_specs, out_specs=out_specs, check_vma=False)
```

```python
import functools

import jax
import jax.numpy as jnp
import numpy as np
from jax import lax
from jax.experimental import pallas as pl
from jax.experimental.pallas import tpu as pltpu
from jax.sharding import PartitionSpec as P

HEADS = 32
HEAD_DIM = 64
ROT = 16
BLOCK = 128
TILE = 256

eps_norm = 1e-05
theta_base = 10000.0
masked_score = -1e30
bf16 = jnp.bfloat16
f32 = jnp.float32


def ring_order(n):
    return [0, 2, 4, 6, 7, 5, 3, 1] if n == 8 else list(range(n))


class Ring:
    def __init__(self, axis):
        self.axis = axis
        self.n = n = lax.axis_size(axis)
        order = ring_order(n)
        self.ahead = [(order[i], order[(i + 1) % n]) for i in range(n)]
        self.behind = [(b, a) for a, b in self.ahead]
        half = n // 2
        table = np.zeros((n, 2 * n), np.int32)
        for i, device in enumerate(order):
            for slot in range(n):
                step = -((slot + 1) // 2) if slot % 2 and slot < n - 1 else slot // 2 if slot < n - 1 else half
                natural = order[(i + step) % n]
                table[device, natural], table[device, n + slot] = slot, natural
        self.table = jnp.asarray(table)

    def up(self, v):
        return lax.ppermute(v, self.axis, self.ahead)

    def down(self, v):
        return lax.ppermute(v, self.axis, self.behind)


class Gather:
    def __init__(self, ring, line, v):
        self.ring, self.line, self.d = ring, line, 1
        self.half = v.shape[0] // 2
        self.blocks = [v]
        self.flying = ring.up(v), ring.down(v)

    def step(self):
        got = self.line(lambda *v: v, *self.flying)
        self.blocks += got
        self.d += 1
        last = self.ring.n // 2
        if self.d < last:
            self.flying = self.ring.up(got[0]), self.ring.down(got[1])
        elif self.d == last:
            top, bottom = halves(*got)
            self.flying = self.ring.up(top), self.ring.down(bottom)
        return got


class Line:
    def __init__(self):
        self.last = ()

    def __call__(self, work, *given):
        given, _ = lax.optimization_barrier((given, self.last))
        out = work(*given)
        self.last = out
        return out


def swap(v, axis, bit):
    n = lax.axis_size(axis)
    return lax.ppermute(v, axis, [(i, i ^ bit) for i in range(n)])


def bits_of(n):
    return [1 << i for i in range(n.bit_length() - 1)]


def after(v, *others):
    return lax.optimization_barrier((v, *others))[0]


class Places:
    def __init__(self, model):
        u = functools.partial(jnp.asarray, dtype=jnp.uint32)
        seq, batch = lax.axis_index("seq").astype(jnp.uint32), lax.axis_index("batch").astype(jnp.uint32)
        core, y = batch % u(2), batch // u(2)
        self.seq = seq
        self.quarter = [batch ^ u(k) for k in range(4)]
        self.order = [(q % u(2)) * u(2) + q // u(2) for q in self.quarter]
        self.starts = {
            (name, size): which * u(size)
            for name, which in (("core", core), ("across", u(1) - core), ("y", y), ("other", u(1) - y))
            for size in (model // 2, model // 4)
        }
        for name in ("y", "other"):
            self.starts["mine " + name, model // 4] = (
                self.starts["core", model // 2] + self.starts[name, model // 4]
            )
        self.column_place = jnp.stack([(core * u(2) + y) ^ u(k) for k in range(4)]).astype(jnp.int32)
        self.row_place = jnp.stack([batch ^ u(k) for k in (0, 2, 1, 3)]).astype(jnp.int32)
        peers = [seq ^ u(k) for k in range(lax.axis_size("seq"))]
        self.peers = jnp.stack([batch, *peers]).astype(jnp.int32)

    def scalars(self):
        return [self.seq, *self.quarter, *self.order, *self.starts.values(), self.column_place, self.row_place, self.peers]

    def tied(self, scalars):
        self.seq, self.quarter, self.order = scalars[0], scalars[1:5], scalars[5:9]
        self.starts = dict(zip(self.starts, scalars[9:-3], strict=True))
        self.column_place, self.row_place, self.peers = scalars[-3:]

    def side(self, v, which, parts=2):
        size = v.shape[1] // parts
        return lax.dynamic_slice(v, (jnp.uint32(0), self.starts[which, size]), (v.shape[0], size))


def pick(v, index, axis):
    starts = [jnp.uint32(0)] * v.ndim
    starts[axis] = index
    sizes = list(v.shape)
    sizes[axis] = 1
    return lax.squeeze(lax.dynamic_slice(v, starts, sizes), (axis,))


def norm_parts(values, gain_vector, shift_vector):
    mean_value = jnp.mean(values, axis=-1, keepdims=True)
    centred = values - mean_value
    inverse = lax.rsqrt(jnp.mean(centred * centred, axis=-1, keepdims=True) + eps_norm)
    unit_value = centred * inverse
    return (unit_value * gain_vector + shift_vector, unit_value, inverse)


def norm_back(gradient, unit_value, inverse, gain_vector):
    scaled = gradient * gain_vector
    return inverse * (
        scaled
        - jnp.mean(scaled, axis=-1, keepdims=True)
        - unit_value * jnp.mean(scaled * unit_value, axis=-1, keepdims=True)
    )


def dot(a, b):
    return jnp.dot(a, b, preferred_element_type=f32)


def dot_rows(a, b):
    return lax.dot_general(a, b, (((0,), (0,)), ((), ())), preferred_element_type=f32)


def dot_last(a, b):
    return lax.dot_general(a, b, (((1,), (1,)), ((), ())), preferred_element_type=f32)


def rotary_waves(positions):
    half = ROT // 2
    frequency = theta_base ** (-(jnp.arange(half, dtype=f32) * 2.0 / ROT))
    angles = frequency[:, None] * positions
    return jnp.concatenate([jnp.cos(angles), jnp.sin(angles)], 0)


def fill_table(table_ref, waves_ref):
    half = ROT // 2
    for start in range(0, table_ref.shape[0], BLOCK):
        here = slice(start, start + BLOCK)
        cosine, sine = waves_ref[:half, here], waves_ref[half:, here]
        rest = jnp.zeros((HEAD_DIM - ROT, BLOCK), f32)
        table_ref[here, :] = jnp.concatenate([cosine, cosine, rest + 1.0, -sine, sine, rest], 0).T


def spread_table(table, width):
    own, other = table[:, :HEAD_DIM], table[:, HEAD_DIM:]
    return (jnp.concatenate([v] * (width // HEAD_DIM), 1) for v in (own, other))


def rotate_lanes(x, own, other):
    half = ROT // 2
    width = x.shape[1]
    lane = lax.broadcasted_iota(jnp.int32, x.shape, 1) % HEAD_DIM
    partner = jnp.where(lane < half, pltpu.roll(x, width - half, 1), pltpu.roll(x, half, 1))
    return x * own + partner * other


def visible_to(first_ref, start, keys, tile):
    key = lax.broadcasted_iota(jnp.int32, (keys, tile), 0)
    query = lax.broadcasted_iota(jnp.int32, (keys, tile), 1) + start
    return (key <= query) & (key >= first_ref[0:1, start : start + tile])


def head_rows(x, h):
    if x.shape[0] == HEAD_DIM:
        return x
    row = lax.broadcasted_iota(jnp.int32, x.shape, 0) // HEAD_DIM
    return jnp.where(row == h, x, jnp.zeros_like(x))


def head_lanes(x, h):
    if x.shape[1] == HEAD_DIM:
        return x
    lane = lax.broadcasted_iota(jnp.int32, x.shape, 1) // HEAD_DIM
    return jnp.where(lane == h, x, jnp.zeros_like(x))


def row_list(refs):
    return jnp.concatenate([ref[...] for ref in refs], 0)


def at_block(ref, index):
    return pl.ds(pl.multiple_of(ref[index] * BLOCK, BLOCK), BLOCK)


def grouped(refs, rows):
    groups, held, count = [], [], 0
    for ref in refs:
        held.append(ref)
        count += ref.shape[0]
        if count == rows:
            groups.append(held)
            held, count = [], 0
    return groups


def attend_kernel(blocks, maps_ref, *refs):
    block_refs, refs = refs[:blocks], refs[blocks:]
    piece_refs, refs = refs[:4], refs[4:]
    bias_ref, waves_ref, first_ref, all_ref, qkv_ref, mixed_ref, lse_ref, q_t, v_t, table_ref = refs
    fill_table(table_ref, waves_ref)
    length, width = mixed_ref.shape
    heads = width // HEAD_DIM
    blocks = length // BLOCK
    scale = HEAD_DIM ** (-0.5)
    tile = min(TILE, length)
    depth = piece_refs[0].shape[0]
    for i, group in enumerate(grouped(block_refs, tile)):
        rows = row_list(group)
        all_ref[i * tile : (i + 1) * tile, :] = rows
        x = bias_ref[...] + sum(dot(rows[:, g * depth : (g + 1) * depth], p[...]) for g, p in enumerate(piece_refs))
        for k in range(tile // BLOCK):
            here = at_block(maps_ref, blocks + i * (tile // BLOCK) + k)
            part = x[k * BLOCK : (k + 1) * BLOCK]
            own, other = spread_table(table_ref[here, :], width)
            q = rotate_lanes(part[:, :width], own, other).astype(bf16)
            v = part[:, 2 * width :].astype(bf16)
            qkv_ref[0, here, :] = q
            qkv_ref[1, here, :] = rotate_lanes(part[:, width : 2 * width], own, other).astype(bf16)
            qkv_ref[2, here, :] = v
            q_t[:, here] = (q.astype(f32) * scale).T.astype(bf16)
            v_t[:, here] = v.astype(f32).T.astype(bf16)
    lse_ref[...] = jnp.zeros_like(lse_ref)
    for start in range(0, length, tile):
        keys = start + tile
        seen = visible_to(first_ref, start, keys, tile)
        queries = q_t[:, start : start + tile]
        outs = []
        for h in range(heads):
            scores = dot(qkv_ref[1, :keys, :], head_rows(queries, h))
            scores = jnp.where(seen, scores, masked_score)
            top = jnp.max(scores, axis=0, keepdims=True)
            weights = jnp.exp(scores - top)
            total = jnp.sum(weights, axis=0, keepdims=True)
            lse_ref[h : h + 1, start : start + tile] = top + jnp.log(total)
            prob = (weights * (1.0 / total)).astype(bf16)
            outs.append(dot(v_t[h * HEAD_DIM : (h + 1) * HEAD_DIM, :keys], prob))
        out = jnp.concatenate(outs, 0).T.astype(bf16)
        for i in range(tile // BLOCK):
            mixed_ref[at_block(maps_ref, start // BLOCK + i), :] = out[i * BLOCK : (i + 1) * BLOCK]


def attend_back_kernel(blocks, maps_ref, *refs):
    block_refs, refs = refs[:blocks], refs[blocks:]
    w_ref, qkv_ref, mixed_ref, lse_ref, waves_ref, first_ref, out_ref, outer_ref = refs[:8]
    q_t, k_t, g_t, grads, delta, dk, dv, table_ref = refs[8:]
    fill_table(table_ref, waves_ref)
    length, width = mixed_ref.shape
    blocks = length // BLOCK
    heads = width // HEAD_DIM
    scale = HEAD_DIM ** (-0.5)
    tile = min(TILE, length)
    for i, group in enumerate(grouped(block_refs, tile)):
        rows = dot_last(row_list(group), w_ref[...]).astype(bf16)
        for k in range(tile // BLOCK):
            s = i * (tile // BLOCK) + k
            here = at_block(maps_ref, blocks + s)
            g = rows[k * BLOCK : (k + 1) * BLOCK]
            g_flip = g.astype(f32).T
            both = g_flip * mixed_ref[s * BLOCK : (s + 1) * BLOCK, :].astype(f32).T
            for h in range(heads):
                delta[h : h + 1, here] = jnp.sum(both[h * HEAD_DIM : (h + 1) * HEAD_DIM], axis=0, keepdims=True)
            grads[here, :] = g
            g_t[:, here] = g_flip.astype(bf16)
    for j in range(blocks):
        here = slice(j * BLOCK, (j + 1) * BLOCK)
        q_t[:, here] = (qkv_ref[0, here, :].astype(f32) * scale).T.astype(bf16)
        k_t[:, here] = qkv_ref[1, here, :].astype(f32).T.astype(bf16)
    dk[...] = jnp.zeros_like(dk)
    dv[...] = jnp.zeros_like(dv)
    for start in range(0, length, tile):
        keys = start + tile
        here = slice(start, keys)
        seen = visible_to(first_ref, start, keys, tile)
        q_tile, g_tile = q_t[:, here], g_t[:, here]
        q_rows, g_rows = qkv_ref[0, here, :], grads[here, :]
        dq, dk_sum, dv_sum = [], dk[:keys, :], dv[:keys, :]
        for h in range(heads):
            scores = dot(qkv_ref[1, :keys, :], head_rows(q_tile, h))
            prob = jnp.where(seen, jnp.exp(scores - lse_ref[h : h + 1, here]), 0.0)
            grad_prob = dot(qkv_ref[2, :keys, :], head_rows(g_tile, h))
            grad_score = (prob * (grad_prob - delta[h : h + 1, here])).astype(bf16)
            dv_sum += dot(prob.astype(bf16), head_lanes(g_rows, h))
            dk_sum += dot(grad_score, head_lanes(q_rows, h))
            dq.append(dot(k_t[h * HEAD_DIM : (h + 1) * HEAD_DIM, :keys], grad_score))
        dk[:keys, :] = dk_sum
        dv[:keys, :] = dv_sum
        dq = jnp.concatenate(dq, 0).T * scale
        for i in range(tile // BLOCK):
            at = slice(i * BLOCK, (i + 1) * BLOCK)
            place = slice(start + i * BLOCK, start + (i + 1) * BLOCK)
            own, other = spread_table(table_ref[place, :], width)
            turned = rotate_lanes(dq[at], own, -other)
            out_ref[at_block(maps_ref, start // BLOCK + i), :width] = turned.astype(bf16)
    for j in range(blocks):
        rows = at_block(maps_ref, j)
        here = slice(j * BLOCK, (j + 1) * BLOCK)
        own, other = spread_table(table_ref[here, :], width)
        turned = rotate_lanes(dk[here, :] * scale, own, -other)
        out_ref[rows, width : 2 * width] = turned.astype(bf16)
        out_ref[rows, 2 * width :] = dv[here, :].astype(bf16)
    for start in range(0, outer_ref.shape[1], 512):
        columns = slice(start, start + 512)
        outer_ref[:, columns] = sum(
            dot_rows(
                mixed_ref[i * tile : (i + 1) * tile, :], jnp.concatenate([ref[:, columns] for ref in group], 0)
            )
            for i, group in enumerate(grouped(block_refs, tile))
        )


def once(kernel, name, megabytes, out_shape, scratch, *given, maps=None):
    vmem = pl.BlockSpec(memory_space=pltpu.VMEM)
    many = isinstance(out_shape, (tuple, list))
    small = [] if maps is None else [maps]
    return pl.pallas_call(
        kernel,
        out_shape=out_shape,
        in_specs=[pl.BlockSpec(memory_space=pltpu.SMEM)] * len(small) + [vmem] * len(given),
        out_specs=[vmem] * len(out_shape) if many else vmem,
        scratch_shapes=scratch,
        compiler_params=pltpu.CompilerParams(vmem_limit_bytes=megabytes * 2**20),
        cost_estimate=BRIEF,
        name=name,
    )(*small, *given)


BRIEF = pl.CostEstimate(flops=1, bytes_accessed=1, transcendentals=0)


def attend(maps, blocks, pieces, bias, waves, first):
    length, width = waves.shape[1], pieces[0].shape[1] // 3
    return once(
        functools.partial(attend_kernel, len(blocks)),
        "attend",
        16 if length <= 1024 else 40,
        (
            jax.ShapeDtypeStruct((length, blocks[0].shape[1]), bf16),
            jax.ShapeDtypeStruct((3, length, width), bf16),
            jax.ShapeDtypeStruct((length, width), bf16),
            jax.ShapeDtypeStruct((max(8, width // HEAD_DIM), length), f32),
        ),
        [pltpu.VMEM((width, length), bf16), pltpu.VMEM((width, length), bf16), pltpu.VMEM((length, 2 * HEAD_DIM), f32)],
        *blocks,
        *pieces,
        bias,
        waves,
        first,
        maps=maps,
    )


def attend_back(maps, blocks, w_out, qkv, mixed, lse, waves, first):
    length, width = mixed.shape
    return once(
        functools.partial(attend_back_kernel, len(blocks)),
        "attend_back",
        16 if length <= 1024 else 40,
        (
            jax.ShapeDtypeStruct((length, 3 * width), bf16),
            jax.ShapeDtypeStruct((width, blocks[0].shape[1]), f32),
        ),
        [
            pltpu.VMEM((width, length), bf16),
            pltpu.VMEM((width, length), bf16),
            pltpu.VMEM((width, length), bf16),
            pltpu.VMEM((length, width), bf16),
            pltpu.VMEM((lse.shape[0], length), f32),
            pltpu.VMEM((length, width), f32),
            pltpu.VMEM((length, width), f32),
            pltpu.VMEM((length, 2 * HEAD_DIM), f32),
        ],
        *blocks,
        w_out,
        qkv,
        mixed,
        lse,
        waves,
        first,
        maps=maps,
    )


def products_kernel(items, *refs):
    out_ref, offset = refs[-1], 0
    rows = out_ref.shape[0]
    for (start, last), a, b in zip(items, refs[:-1:2], refs[1:-1:2], strict=True):
        width = b.shape[0 if last else 1]
        left = a[start : start + rows, :]
        for begin in range(0, width, 512):
            columns = slice(begin, begin + 512)
            out_ref[:, offset + begin : offset + begin + 512] = (
                dot_last(left, b[columns, :]) if last else dot(left, b[:, columns])
            )
        offset += width


def products(rows, items, *given):
    width = sum(b.shape[0 if last else 1] for (_, last), b in zip(items, given[1::2], strict=True))
    out = jax.ShapeDtypeStruct((rows, width), f32)
    return once(functools.partial(products_kernel, items), "products", 8, out, [], *given)


def hop_kernel(items, *refs):
    given, (first_ref, second_ref, ahead_ref, behind_ref) = refs[:-4], refs[-4:]
    rows, half, offset = ahead_ref.shape[0], first_ref.shape[0], 0
    for (start, last), a, b in zip(items, given[::2], given[1::2], strict=True):
        width = b.shape[0 if last else 1]
        left = a[start : start + 2 * rows, :]
        for begin in range(0, width, 512):
            columns = slice(begin, begin + 512)
            term = dot_last(left, b[columns, :]) if last else dot(left, b[:, columns])
            here = slice(offset + begin, offset + begin + 512)
            first, second = first_ref[:, here].astype(f32), second_ref[:, here].astype(f32)
            ahead_ref[:half, here] = (term[rows : rows + half] + first).astype(bf16)
            behind_ref[rows - half :, here] = (term[rows - half : rows] + second).astype(bf16)
            if half < rows:
                ahead_ref[half:, here] = term[rows + half :].astype(bf16)
                behind_ref[: rows - half, here] = term[: rows - half].astype(bf16)
        offset += width


def hop(rows, items, given, first, second):
    out = jax.ShapeDtypeStruct((rows, first.shape[1]), bf16)
    return once(functools.partial(hop_kernel, items), "hop", 10, (out, out), [], *given, first, second)


def vectors_kernel(n, peers_ref, joined_ref, w_ref, local_ref, give_ref, shift_ref, gain_ref, two_ref, out_ref, turned):
    width = joined_ref.shape[1] // 3
    ones = jnp.ones((8, joined_ref.shape[0]), bf16)
    bias = dot(ones, joined_ref[...])[0:1]
    parts = []
    for _ in range(3):
        parts.append(bias.astype(bf16).astype(f32))
        bias = bias - parts[-1]
    shift = jnp.sum(dot_last(jnp.concatenate(parts, 0).astype(bf16), w_ref[...]), axis=0, keepdims=True)
    ones = jnp.ones((8, w_ref.shape[1]), bf16)
    half = w_ref.shape[0] // 2
    rows = []
    for start, ref in ((0, local_ref), (half, give_ref)):
        product = w_ref[start : start + half, :].astype(f32) * ref[...].astype(f32)
        upper = product.astype(bf16)
        lower = (product - upper.astype(f32)).astype(bf16)
        rows.append((dot_last(ones, upper) + dot_last(ones, lower))[0:1])
    both = jnp.concatenate([jnp.concatenate(rows, 1), shift], 0)
    for number in range(4):

        @pl.when(peers_ref[0] == number)
        def _(number=number):
            turned[...] = in_plain_order(both, number, n)

    out_ref[...] = jnp.zeros_like(out_ref)
    out_ref[0:1, :] = (turned[0:1, :] - shift_ref[...] * turned[1:2, :]) / gain_ref[...]
    out_ref[1:2, :] = turned[1:2, :]
    out_ref[2:4, :] = two_ref[...]
    total = sum(parts)
    for c in range(3):
        here = pl.ds(pl.multiple_of(peers_ref[1] * width, BLOCK), width)
        out_ref[4 + c : 5 + c, here] = total[:, c * width : (c + 1) * width]


def exchange(blocks):
    return [blocks[0]] + [swap(v, "seq", k) for k, v in enumerate(blocks) if k]


def local(kernel, name, out_shape, smem, given, anywhere=0, scratch=()):
    vmem = pl.BlockSpec(memory_space=pltpu.VMEM)
    many = isinstance(out_shape, (tuple, list))
    return pl.pallas_call(
        kernel,
        out_shape=out_shape,
        in_specs=[pl.BlockSpec(memory_space=pltpu.SMEM)]
        + [pl.BlockSpec(memory_space=pl.ANY)] * anywhere
        + [vmem] * (len(given) - anywhere),
        out_specs=[vmem] * len(out_shape) if many else vmem,
        scratch_shapes=list(scratch),
        compiler_params=pltpu.CompilerParams(vmem_limit_bytes=6 * 2**20),
        cost_estimate=BRIEF,
        name=name,
    )(smem, *given)


def cut_kernel(peers_ref, w_ref, place_ref, *refs):
    outs, semaphores = refs[:-1], refs[-1]
    extra, width = place_ref.shape[0], place_ref.shape[1] // 3
    share, model = outs[0].shape[0] - extra, w_ref.shape[1] // 3
    rows = pl.ds(pl.multiple_of(peers_ref[0] * share, share), share)
    copies = []
    for k, out in enumerate(outs):
        for c in range(3):
            columns = pl.ds(pl.multiple_of(c * model + peers_ref[1 + k] * width, BLOCK), width)
            copies.append(
                pltpu.make_async_copy(
                    w_ref.at[rows, columns],
                    out.at[pl.ds(0, share), pl.ds(c * width, width)],
                    semaphores.at[3 * k + c],
                )
            )
            copies[-1].start()
    for out in outs:
        out[share:, :] = place_ref[...]
    for copy in copies:
        copy.wait()


def cut(at, w, place, n):
    extra, columns = place.shape
    share, width = w.shape[0] // 4, columns // 3
    if width % BLOCK:
        mine = pick(w.reshape(4, share, 3 * width * n), at.quarter[0], 0).reshape(share, 3, n, width)
        mine = [pick(mine, at.seq ^ jnp.uint32(k), 2).reshape(share, columns) for k in range(n)]
        return [jnp.concatenate([v, place]) for v in mine]
    out = jax.ShapeDtypeStruct((share + extra, columns), bf16)
    return local(cut_kernel, "cut", [out] * n, at.peers, (w, place), 1, [pltpu.SemaphoreType.DMA((3 * n,))])


def stack_kernel(peers_ref, *refs):
    ins, (piece_ref, place_ref) = refs[:-2], refs[-2:]
    share = piece_ref.shape[0] // len(ins)
    tokens = place_ref.shape[1] // len(ins)
    for k, ref in enumerate(ins):
        peer = peers_ref[1 + k]
        piece_ref[pl.ds(pl.multiple_of(peer * share, share), share), :] = ref[:share, :]
        place = ref[share:, :tokens].astype(f32)
        place_ref[:, pl.ds(pl.multiple_of(peer * tokens, tokens), tokens)] = place[0:1] * 64.0 + place[1:2]


def stacked(at, blocks, extra, tokens):
    n, (rows, columns) = len(blocks), blocks[0].shape
    shapes = [
        jax.ShapeDtypeStruct((n * (rows - extra), columns), bf16),
        jax.ShapeDtypeStruct((1, n * tokens), f32),
    ]
    return local(stack_kernel, "stacked", shapes, at.peers, blocks)


def in_plain_order(x, number, n):
    share = x.shape[1] // (4 * n)
    order = [(q % 2) * 2 + q // 2 for q in (number ^ j for j in range(4))]
    starts = [order[j] * n * share + s * share for s in range(n) for j in range(4)]
    return jnp.concatenate([x[:, start : start + share] for start in starts], 1)


def last_back_kernel(
    n, peers_ref, term_ref, first_ref, second_ref, unit_ref, inverse_ref, gain_ref, grad_ref, middle_ref, out_ref, sum_ref
):
    total = term_ref[...] + first_ref[...].astype(f32) + second_ref[...].astype(f32)
    model = out_ref.shape[1]
    sum_ref[...] = (middle_ref[...] + total[:, model:]).astype(bf16)
    total = total[:, :model]
    for number in range(4):

        @pl.when(peers_ref[0] == number)
        def _(number=number):
            out_ref[...] = in_plain_order(total, number, n)

    out_ref[...] = grad_ref[...] + norm_back(out_ref[...], unit_ref[...], inverse_ref[...], gain_ref[...])


def beside_kernel(in_ref, out_ref):
    n, _, columns = in_ref.shape
    width = columns // 3
    for k in range(n):
        for c in range(3):
            start = (c * n + k) * width
            out_ref[:, start : start + width] = in_ref[k, :, c * width : (c + 1) * width]


def beside(v):
    n, rows, columns = v.shape
    return once(beside_kernel, "beside", 6, jax.ShapeDtypeStruct((rows, n * columns), bf16), [], v)


def halves_kernel(first_ref, second_ref, top_ref, bottom_ref):
    half = top_ref.shape[0]
    top_ref[...] = first_ref[:half, :]
    bottom_ref[...] = second_ref[half:, :]


def halves(first, second):
    half = jax.ShapeDtypeStruct((first.shape[0] // 2, first.shape[1]), first.dtype)
    vmem = pl.BlockSpec(memory_space=pltpu.VMEM)
    return pl.pallas_call(
        halves_kernel,
        out_shape=(half, half),
        in_specs=[vmem] * 2,
        out_specs=(vmem,) * 2,
        compiler_params=pltpu.CompilerParams(vmem_limit_bytes=4 * 2**20),
        cost_estimate=BRIEF,
        name="halves",
    )(first, second)


def hidden_kernel(at, tokens, cots, held, *refs):
    token_refs, refs = refs[:tokens], refs[tokens:]
    cot_refs, refs = refs[:cots], refs[cots:]
    gate_ref, up_ref, down_ref, refs = refs[0], refs[1], refs[2], refs[3 + held :]
    results, scratch, semaphores = refs[:5], refs[5:10], refs[10]
    rows = scratch[0].shape[0]
    copies = [
        pltpu.make_async_copy(v, out.at[pl.ds(at * rows, rows), :], semaphores.at[i])
        for i, (v, out) in enumerate(zip(scratch, results, strict=True))
    ]
    two, cot, hidden, grad_gate, grad_up = scratch
    two[...] = row_list(token_refs)
    copies[0].start()
    cot[...] = row_list(cot_refs)
    copies[1].start()
    units = gate_ref.shape[0]
    for start in range(0, units, TILE):
        here = slice(start, min(start + TILE, units))
        gate, up = dot_last(two[...], gate_ref[here, :]), dot_last(two[...], up_ref[here, :])
        grad_hidden = dot_last(cot[...], down_ref[here, :])
        sigmoid = 1.0 / (1.0 + jnp.exp(-gate))
        silu = gate * sigmoid
        hidden[:, here] = (silu * up).astype(bf16)
        grad_gate[:, here] = (grad_hidden * up * sigmoid * (1.0 + gate * (1.0 - sigmoid))).astype(bf16)
        grad_up[:, here] = (grad_hidden * silu).astype(bf16)
    for copy in copies[2:]:
        copy.start()
    for copy in copies:
        copy.wait()


def hidden_pair(at, pairs, tokens, cots, gate_rows, up_rows, w_down, held):
    rows = sum(b.shape[0] for b in tokens)
    units, model = gate_rows.shape
    widths = (model, model, units, units, units)
    first = len(tokens) + len(cots) + 3
    hbm = pl.BlockSpec(memory_space=pltpu.HBM)
    return pl.pallas_call(
        functools.partial(hidden_kernel, at, len(tokens), len(cots), len(held)),
        out_shape=[jax.ShapeDtypeStruct((rows * pairs, w), bf16) for w in widths],
        in_specs=[pl.BlockSpec(memory_space=pltpu.VMEM)] * first + [hbm] * len(held),
        out_specs=[hbm] * 5,
        scratch_shapes=[pltpu.VMEM((rows, w), bf16) for w in widths] + [pltpu.SemaphoreType.DMA((5,))],
        input_output_aliases={first + i: i for i in range(len(held))},
        compiler_params=pltpu.CompilerParams(vmem_limit_bytes=12 * 2**20),
        cost_estimate=BRIEF,
        name="hidden_pair",
    )(*tokens, *cots, gate_rows, up_rows, w_down, *held)


def place_kernel(at_ref, *refs):
    out_ref = refs[-1]
    for i, ref in enumerate(refs[:-1]):

        @pl.when(pl.program_id(0) == i)
        def _(ref=ref):
            out_ref[...] = ref[...].astype(f32)


def placed(at, pieces, axis):
    shape = list(pieces[0].shape)
    total = list(shape)
    total[axis] *= len(pieces)
    return pl.pallas_call(
        place_kernel,
        out_shape=jax.ShapeDtypeStruct(tuple(total), f32),
        grid_spec=pltpu.PrefetchScalarGridSpec(
            num_scalar_prefetch=1,
            grid=(len(pieces),),
            in_specs=[pl.BlockSpec(tuple(shape), lambda i, at: (0, 0)) for _ in pieces],
            out_specs=pl.BlockSpec(tuple(shape), lambda i, at: (0, at[i]) if axis else (at[i], 0)),
        ),
        compiler_params=pltpu.CompilerParams(vmem_limit_bytes=16 * 2**20),
        cost_estimate=BRIEF,
        name="placed",
    )(at, *pieces)


def on_device(
    inputs, positions, ln1_gain, ln1_bias, w_qkv, qkv_bias, w_out, ln2_gain, ln2_bias, w_gate, w_up, w_down, cotangent
):
    n = lax.axis_size("seq")
    ring = Ring("seq")
    line = Line()
    tokens, model = inputs.shape[0], inputs.shape[2]
    length = tokens * n
    pairs = n // 2
    width = model // n
    depth = w_qkv.shape[0]
    share = depth // 4
    x = inputs.reshape(tokens, model).astype(f32)
    cot = cotangent.reshape(tokens, model)
    gate_rows, up_rows = w_gate.T, w_up.T
    others = (0, 2, 1, 3)
    at = Places(model)
    at.tied(line(lambda *v: v, *at.scalars()))

    def other_y(v):
        return swap(v, "batch", 2)

    def other_core(v):
        return swap(v, "batch", 1)

    place = positions.reshape(tokens)
    extra = 8
    place = jnp.stack([place // 64, place % 64]).astype(bf16)
    place = jnp.pad(place, ((0, extra - 2), (0, 3 * width - tokens)))
    fetched = exchange(line(lambda w, place: cut(at, w, place, n), w_qkv, place))
    bias_heads = line(lambda v: pick(v.reshape(3, n, width), at.seq, 1).reshape(1, 3 * width), qkv_bias)

    def first_norm(x):
        normed, unit, inverse = norm_parts(x, ln1_gain, ln1_bias)
        normed = normed.astype(bf16).reshape(tokens, n, 4, share)
        normed = [pick(normed, at.quarter[k], 2).reshape(tokens, -1) for k in others]
        return jnp.concatenate(normed, 1), unit, inverse

    normed, unit_one, inverse_one = line(first_norm, x)
    normed_blocks = Gather(ring, line, after(normed, fetched[1]))

    piece, places = line(lambda *v: stacked(at, v, extra, tokens), *fetched)
    piece_y, piece_core = other_y(piece), other_core(piece)
    normed_blocks.step()

    def take(places, maps):
        maps = pick(maps, at.seq, 0)
        first = jnp.arange(length, dtype=jnp.int32)[None] - places.astype(jnp.int32)
        return maps, rotary_waves(places), first

    normed_blocks.step()
    ring.maps, waves, seen_from = line(take, places, ring.table)
    piece_core = line(lambda v: v, piece_core)
    for _ in range(pairs - 3):
        normed_blocks.step()
    piece_y = line(lambda v: v, piece_y)
    piece_both = other_core(piece_y)
    normed_blocks.step()
    cot_blocks = Gather(ring, line, cot)
    pieces = [piece, piece_y, piece_core, piece_both]
    all_normed, qkv, mixed, lse = line(
        lambda pieces: attend(ring.maps, normed_blocks.blocks, pieces, bias_heads, waves, seen_from), pieces
    )

    def block(v, i):
        return v[i * tokens : (i + 1) * tokens]

    class Scatter:
        def __init__(self, given, far, pair, own, fused=False):
            self.given, self.pair, self.own, self.fused = given, pair, own, fused
            top, bottom = line(lambda *v: halves(*[far(*v).astype(bf16)] * 2), *given)
            self.first, self.second = ring.up(top), ring.down(bottom)
            self.d = pairs - 1
            if not fused:
                self.term = line(lambda *v: pair(self.d, *v), *given)

        def step(self):
            half = tokens // 2

            def add(term, first, second):
                first, second = first.astype(f32), second.astype(f32)
                if self.d == pairs - 1:
                    first = jnp.pad(first, ((0, half), (0, 0)))
                    second = jnp.pad(second, ((half, 0), (0, 0)))
                return (term[tokens:] + first).astype(bf16), (term[:tokens] + second).astype(bf16)

            if self.fused:
                first, second = line(
                    lambda first, second, *v: self.pair(self.d, first, second, *v), self.first, self.second, *self.given
                )
            else:
                first, second = line(add, self.term, self.first, self.second)
            self.first, self.second = ring.up(first), ring.down(second)
            self.d -= 1
            if not (self.fused and self.d):
                self.term = line(lambda *v: self.pair(self.d, *v) if self.d else self.own(*v), *self.given)

        def parts(self):
            return self.term, self.first, self.second

        def finish(self):
            return line(lambda a, b, c: a + b.astype(f32) + c.astype(f32), *self.parts())

    def scattered(given, far, pair, own, fill, whole=True, fused=False):
        going = Scatter(given, far, pair, own, fused)
        for k in range(pairs):
            for work in fill[k] if k < len(fill) else ():
                work()
            if k < pairs - 1:
                going.step()
        return going.finish() if whole else going.parts()

    def pair_rows(v, d):
        return v[(2 * d - 1) * tokens : (2 * d + 1) * tokens]

    heads = {}

    def join_heads():
        heads["w"] = line(lambda *p: jnp.concatenate(p), *pieces)

    cot_step = cot_blocks.step
    branch = scattered(
        (mixed, w_out),
        lambda v, w: dot(block(v, n - 1), w),
        lambda d, v, w: dot(pair_rows(v, d), w),
        lambda v, w: dot(block(v, 0), w),
        [(cot_step,), (cot_step,), (cot_step,), (join_heads,)],
    )

    def second_norm(x, branch):
        middle = x + branch
        normed, unit, inverse = norm_parts(middle, ln2_gain, ln2_bias)
        return normed.astype(bf16), middle, unit, inverse

    normed_two, middle, unit_two, inverse_two = line(second_norm, x, branch)
    two_blocks = Gather(ring, line, normed_two)
    while len(cot_blocks.blocks) < n + 1:
        cot_blocks.step()
    held = []
    for d in range(1, pairs + 1):
        two_blocks.step()
        first, second = (v.blocks[2 * d - 1 : 2 * d + 1] for v in (two_blocks, cot_blocks))
        if d == pairs:
            first, second = [normed_two, *first], [cot, *second]
        held = line(
            lambda t, held, c=second, d=d: hidden_pair(d - 1, pairs, t, c, gate_rows, up_rows, w_down, held), first, held
        )
    all_two, all_cot, all_hidden, all_gate, all_up = held

    def last(v):
        return v[(n - 2) * tokens :]

    def ffn_rows(v, d):
        return v[2 * (d - 1) * tokens : 2 * d * tokens]

    def both(gate, up, gate_rows, up_rows):
        return dot(gate, gate_rows) + dot(up, up_rows)

    def quarter_one(units, rows, got):
        return (dot_rows(units, at.side(rows, "mine other", 4)) + at.side(got, "other").astype(f32)).astype(bf16)

    def quarter_two(units, rows, got, got_y):
        return (dot_rows(units, at.side(rows, "mine y", 4)) + at.side(got, "y").astype(f32) + got_y.astype(f32)).astype(bf16)

    class Reduced:
        def __init__(self, units, rows):
            self.units, self.rows = units, rows

        def one(self):
            self.got = other_core(line(lambda u, r: dot_rows(u, at.side(r, "across")).astype(bf16), self.units, self.rows))

        def two(self):
            self.got_y = other_y(line(quarter_one, self.units, self.rows, self.got))

        def three(self):
            piece = line(quarter_two, self.units, self.rows, self.got, self.got_y)
            self.pieces = [piece, other_y(piece), other_core(piece)]

        def four(self):
            self.pieces[1] = line(lambda v: v, self.pieces[1])
            self.pieces.append(other_core(self.pieces[1]))

        def five(self):
            self.out = line(lambda *p: placed(at.column_place, p, 1), *self.pieces)

    down, gate, up = Reduced(all_hidden, all_cot), Reduced(all_gate, all_two), Reduced(all_up, all_two)
    last_term = line(lambda g, u, *w: both(last(g), last(u), *w), all_gate, all_up, gate_rows, up_rows)
    grad_two = scattered(
        (last_term, all_gate, all_up, gate_rows, up_rows),
        lambda v, *_: v[tokens:],
        lambda d, _, g, u, *w: both(ffn_rows(g, d), ffn_rows(u, d), *w),
        lambda v, *_: v[:tokens],
        [(down.one, gate.one), (down.two,), (gate.two, up.one), (down.three,)],
    )

    def second_back(grad_two):
        grad_middle = cot.astype(f32) + norm_back(grad_two, unit_two, inverse_two, ln2_gain)
        sums = jnp.stack([jnp.sum(grad_two * unit_two, axis=0), jnp.sum(grad_two, axis=0)])
        return grad_middle, grad_middle.astype(bf16), sums

    grad_middle, grad_branch, two_grads = line(second_back, grad_two)

    branch_blocks = Gather(ring, line, grad_branch)
    fill = [(), (gate.three, down.four), (up.two,), (gate.four, down.five)]
    for k in range(pairs):
        for work in fill[k] if k < len(fill) else ():
            work()
        branch_blocks.step()
    grad_joined, outer = line(
        lambda w: attend_back(ring.maps, branch_blocks.blocks, w, qkv, mixed, lse, waves, seen_from), w_out
    )

    grad_w_out = {}

    def out_one():
        grad_w_out["mine"], give = line(lambda v: (at.side(v, "core"), at.side(v, "across").astype(bf16)), outer)
        grad_w_out["got"] = other_core(give)

    def out_two():
        def work(v, got):
            v = v + got.astype(f32)
            return at.side(v, "y"), at.side(v, "other").astype(bf16)

        grad_w_out["mine"], give = line(work, grad_w_out["mine"], grad_w_out["got"])
        grad_w_out["got"] = other_y(give)

    def out_three():
        v = line(lambda v, got: (v + got.astype(f32)).astype(bf16), grad_w_out["mine"], grad_w_out["got"])
        grad_w_out["pieces"] = [v, other_y(v), other_core(v)]

    qkv_grad = {}

    def qkv_one():
        give = line(lambda a, b: dot_rows(a[:, model // 2 :], b).astype(bf16), all_normed, grad_joined)
        qkv_grad["give"], qkv_grad["got"] = give, other_core(give)

    def qkv_local():
        qkv_grad["local"] = line(lambda a, b: dot_rows(a[:, : model // 2], b), all_normed, grad_joined)

    def qkv_two():
        def work(v, got):
            return (v[model // 4 :] + got[model // 4 :].astype(f32)).astype(bf16)

        qkv_grad["got_y"] = other_y(line(work, qkv_grad["local"], qkv_grad["got"]))

    def qkv_three():
        def work(v, got, got_y):
            return (v[: model // 4] + got[: model // 4].astype(f32) + got_y.astype(f32)).astype(bf16)

        piece = line(work, qkv_grad["local"], qkv_grad["got"], qkv_grad["got_y"])
        piece = piece.reshape(n, share, 3 * width)
        qkv_grad["back"] = lax.all_to_all(piece, "seq", split_axis=0, concat_axis=0, tiled=True)

    def to_rows():
        back = line(beside, qkv_grad["back"])
        qkv_grad["rows"], qkv_grad["back_y"], qkv_grad["back_core"] = back, other_y(back), other_core(back)

    def natural(v):
        v = v.reshape(-1, 4, n, share)
        v = [pick(v, at.order[j], 1) for j in range(4)]
        return jnp.stack(v, 2).reshape(-1, model)

    vectors = {}

    def sum_vectors():
        def plain(joined, w, local, give):
            bias = jnp.sum(joined.astype(f32), axis=0)
            w = w.astype(f32)
            shift = natural(jnp.sum(w * bias, axis=1))[0]
            rows = jnp.concatenate([local, give.astype(f32)])
            gain = (natural(jnp.sum(w * rows, axis=1))[0] - ln1_bias * shift) / ln1_gain
            bias_all = jnp.zeros((3, n, width), f32)
            start = (jnp.uint32(0), at.seq, jnp.uint32(0))
            bias_all = lax.dynamic_update_slice(bias_all, bias.reshape(3, 1, width), start).reshape(3, model)
            return jnp.concatenate([jnp.stack([gain, shift]), two_grads, bias_all, jnp.zeros((1, model), f32)])

        def work(*v):
            if share % HEAD_DIM:
                return plain(*v)
            out = jax.ShapeDtypeStruct((8, model), f32)
            kernel = functools.partial(vectors_kernel, n)
            scratch = [pltpu.VMEM((2, model), f32)]
            return once(kernel, "vectors", 16, out, scratch, *v, ln1_bias[None], ln1_gain[None], two_grads, maps=at.peers)

        v = line(work, grad_joined, heads["w"], qkv_grad["local"], qkv_grad["give"])
        vectors["sum"] = v
        vectors["hops"] = [[("batch", 1)], [("batch", 2)], [("seq", k) for k in (1, 2, 3) if k < n]]
        vectors["hops"] += [[("seq", bit)] for bit in bits_of(n)[2:]]
        vectors["other"] = [swap(v, *k) for k in vectors["hops"][0]]

    def vector_step():
        v = line(lambda a, *b: sum_in_order(a, b), vectors["sum"], *vectors["other"])
        vectors["sum"] = v
        vectors["hops"].pop(0)
        if vectors["hops"]:
            vectors["other"] = [swap(v, *k) for k in vectors["hops"][0]]

    def sum_in_order(a, b):
        if len(b) == 1:
            return a + b[0]
        return (a + b[0]) + (b[1] + b[2]) if len(b) == 3 else functools.reduce(jnp.add, b, a)

    def up_back():
        up.got_y = line(lambda v: v, up.got_y)

    def back_done():
        qkv_grad["back_y"] = line(lambda v: v, qkv_grad["back_y"])
        qkv_grad["back_both"] = other_core(qkv_grad["back_y"])

    def out_done():
        v = grad_w_out["pieces"]
        v[1] = line(lambda v: v, v[1])
        v.append(other_core(v[1]))

    def qkv_done():
        parts = (qkv_grad[k] for k in ("rows", "back_y", "back_core", "back_both"))
        qkv_grad["out"] = line(lambda *p: placed(at.row_place, p, 0), *parts)

    up_back()
    qkv_one()
    last = (n - 1) * tokens
    summed = scattered(
        (grad_joined, heads["w"], all_hidden, w_down),
        lambda *v: products(tokens, ((last, True), (last, False)), *v),
        lambda d, first, second, *v: hop(
            tokens, (((2 * d - 1) * tokens, True), (2 * (d - 1) * tokens, False)), v, first, second
        ),
        lambda *v: products(tokens, ((0, True), (last - tokens, False)), *v),
        [
            (qkv_local, qkv_two, sum_vectors, out_one),
            (vector_step, qkv_three, vector_step, up.three, gate.five, up.four, out_two, out_three),
            (to_rows, up.five),
            (back_done, qkv_done, out_done),
        ],
        whole=False,
        fused=True,
    )

    def last_back(term, first, second):
        if share % HEAD_DIM:
            total = term + first.astype(f32) + second.astype(f32)
            back = grad_middle + norm_back(natural(total[:, :model]), unit_one, inverse_one, ln1_gain)
            return back, (middle + total[:, model:]).astype(bf16)
        given = term, first, second, unit_one, inverse_one, ln1_gain[None], grad_middle, middle
        out = jax.ShapeDtypeStruct((tokens, model), f32), jax.ShapeDtypeStruct((tokens, model), bf16)
        return once(functools.partial(last_back_kernel, n), "last_back", 10, out, [], *given, maps=at.peers)

    grad_input, output = line(last_back, *summed)
    vector_step()
    while vectors["hops"]:
        vector_step()
    grad_w_out = line(lambda *p: placed(at.column_place, p, 1), *grad_w_out["pieces"])
    gain_one_sum, bias_one_sum, gain_two_sum, bias_two_sum = (vectors["sum"][i] for i in range(4))
    qkv_bias_sum = vectors["sum"][4:7].reshape(-1)
    return (
        output.reshape(tokens, 1, model),
        grad_input.reshape(tokens, 1, model),
        gain_one_sum,
        bias_one_sum,
        qkv_grad["out"],
        qkv_bias_sum,
        grad_w_out,
        gain_two_sum,
        bias_two_sum,
        gate.out.T,
        up.out.T,
        down.out,
    )


def solution(mesh):
    token, shard, column, whole = P("seq", "batch", None), P("seq", None), P(None, "seq"), P()
    in_specs = (
        token, P("seq", "batch"), whole, whole, shard, whole, shard, whole, whole, column, column, shard, token
    )
    out_specs = (token, token, whole, whole, shard, whole, shard, whole, whole, column, column, shard)
    return jax.shard_map(on_device, mesh=mesh, in_specs=in_specs, out_specs=out_specs, check_vma=False)
```

```python
import functools

import jax
import jax.numpy as jnp
import numpy as np
from jax import lax
from jax.experimental import pallas as pl
from jax.experimental.pallas import tpu as pltpu
from jax.sharding import PartitionSpec as P

HEADS = 32
HEAD_DIM = 64
ROT = 16
BLOCK = 128
TILE = 256

eps_norm = 1e-05
theta_base = 10000.0
masked_score = -1e30
bf16 = jnp.bfloat16
f32 = jnp.float32


def ring_order(n):
    return [0, 2, 4, 6, 7, 5, 3, 1] if n == 8 else list(range(n))


class Ring:
    def __init__(self, axis):
        self.axis = axis
        self.n = n = lax.axis_size(axis)
        order = ring_order(n)
        self.ahead = [(order[i], order[(i + 1) % n]) for i in range(n)]
        self.behind = [(b, a) for a, b in self.ahead]
        half = n // 2
        table = np.zeros((n, 2 * n), np.int32)
        for i, device in enumerate(order):
            for slot in range(n):
                step = -((slot + 1) // 2) if slot % 2 and slot < n - 1 else slot // 2 if slot < n - 1 else half
                natural = order[(i + step) % n]
                table[device, natural], table[device, n + slot] = slot, natural
        self.table = jnp.asarray(table)

    def up(self, v):
        return lax.ppermute(v, self.axis, self.ahead)

    def down(self, v):
        return lax.ppermute(v, self.axis, self.behind)


class Gather:
    def __init__(self, ring, line, v):
        self.ring, self.line, self.d = ring, line, 1
        self.half = v.shape[0] // 2
        self.blocks = [v]
        self.flying = ring.up(v), ring.down(v)

    def step(self):
        got = self.line(lambda *v: v, *self.flying)
        self.blocks += got
        self.d += 1
        last = self.ring.n // 2
        if self.d < last:
            self.flying = self.ring.up(got[0]), self.ring.down(got[1])
        elif self.d == last:
            top, bottom = halves(*got)
            self.flying = self.ring.up(top), self.ring.down(bottom)
        return got


class Line:
    def __init__(self):
        self.last = ()

    def __call__(self, work, *given):
        given, _ = lax.optimization_barrier((given, self.last))
        out = work(*given)
        self.last = out
        return out


def swap(v, axis, bit):
    n = lax.axis_size(axis)
    return lax.ppermute(v, axis, [(i, i ^ bit) for i in range(n)])


def bits_of(n):
    return [1 << i for i in range(n.bit_length() - 1)]


def after(v, *others):
    return lax.optimization_barrier((v, *others))[0]


class Places:
    def __init__(self, model):
        u = functools.partial(jnp.asarray, dtype=jnp.uint32)
        seq, batch = lax.axis_index("seq").astype(jnp.uint32), lax.axis_index("batch").astype(jnp.uint32)
        core, y = batch % u(2), batch // u(2)
        self.seq = seq
        self.quarter = [batch ^ u(k) for k in range(4)]
        self.order = [(q % u(2)) * u(2) + q // u(2) for q in self.quarter]
        self.starts = {
            (name, size): which * u(size)
            for name, which in (("core", core), ("across", u(1) - core), ("y", y), ("other", u(1) - y))
            for size in (model // 2, model // 4)
        }
        for name in ("y", "other"):
            self.starts["mine " + name, model // 4] = (
                self.starts["core", model // 2] + self.starts[name, model // 4]
            )
        self.column_place = jnp.stack([(core * u(2) + y) ^ u(k) for k in range(4)]).astype(jnp.int32)
        self.row_place = jnp.stack([batch ^ u(k) for k in (0, 2, 1, 3)]).astype(jnp.int32)
        peers = [seq ^ u(k) for k in range(lax.axis_size("seq"))]
        self.peers = jnp.stack([batch, *peers]).astype(jnp.int32)

    def scalars(self):
        return [self.seq, *self.quarter, *self.order, *self.starts.values(), self.column_place, self.row_place, self.peers]

    def tied(self, scalars):
        self.seq, self.quarter, self.order = scalars[0], scalars[1:5], scalars[5:9]
        self.starts = dict(zip(self.starts, scalars[9:-3], strict=True))
        self.column_place, self.row_place, self.peers = scalars[-3:]

    def side(self, v, which, parts=2):
        size = v.shape[1] // parts
        return lax.dynamic_slice(v, (jnp.uint32(0), self.starts[which, size]), (v.shape[0], size))


def pick(v, index, axis):
    starts = [jnp.uint32(0)] * v.ndim
    starts[axis] = index
    sizes = list(v.shape)
    sizes[axis] = 1
    return lax.squeeze(lax.dynamic_slice(v, starts, sizes), (axis,))


def norm_parts(values, gain_vector, shift_vector):
    mean_value = jnp.mean(values, axis=-1, keepdims=True)
    centred = values - mean_value
    inverse = lax.rsqrt(jnp.mean(centred * centred, axis=-1, keepdims=True) + eps_norm)
    unit_value = centred * inverse
    return (unit_value * gain_vector + shift_vector, unit_value, inverse)


def norm_back(gradient, unit_value, inverse, gain_vector):
    scaled = gradient * gain_vector
    return inverse * (
        scaled
        - jnp.mean(scaled, axis=-1, keepdims=True)
        - unit_value * jnp.mean(scaled * unit_value, axis=-1, keepdims=True)
    )


def dot(a, b):
    return jnp.dot(a, b, preferred_element_type=f32)


def dot_rows(a, b):
    return lax.dot_general(a, b, (((0,), (0,)), ((), ())), preferred_element_type=f32)


def dot_last(a, b):
    return lax.dot_general(a, b, (((1,), (1,)), ((), ())), preferred_element_type=f32)


def rotary_waves(positions):
    half = ROT // 2
    frequency = theta_base ** (-(jnp.arange(half, dtype=f32) * 2.0 / ROT))
    angles = frequency[:, None] * positions
    return jnp.concatenate([jnp.cos(angles), jnp.sin(angles)], 0)


def fill_table(table_ref, waves_ref):
    half = ROT // 2
    for start in range(0, table_ref.shape[0], BLOCK):
        here = slice(start, start + BLOCK)
        cosine, sine = waves_ref[:half, here], waves_ref[half:, here]
        rest = jnp.zeros((HEAD_DIM - ROT, BLOCK), f32)
        table_ref[here, :] = jnp.concatenate([cosine, cosine, rest + 1.0, -sine, sine, rest], 0).T


def spread_table(table, width):
    own, other = table[:, :HEAD_DIM], table[:, HEAD_DIM:]
    return (jnp.concatenate([v] * (width // HEAD_DIM), 1) for v in (own, other))


def rotate_lanes(x, own, other):
    half = ROT // 2
    width = x.shape[1]
    lane = lax.broadcasted_iota(jnp.int32, x.shape, 1) % HEAD_DIM
    partner = jnp.where(lane < half, pltpu.roll(x, width - half, 1), pltpu.roll(x, half, 1))
    return x * own + partner * other


def visible_to(first_ref, start, keys, tile):
    key = lax.broadcasted_iota(jnp.int32, (keys, tile), 0)
    query = lax.broadcasted_iota(jnp.int32, (keys, tile), 1) + start
    return (key <= query) & (key >= first_ref[0:1, start : start + tile])


def head_rows(x, h):
    if x.shape[0] == HEAD_DIM:
        return x
    row = lax.broadcasted_iota(jnp.int32, x.shape, 0) // HEAD_DIM
    return jnp.where(row == h, x, jnp.zeros_like(x))


def head_lanes(x, h):
    if x.shape[1] == HEAD_DIM:
        return x
    lane = lax.broadcasted_iota(jnp.int32, x.shape, 1) // HEAD_DIM
    return jnp.where(lane == h, x, jnp.zeros_like(x))


def row_list(refs):
    return jnp.concatenate([ref[...] for ref in refs], 0)


def at_block(ref, index):
    return pl.ds(pl.multiple_of(ref[index] * BLOCK, BLOCK), BLOCK)


def grouped(refs, rows):
    groups, held, count = [], [], 0
    for ref in refs:
        held.append(ref)
        count += ref.shape[0]
        if count == rows:
            groups.append(held)
            held, count = [], 0
    return groups


def attend_kernel(blocks, maps_ref, *refs):
    block_refs, refs = refs[:blocks], refs[blocks:]
    piece_refs, refs = refs[:4], refs[4:]
    bias_ref, waves_ref, first_ref, all_ref, qkv_ref, mixed_ref, lse_ref, q_t, v_t, table_ref = refs
    fill_table(table_ref, waves_ref)
    length, width = mixed_ref.shape
    heads = width // HEAD_DIM
    blocks = length // BLOCK
    scale = HEAD_DIM ** (-0.5)
    tile = min(TILE, length)
    depth = piece_refs[0].shape[0]
    for i, group in enumerate(grouped(block_refs, tile)):
        rows = row_list(group)
        all_ref[i * tile : (i + 1) * tile, :] = rows
        x = bias_ref[...] + sum(dot(rows[:, g * depth : (g + 1) * depth], p[...]) for g, p in enumerate(piece_refs))
        for k in range(tile // BLOCK):
            here = at_block(maps_ref, blocks + i * (tile // BLOCK) + k)
            part = x[k * BLOCK : (k + 1) * BLOCK]
            own, other = spread_table(table_ref[here, :], width)
            q = rotate_lanes(part[:, :width], own, other).astype(bf16)
            v = part[:, 2 * width :].astype(bf16)
            qkv_ref[0, here, :] = q
            qkv_ref[1, here, :] = rotate_lanes(part[:, width : 2 * width], own, other).astype(bf16)
            qkv_ref[2, here, :] = v
            q_t[:, here] = (q.astype(f32) * scale).T.astype(bf16)
            v_t[:, here] = v.astype(f32).T.astype(bf16)
    lse_ref[...] = jnp.zeros_like(lse_ref)
    for start in range(0, length, tile):
        keys = start + tile
        seen = visible_to(first_ref, start, keys, tile)
        queries = q_t[:, start : start + tile]
        outs = []
        for h in range(heads):
            scores = dot(qkv_ref[1, :keys, :], head_rows(queries, h))
            scores = jnp.where(seen, scores, masked_score)
            top = jnp.max(scores, axis=0, keepdims=True)
            weights = jnp.exp(scores - top)
            total = jnp.sum(weights, axis=0, keepdims=True)
            lse_ref[h : h + 1, start : start + tile] = top + jnp.log(total)
            out = dot(v_t[h * HEAD_DIM : (h + 1) * HEAD_DIM, :keys], weights.astype(bf16))
            outs.append(out * (1.0 / total))
        out = jnp.concatenate(outs, 0).T.astype(bf16)
        for i in range(tile // BLOCK):
            mixed_ref[at_block(maps_ref, start // BLOCK + i), :] = out[i * BLOCK : (i + 1) * BLOCK]


def attend_back_kernel(blocks, maps_ref, *refs):
    block_refs, refs = refs[:blocks], refs[blocks:]
    w_ref, qkv_ref, mixed_ref, lse_ref, waves_ref, first_ref, out_ref, outer_ref = refs[:8]
    q_t, k_t, g_t, grads, delta, dk, dv, table_ref = refs[8:]
    fill_table(table_ref, waves_ref)
    length, width = mixed_ref.shape
    blocks = length // BLOCK
    heads = width // HEAD_DIM
    scale = HEAD_DIM ** (-0.5)
    tile = min(TILE, length)
    for i, group in enumerate(grouped(block_refs, tile)):
        rows = dot_last(row_list(group), w_ref[...]).astype(bf16)
        for k in range(tile // BLOCK):
            s = i * (tile // BLOCK) + k
            here = at_block(maps_ref, blocks + s)
            g = rows[k * BLOCK : (k + 1) * BLOCK]
            g_flip = g.astype(f32).T
            both = g_flip * mixed_ref[s * BLOCK : (s + 1) * BLOCK, :].astype(f32).T
            for h in range(heads):
                delta[h : h + 1, here] = jnp.sum(both[h * HEAD_DIM : (h + 1) * HEAD_DIM], axis=0, keepdims=True)
            grads[here, :] = g
            g_t[:, here] = g_flip.astype(bf16)
    for j in range(blocks):
        here = slice(j * BLOCK, (j + 1) * BLOCK)
        q_t[:, here] = (qkv_ref[0, here, :].astype(f32) * scale).T.astype(bf16)
        k_t[:, here] = qkv_ref[1, here, :].astype(f32).T.astype(bf16)
    dk[...] = jnp.zeros_like(dk)
    dv[...] = jnp.zeros_like(dv)
    for start in range(0, length, tile):
        keys = start + tile
        here = slice(start, keys)
        seen = visible_to(first_ref, start, keys, tile)
        q_tile, g_tile = q_t[:, here], g_t[:, here]
        q_rows, g_rows = qkv_ref[0, here, :], grads[here, :]
        dq, dk_sum, dv_sum = [], dk[:keys, :], dv[:keys, :]
        for h in range(heads):
            scores = dot(qkv_ref[1, :keys, :], head_rows(q_tile, h))
            prob = jnp.where(seen, jnp.exp(scores - lse_ref[h : h + 1, here]), 0.0)
            grad_prob = dot(qkv_ref[2, :keys, :], head_rows(g_tile, h))
            grad_score = (prob * (grad_prob - delta[h : h + 1, here])).astype(bf16)
            dv_sum += dot(prob.astype(bf16), head_lanes(g_rows, h))
            dk_sum += dot(grad_score, head_lanes(q_rows, h))
            dq.append(dot(k_t[h * HEAD_DIM : (h + 1) * HEAD_DIM, :keys], grad_score))
        dk[:keys, :] = dk_sum
        dv[:keys, :] = dv_sum
        dq = jnp.concatenate(dq, 0).T * scale
        for i in range(tile // BLOCK):
            at = slice(i * BLOCK, (i + 1) * BLOCK)
            place = slice(start + i * BLOCK, start + (i + 1) * BLOCK)
            own, other = spread_table(table_ref[place, :], width)
            turned = rotate_lanes(dq[at], own, -other)
            out_ref[at_block(maps_ref, start // BLOCK + i), :width] = turned.astype(bf16)
    for j in range(blocks):
        rows = at_block(maps_ref, j)
        here = slice(j * BLOCK, (j + 1) * BLOCK)
        own, other = spread_table(table_ref[here, :], width)
        turned = rotate_lanes(dk[here, :] * scale, own, -other)
        out_ref[rows, width : 2 * width] = turned.astype(bf16)
        out_ref[rows, 2 * width :] = dv[here, :].astype(bf16)
    for start in range(0, outer_ref.shape[1], 512):
        columns = slice(start, start + 512)
        outer_ref[:, columns] = sum(
            dot_rows(
                mixed_ref[i * tile : (i + 1) * tile, :], jnp.concatenate([ref[:, columns] for ref in group], 0)
            )
            for i, group in enumerate(grouped(block_refs, tile))
        )


def once(kernel, name, megabytes, out_shape, scratch, *given, maps=None):
    vmem = pl.BlockSpec(memory_space=pltpu.VMEM)
    many = isinstance(out_shape, (tuple, list))
    small = [] if maps is None else [maps]
    return pl.pallas_call(
        kernel,
        out_shape=out_shape,
        in_specs=[pl.BlockSpec(memory_space=pltpu.SMEM)] * len(small) + [vmem] * len(given),
        out_specs=[vmem] * len(out_shape) if many else vmem,
        scratch_shapes=scratch,
        compiler_params=pltpu.CompilerParams(vmem_limit_bytes=megabytes * 2**20),
        cost_estimate=BRIEF,
        name=name,
    )(*small, *given)


BRIEF = pl.CostEstimate(flops=1, bytes_accessed=1, transcendentals=0)


def attend(maps, blocks, pieces, bias, waves, first):
    length, width = waves.shape[1], pieces[0].shape[1] // 3
    return once(
        functools.partial(attend_kernel, len(blocks)),
        "attend",
        16 if length <= 1024 else 40,
        (
            jax.ShapeDtypeStruct((length, blocks[0].shape[1]), bf16),
            jax.ShapeDtypeStruct((3, length, width), bf16),
            jax.ShapeDtypeStruct((length, width), bf16),
            jax.ShapeDtypeStruct((max(8, width // HEAD_DIM), length), f32),
        ),
        [pltpu.VMEM((width, length), bf16), pltpu.VMEM((width, length), bf16), pltpu.VMEM((length, 2 * HEAD_DIM), f32)],
        *blocks,
        *pieces,
        bias,
        waves,
        first,
        maps=maps,
    )


def attend_back(maps, blocks, w_out, qkv, mixed, lse, waves, first):
    length, width = mixed.shape
    return once(
        functools.partial(attend_back_kernel, len(blocks)),
        "attend_back",
        16 if length <= 1024 else 40,
        (
            jax.ShapeDtypeStruct((length, 3 * width), bf16),
            jax.ShapeDtypeStruct((width, blocks[0].shape[1]), f32),
        ),
        [
            pltpu.VMEM((width, length), bf16),
            pltpu.VMEM((width, length), bf16),
            pltpu.VMEM((width, length), bf16),
            pltpu.VMEM((length, width), bf16),
            pltpu.VMEM((lse.shape[0], length), f32),
            pltpu.VMEM((length, width), f32),
            pltpu.VMEM((length, width), f32),
            pltpu.VMEM((length, 2 * HEAD_DIM), f32),
        ],
        *blocks,
        w_out,
        qkv,
        mixed,
        lse,
        waves,
        first,
        maps=maps,
    )


def products_kernel(items, *refs):
    out_ref, offset = refs[-1], 0
    rows = out_ref.shape[0]
    for (start, last), a, b in zip(items, refs[:-1:2], refs[1:-1:2], strict=True):
        width = b.shape[0 if last else 1]
        left = a[start : start + rows, :]
        for begin in range(0, width, 512):
            columns = slice(begin, begin + 512)
            term = dot_last(left, b[columns, :]) if last else dot(left, b[:, columns])
            out_ref[:, offset + begin : offset + begin + 512] = term.astype(out_ref.dtype)
        offset += width


def products(rows, items, *given, dtype=f32):
    width = sum(b.shape[0 if last else 1] for (_, last), b in zip(items, given[1::2], strict=True))
    out = jax.ShapeDtypeStruct((rows, width), dtype)
    return once(functools.partial(products_kernel, items), "products", 8, out, [], *given)


def hop_kernel(term_ref, first_ref, second_ref, ahead_ref, behind_ref):
    rows, half = ahead_ref.shape[0], first_ref.shape[0]
    ahead = term_ref[rows : rows + half, :].astype(f32) + first_ref[...].astype(f32)
    behind = term_ref[rows - half : rows, :].astype(f32) + second_ref[...].astype(f32)
    ahead_ref[:half, :] = ahead.astype(bf16)
    behind_ref[rows - half :, :] = behind.astype(bf16)
    if half < rows:
        ahead_ref[half:, :] = term_ref[rows + half :, :]
        behind_ref[: rows - half, :] = term_ref[: rows - half, :]


def hop(term, first, second):
    out = jax.ShapeDtypeStruct((term.shape[0] // 2, term.shape[1]), bf16)
    return once(hop_kernel, "hop", 8, (out, out), [], term, first, second)


def vectors_kernel(n, peers_ref, joined_ref, w_ref, local_ref, give_ref, shift_ref, gain_ref, two_ref, out_ref, turned):
    width = joined_ref.shape[1] // 3
    ones = jnp.ones((8, joined_ref.shape[0]), bf16)
    bias = dot(ones, joined_ref[...])[0:1]
    parts = []
    for _ in range(3):
        parts.append(bias.astype(bf16).astype(f32))
        bias = bias - parts[-1]
    shift = jnp.sum(dot_last(jnp.concatenate(parts, 0).astype(bf16), w_ref[...]), axis=0, keepdims=True)
    ones = jnp.ones((8, w_ref.shape[1]), bf16)
    half = w_ref.shape[0] // 2
    rows = []
    for start, ref in ((0, local_ref), (half, give_ref)):
        product = w_ref[start : start + half, :].astype(f32) * ref[...].astype(f32)
        upper = product.astype(bf16)
        lower = (product - upper.astype(f32)).astype(bf16)
        rows.append((dot_last(ones, upper) + dot_last(ones, lower))[0:1])
    both = jnp.concatenate([jnp.concatenate(rows, 1), shift], 0)
    for number in range(4):

        @pl.when(peers_ref[0] == number)
        def _(number=number):
            turned[...] = in_plain_order(both, number, n)

    out_ref[...] = jnp.zeros_like(out_ref)
    out_ref[0:1, :] = (turned[0:1, :] - shift_ref[...] * turned[1:2, :]) / gain_ref[...]
    out_ref[1:2, :] = turned[1:2, :]
    out_ref[2:4, :] = two_ref[...]
    total = sum(parts)
    for c in range(3):
        here = pl.ds(pl.multiple_of(peers_ref[1] * width, BLOCK), width)
        out_ref[4 + c : 5 + c, here] = total[:, c * width : (c + 1) * width]


def exchange(blocks):
    return [blocks[0]] + [swap(v, "seq", k) for k, v in enumerate(blocks) if k]


def local(kernel, name, out_shape, smem, given, anywhere=0, scratch=()):
    vmem = pl.BlockSpec(memory_space=pltpu.VMEM)
    many = isinstance(out_shape, (tuple, list))
    return pl.pallas_call(
        kernel,
        out_shape=out_shape,
        in_specs=[pl.BlockSpec(memory_space=pltpu.SMEM)]
        + [pl.BlockSpec(memory_space=pl.ANY)] * anywhere
        + [vmem] * (len(given) - anywhere),
        out_specs=[vmem] * len(out_shape) if many else vmem,
        scratch_shapes=list(scratch),
        compiler_params=pltpu.CompilerParams(vmem_limit_bytes=6 * 2**20),
        cost_estimate=BRIEF,
        name=name,
    )(smem, *given)


def cut_kernel(peers_ref, w_ref, place_ref, *refs):
    outs, semaphores = refs[:-1], refs[-1]
    extra, width = place_ref.shape[0], place_ref.shape[1] // 3
    share, model = outs[0].shape[0] - extra, w_ref.shape[1] // 3
    rows = pl.ds(pl.multiple_of(peers_ref[0] * share, share), share)
    copies = []
    for k, out in enumerate(outs):
        for c in range(3):
            columns = pl.ds(pl.multiple_of(c * model + peers_ref[1 + k] * width, BLOCK), width)
            copies.append(
                pltpu.make_async_copy(
                    w_ref.at[rows, columns],
                    out.at[pl.ds(0, share), pl.ds(c * width, width)],
                    semaphores.at[3 * k + c],
                )
            )
            copies[-1].start()
    for out in outs:
        out[share:, :] = place_ref[...]
    for copy in copies:
        copy.wait()


def cut(at, w, place, n):
    extra, columns = place.shape
    share, width = w.shape[0] // 4, columns // 3
    if width % BLOCK:
        mine = pick(w.reshape(4, share, 3 * width * n), at.quarter[0], 0).reshape(share, 3, n, width)
        mine = [pick(mine, at.seq ^ jnp.uint32(k), 2).reshape(share, columns) for k in range(n)]
        return [jnp.concatenate([v, place]) for v in mine]
    out = jax.ShapeDtypeStruct((share + extra, columns), bf16)
    return local(cut_kernel, "cut", [out] * n, at.peers, (w, place), 1, [pltpu.SemaphoreType.DMA((3 * n,))])


def stack_kernel(peers_ref, *refs):
    ins, (piece_ref, place_ref) = refs[:-2], refs[-2:]
    share = piece_ref.shape[0] // len(ins)
    tokens = place_ref.shape[1] // len(ins)
    for k, ref in enumerate(ins):
        peer = peers_ref[1 + k]
        piece_ref[pl.ds(pl.multiple_of(peer * share, share), share), :] = ref[:share, :]
        place = ref[share:, :tokens].astype(f32)
        place_ref[:, pl.ds(pl.multiple_of(peer * tokens, tokens), tokens)] = place[0:1] * 64.0 + place[1:2]


def stacked(at, blocks, extra, tokens):
    n, (rows, columns) = len(blocks), blocks[0].shape
    shapes = [
        jax.ShapeDtypeStruct((n * (rows - extra), columns), bf16),
        jax.ShapeDtypeStruct((1, n * tokens), f32),
    ]
    return local(stack_kernel, "stacked", shapes, at.peers, blocks)


def in_plain_order(x, number, n):
    share = x.shape[1] // (4 * n)
    order = [(q % 2) * 2 + q // 2 for q in (number ^ j for j in range(4))]
    starts = [order[j] * n * share + s * share for s in range(n) for j in range(4)]
    return jnp.concatenate([x[:, start : start + share] for start in starts], 1)


def last_back_kernel(
    n, peers_ref, term_ref, first_ref, second_ref, unit_ref, inverse_ref, gain_ref, grad_ref, middle_ref, out_ref, sum_ref
):
    total = term_ref[...] + first_ref[...].astype(f32) + second_ref[...].astype(f32)
    model = out_ref.shape[1]
    sum_ref[...] = (middle_ref[...] + total[:, model:]).astype(bf16)
    total = total[:, :model]
    for number in range(4):

        @pl.when(peers_ref[0] == number)
        def _(number=number):
            out_ref[...] = in_plain_order(total, number, n)

    out_ref[...] = grad_ref[...] + norm_back(out_ref[...], unit_ref[...], inverse_ref[...], gain_ref[...])


def beside_kernel(in_ref, out_ref):
    n, _, columns = in_ref.shape
    width = columns // 3
    for k in range(n):
        for c in range(3):
            start = (c * n + k) * width
            out_ref[:, start : start + width] = in_ref[k, :, c * width : (c + 1) * width]


def beside(v):
    n, rows, columns = v.shape
    return once(beside_kernel, "beside", 6, jax.ShapeDtypeStruct((rows, n * columns), bf16), [], v)


def halves_kernel(first_ref, second_ref, top_ref, bottom_ref):
    half = top_ref.shape[0]
    top_ref[...] = first_ref[:half, :]
    bottom_ref[...] = second_ref[half:, :]


def halves(first, second):
    half = jax.ShapeDtypeStruct((first.shape[0] // 2, first.shape[1]), first.dtype)
    vmem = pl.BlockSpec(memory_space=pltpu.VMEM)
    return pl.pallas_call(
        halves_kernel,
        out_shape=(half, half),
        in_specs=[vmem] * 2,
        out_specs=(vmem,) * 2,
        compiler_params=pltpu.CompilerParams(vmem_limit_bytes=4 * 2**20),
        cost_estimate=BRIEF,
        name="halves",
    )(first, second)


def hidden_kernel(at, tokens, cots, held, *refs):
    token_refs, refs = refs[:tokens], refs[tokens:]
    cot_refs, refs = refs[:cots], refs[cots:]
    gate_ref, up_ref, down_ref, refs = refs[0], refs[1], refs[2], refs[3 + held :]
    results, scratch, semaphores = refs[:5], refs[5:10], refs[10]
    rows = scratch[0].shape[0]
    copies = [
        pltpu.make_async_copy(v, out.at[pl.ds(at * rows, rows), :], semaphores.at[i])
        for i, (v, out) in enumerate(zip(scratch, results, strict=True))
    ]
    two, cot, hidden, grad_gate, grad_up = scratch
    two[...] = row_list(token_refs)
    copies[0].start()
    cot[...] = row_list(cot_refs)
    copies[1].start()
    units = gate_ref.shape[0]
    for start in range(0, units, TILE):
        here = slice(start, min(start + TILE, units))
        gate, up = dot_last(two[...], gate_ref[here, :]), dot_last(two[...], up_ref[here, :])
        grad_hidden = dot_last(cot[...], down_ref[here, :])
        sigmoid = 1.0 / (1.0 + jnp.exp(-gate))
        silu = gate * sigmoid
        hidden[:, here] = (silu * up).astype(bf16)
        grad_gate[:, here] = (grad_hidden * up * sigmoid * (1.0 + gate * (1.0 - sigmoid))).astype(bf16)
        grad_up[:, here] = (grad_hidden * silu).astype(bf16)
    for copy in copies[2:]:
        copy.start()
    for copy in copies:
        copy.wait()


def hidden_pair(at, pairs, tokens, cots, gate_rows, up_rows, w_down, held):
    rows = sum(b.shape[0] for b in tokens)
    units, model = gate_rows.shape
    widths = (model, model, units, units, units)
    first = len(tokens) + len(cots) + 3
    hbm = pl.BlockSpec(memory_space=pltpu.HBM)
    return pl.pallas_call(
        functools.partial(hidden_kernel, at, len(tokens), len(cots), len(held)),
        out_shape=[jax.ShapeDtypeStruct((rows * pairs, w), bf16) for w in widths],
        in_specs=[pl.BlockSpec(memory_space=pltpu.VMEM)] * first + [hbm] * len(held),
        out_specs=[hbm] * 5,
        scratch_shapes=[pltpu.VMEM((rows, w), bf16) for w in widths] + [pltpu.SemaphoreType.DMA((5,))],
        input_output_aliases={first + i: i for i in range(len(held))},
        compiler_params=pltpu.CompilerParams(vmem_limit_bytes=12 * 2**20),
        cost_estimate=BRIEF,
        name="hidden_pair",
    )(*tokens, *cots, gate_rows, up_rows, w_down, *held)


def place_kernel(at_ref, *refs):
    out_ref = refs[-1]
    for i, ref in enumerate(refs[:-1]):

        @pl.when(pl.program_id(0) == i)
        def _(ref=ref):
            out_ref[...] = ref[...].astype(f32)


def placed(at, pieces, axis):
    shape = list(pieces[0].shape)
    total = list(shape)
    total[axis] *= len(pieces)
    return pl.pallas_call(
        place_kernel,
        out_shape=jax.ShapeDtypeStruct(tuple(total), f32),
        grid_spec=pltpu.PrefetchScalarGridSpec(
            num_scalar_prefetch=1,
            grid=(len(pieces),),
            in_specs=[pl.BlockSpec(tuple(shape), lambda i, at: (0, 0)) for _ in pieces],
            out_specs=pl.BlockSpec(tuple(shape), lambda i, at: (0, at[i]) if axis else (at[i], 0)),
        ),
        compiler_params=pltpu.CompilerParams(vmem_limit_bytes=16 * 2**20),
        cost_estimate=BRIEF,
        name="placed",
    )(at, *pieces)


def on_device(
    inputs, positions, ln1_gain, ln1_bias, w_qkv, qkv_bias, w_out, ln2_gain, ln2_bias, w_gate, w_up, w_down, cotangent
):
    n = lax.axis_size("seq")
    ring = Ring("seq")
    line = Line()
    tokens, model = inputs.shape[0], inputs.shape[2]
    length = tokens * n
    pairs = n // 2
    width = model // n
    depth = w_qkv.shape[0]
    share = depth // 4
    x = inputs.reshape(tokens, model).astype(f32)
    cot = cotangent.reshape(tokens, model)
    gate_rows, up_rows = w_gate.T, w_up.T
    others = (0, 2, 1, 3)
    at = Places(model)
    at.tied(line(lambda *v: v, *at.scalars()))

    def other_y(v):
        return swap(v, "batch", 2)

    def other_core(v):
        return swap(v, "batch", 1)

    place = positions.reshape(tokens)
    extra = 8
    place = jnp.stack([place // 64, place % 64]).astype(bf16)
    place = jnp.pad(place, ((0, extra - 2), (0, 3 * width - tokens)))
    fetched = exchange(line(lambda w, place: cut(at, w, place, n), w_qkv, place))
    bias_heads = line(lambda v: pick(v.reshape(3, n, width), at.seq, 1).reshape(1, 3 * width), qkv_bias)

    def first_norm(x):
        normed, unit, inverse = norm_parts(x, ln1_gain, ln1_bias)
        normed = normed.astype(bf16).reshape(tokens, n, 4, share)
        normed = [pick(normed, at.quarter[k], 2).reshape(tokens, -1) for k in others]
        return jnp.concatenate(normed, 1), unit, inverse

    normed, unit_one, inverse_one = line(first_norm, x)
    normed_blocks = Gather(ring, line, after(normed, fetched[1]))

    piece, places = line(lambda *v: stacked(at, v, extra, tokens), *fetched)
    piece_y, piece_core = other_y(piece), other_core(piece)
    normed_blocks.step()

    def take(places, maps):
        maps = pick(maps, at.seq, 0)
        first = jnp.arange(length, dtype=jnp.int32)[None] - places.astype(jnp.int32)
        return maps, rotary_waves(places), first

    normed_blocks.step()
    ring.maps, waves, seen_from = line(take, places, ring.table)
    piece_core = line(lambda v: v, piece_core)
    for _ in range(pairs - 3):
        normed_blocks.step()
    piece_y = line(lambda v: v, piece_y)
    piece_both = other_core(piece_y)
    normed_blocks.step()
    cot_blocks = Gather(ring, line, cot)
    pieces = [piece, piece_y, piece_core, piece_both]
    all_normed, qkv, mixed, lse = line(
        lambda pieces: attend(ring.maps, normed_blocks.blocks, pieces, bias_heads, waves, seen_from), pieces
    )

    def block(v, i):
        return v[i * tokens : (i + 1) * tokens]

    class Scatter:
        def __init__(self, given, far, pair, own, fused=False):
            self.given, self.pair, self.own, self.fused = given, pair, own, fused
            top, bottom = line(lambda *v: halves(*[far(*v).astype(bf16)] * 2), *given)
            self.first, self.second = ring.up(top), ring.down(bottom)
            self.d = pairs - 1
            self.term = line(lambda *v: pair(self.d, *v), *given)

        def step(self):
            half = tokens // 2

            def add(term, first, second):
                first, second = first.astype(f32), second.astype(f32)
                if self.d == pairs - 1:
                    first = jnp.pad(first, ((0, half), (0, 0)))
                    second = jnp.pad(second, ((half, 0), (0, 0)))
                return (term[tokens:] + first).astype(bf16), (term[:tokens] + second).astype(bf16)

            if self.fused:
                first, second = line(hop, self.term, self.first, self.second)
            else:
                first, second = line(add, self.term, self.first, self.second)
            self.first, self.second = ring.up(first), ring.down(second)
            self.d -= 1
            self.term = line(lambda *v: self.pair(self.d, *v) if self.d else self.own(*v), *self.given)

        def parts(self):
            return self.term, self.first, self.second

        def finish(self):
            return line(lambda a, b, c: a + b.astype(f32) + c.astype(f32), *self.parts())

    def scattered(given, far, pair, own, fill, whole=True, fused=False):
        going = Scatter(given, far, pair, own, fused)
        for k in range(pairs):
            for work in fill[k] if k < len(fill) else ():
                work()
            if k < pairs - 1:
                going.step()
        return going.finish() if whole else going.parts()

    def pair_rows(v, d):
        return v[(2 * d - 1) * tokens : (2 * d + 1) * tokens]

    heads = {}

    def join_heads():
        heads["w"] = line(lambda *p: jnp.concatenate(p), *pieces)

    cot_step = cot_blocks.step
    branch = scattered(
        (mixed, w_out),
        lambda v, w: dot(block(v, n - 1), w),
        lambda d, v, w: dot(pair_rows(v, d), w),
        lambda v, w: dot(block(v, 0), w),
        [(cot_step,), (cot_step,), (cot_step,), (join_heads,)],
    )

    def second_norm(x, branch):
        middle = x + branch
        normed, unit, inverse = norm_parts(middle, ln2_gain, ln2_bias)
        return normed.astype(bf16), middle, unit, inverse

    normed_two, middle, unit_two, inverse_two = line(second_norm, x, branch)
    two_blocks = Gather(ring, line, normed_two)
    while len(cot_blocks.blocks) < n + 1:
        cot_blocks.step()
    held = []
    for d in range(1, pairs + 1):
        two_blocks.step()
        first, second = (v.blocks[2 * d - 1 : 2 * d + 1] for v in (two_blocks, cot_blocks))
        if d == pairs:
            first, second = [normed_two, *first], [cot, *second]
        held = line(
            lambda t, held, c=second, d=d: hidden_pair(d - 1, pairs, t, c, gate_rows, up_rows, w_down, held), first, held
        )
    all_two, all_cot, all_hidden, all_gate, all_up = held

    def last(v):
        return v[(n - 2) * tokens :]

    def ffn_rows(v, d):
        return v[2 * (d - 1) * tokens : 2 * d * tokens]

    def both(gate, up, gate_rows, up_rows):
        return dot(gate, gate_rows) + dot(up, up_rows)

    def quarter_one(units, rows, got):
        return (dot_rows(units, at.side(rows, "mine other", 4)) + at.side(got, "other").astype(f32)).astype(bf16)

    def quarter_two(units, rows, got, got_y):
        return (dot_rows(units, at.side(rows, "mine y", 4)) + at.side(got, "y").astype(f32) + got_y.astype(f32)).astype(bf16)

    class Reduced:
        def __init__(self, units, rows):
            self.units, self.rows = units, rows

        def one(self):
            self.got = other_core(line(lambda u, r: dot_rows(u, at.side(r, "across")).astype(bf16), self.units, self.rows))

        def two(self):
            self.got_y = other_y(line(quarter_one, self.units, self.rows, self.got))

        def three(self):
            piece = line(quarter_two, self.units, self.rows, self.got, self.got_y)
            self.pieces = [piece, other_y(piece), other_core(piece)]

        def four(self):
            self.pieces[1] = line(lambda v: v, self.pieces[1])
            self.pieces.append(other_core(self.pieces[1]))

        def five(self):
            self.out = line(lambda *p: placed(at.column_place, p, 1), *self.pieces)

    down, gate, up = Reduced(all_hidden, all_cot), Reduced(all_gate, all_two), Reduced(all_up, all_two)
    last_term = line(lambda g, u, *w: both(last(g), last(u), *w), all_gate, all_up, gate_rows, up_rows)
    grad_two = scattered(
        (last_term, all_gate, all_up, gate_rows, up_rows),
        lambda v, *_: v[tokens:],
        lambda d, _, g, u, *w: both(ffn_rows(g, d), ffn_rows(u, d), *w),
        lambda v, *_: v[:tokens],
        [(down.one, gate.one), (down.two,), (gate.two, up.one), (down.three,)],
    )

    def second_back(grad_two):
        grad_middle = cot.astype(f32) + norm_back(grad_two, unit_two, inverse_two, ln2_gain)
        sums = jnp.stack([jnp.sum(grad_two * unit_two, axis=0), jnp.sum(grad_two, axis=0)])
        return grad_middle, grad_middle.astype(bf16), sums

    grad_middle, grad_branch, two_grads = line(second_back, grad_two)

    branch_blocks = Gather(ring, line, grad_branch)
    fill = [(), (gate.three, down.four), (up.two,), (gate.four, down.five)]
    for k in range(pairs):
        for work in fill[k] if k < len(fill) else ():
            work()
        branch_blocks.step()
    grad_joined, outer = line(
        lambda w: attend_back(ring.maps, branch_blocks.blocks, w, qkv, mixed, lse, waves, seen_from), w_out
    )

    grad_w_out = {}

    def out_one():
        grad_w_out["mine"], give = line(lambda v: (at.side(v, "core"), at.side(v, "across").astype(bf16)), outer)
        grad_w_out["got"] = other_core(give)

    def out_two():
        def work(v, got):
            v = v + got.astype(f32)
            return at.side(v, "y"), at.side(v, "other").astype(bf16)

        grad_w_out["mine"], give = line(work, grad_w_out["mine"], grad_w_out["got"])
        grad_w_out["got"] = other_y(give)

    def out_three():
        v = line(lambda v, got: (v + got.astype(f32)).astype(bf16), grad_w_out["mine"], grad_w_out["got"])
        grad_w_out["pieces"] = [v, other_y(v), other_core(v)]

    qkv_grad = {}

    def qkv_one():
        give = line(lambda a, b: dot_rows(a[:, model // 2 :], b).astype(bf16), all_normed, grad_joined)
        qkv_grad["give"], qkv_grad["got"] = give, other_core(give)

    def qkv_local():
        qkv_grad["local"] = line(lambda a, b: dot_rows(a[:, : model // 2], b), all_normed, grad_joined)

    def qkv_two():
        def work(v, got):
            return (v[model // 4 :] + got[model // 4 :].astype(f32)).astype(bf16)

        qkv_grad["got_y"] = other_y(line(work, qkv_grad["local"], qkv_grad["got"]))

    def qkv_three():
        def work(v, got, got_y):
            return (v[: model // 4] + got[: model // 4].astype(f32) + got_y.astype(f32)).astype(bf16)

        piece = line(work, qkv_grad["local"], qkv_grad["got"], qkv_grad["got_y"])
        piece = piece.reshape(n, share, 3 * width)
        qkv_grad["back"] = lax.all_to_all(piece, "seq", split_axis=0, concat_axis=0, tiled=True)

    def to_rows():
        back = line(beside, qkv_grad["back"])
        qkv_grad["rows"], qkv_grad["back_y"], qkv_grad["back_core"] = back, other_y(back), other_core(back)

    def natural(v):
        v = v.reshape(-1, 4, n, share)
        v = [pick(v, at.order[j], 1) for j in range(4)]
        return jnp.stack(v, 2).reshape(-1, model)

    vectors = {}

    def sum_vectors():
        def plain(joined, w, local, give):
            bias = jnp.sum(joined.astype(f32), axis=0)
            w = w.astype(f32)
            shift = natural(jnp.sum(w * bias, axis=1))[0]
            rows = jnp.concatenate([local, give.astype(f32)])
            gain = (natural(jnp.sum(w * rows, axis=1))[0] - ln1_bias * shift) / ln1_gain
            bias_all = jnp.zeros((3, n, width), f32)
            start = (jnp.uint32(0), at.seq, jnp.uint32(0))
            bias_all = lax.dynamic_update_slice(bias_all, bias.reshape(3, 1, width), start).reshape(3, model)
            return jnp.concatenate([jnp.stack([gain, shift]), two_grads, bias_all, jnp.zeros((1, model), f32)])

        def work(*v):
            if share % HEAD_DIM:
                return plain(*v)
            out = jax.ShapeDtypeStruct((8, model), f32)
            kernel = functools.partial(vectors_kernel, n)
            scratch = [pltpu.VMEM((2, model), f32)]
            return once(kernel, "vectors", 16, out, scratch, *v, ln1_bias[None], ln1_gain[None], two_grads, maps=at.peers)

        v = line(work, grad_joined, heads["w"], qkv_grad["local"], qkv_grad["give"])
        vectors["sum"] = v
        vectors["hops"] = [[("batch", 1)], [("batch", 2)], [("seq", k) for k in (1, 2, 3) if k < n]]
        vectors["hops"] += [[("seq", bit)] for bit in bits_of(n)[2:]]
        vectors["other"] = [swap(v, *k) for k in vectors["hops"][0]]

    def vector_step():
        v = line(lambda a, *b: sum_in_order(a, b), vectors["sum"], *vectors["other"])
        vectors["sum"] = v
        vectors["hops"].pop(0)
        if vectors["hops"]:
            vectors["other"] = [swap(v, *k) for k in vectors["hops"][0]]

    def sum_in_order(a, b):
        if len(b) == 1:
            return a + b[0]
        return (a + b[0]) + (b[1] + b[2]) if len(b) == 3 else functools.reduce(jnp.add, b, a)

    def up_back():
        up.got_y = line(lambda v: v, up.got_y)

    def back_done():
        qkv_grad["back_y"] = line(lambda v: v, qkv_grad["back_y"])
        qkv_grad["back_both"] = other_core(qkv_grad["back_y"])

    def out_done():
        v = grad_w_out["pieces"]
        v[1] = line(lambda v: v, v[1])
        v.append(other_core(v[1]))

    def qkv_done():
        parts = (qkv_grad[k] for k in ("rows", "back_y", "back_core", "back_both"))
        qkv_grad["out"] = line(lambda *p: placed(at.row_place, p, 0), *parts)

    up_back()
    qkv_one()
    last = (n - 1) * tokens
    summed = scattered(
        (grad_joined, heads["w"], all_hidden, w_down),
        lambda *v: products(tokens, ((last, True), (last, False)), *v),
        lambda d, *v: products(
            2 * tokens, (((2 * d - 1) * tokens, True), (2 * (d - 1) * tokens, False)), *v, dtype=bf16
        ),
        lambda *v: products(tokens, ((0, True), (last - tokens, False)), *v),
        [
            (qkv_local, qkv_two, sum_vectors, up.three, gate.five, vector_step),
            (qkv_three, up.four, vector_step, out_one),
            (out_two, to_rows, out_three, up.five),
            (back_done, qkv_done),
        ],
        whole=False,
        fused=True,
    )

    def last_back(term, first, second):
        if share % HEAD_DIM:
            total = term + first.astype(f32) + second.astype(f32)
            back = grad_middle + norm_back(natural(total[:, :model]), unit_one, inverse_one, ln1_gain)
            return back, (middle + total[:, model:]).astype(bf16)
        given = term, first, second, unit_one, inverse_one, ln1_gain[None], grad_middle, middle
        out = jax.ShapeDtypeStruct((tokens, model), f32), jax.ShapeDtypeStruct((tokens, model), bf16)
        return once(functools.partial(last_back_kernel, n), "last_back", 10, out, [], *given, maps=at.peers)

    grad_input, output = line(last_back, *summed)
    vector_step()
    out_done()
    while vectors["hops"]:
        vector_step()
    grad_w_out = line(lambda *p: placed(at.column_place, p, 1), *grad_w_out["pieces"])
    gain_one_sum, bias_one_sum, gain_two_sum, bias_two_sum = (vectors["sum"][i] for i in range(4))
    qkv_bias_sum = vectors["sum"][4:7].reshape(-1)
    return (
        output.reshape(tokens, 1, model),
        grad_input.reshape(tokens, 1, model),
        gain_one_sum,
        bias_one_sum,
        qkv_grad["out"],
        qkv_bias_sum,
        grad_w_out,
        gain_two_sum,
        bias_two_sum,
        gate.out.T,
        up.out.T,
        down.out,
    )


def solution(mesh):
    token, shard, column, whole = P("seq", "batch", None), P("seq", None), P(None, "seq"), P()
    in_specs = (
        token, P("seq", "batch"), whole, whole, shard, whole, shard, whole, whole, column, column, shard, token
    )
    out_specs = (token, token, whole, whole, shard, whole, shard, whole, whole, column, column, shard)
    return jax.shard_map(on_device, mesh=mesh, in_specs=in_specs, out_specs=out_specs, check_vma=False)
```

```python
import functools

import jax
import jax.numpy as jnp
import numpy as np
from jax import lax
from jax.experimental import pallas as pl
from jax.experimental.pallas import tpu as pltpu
from jax.sharding import PartitionSpec as P

HEADS = 32
HEAD_DIM = 64
ROT = 16
BLOCK = 128
TILE = 256

eps_norm = 1e-05
theta_base = 10000.0
masked_score = -1e30
bf16 = jnp.bfloat16
f32 = jnp.float32


def ring_order(n):
    return [0, 2, 4, 6, 7, 5, 3, 1] if n == 8 else list(range(n))


class Ring:
    def __init__(self, axis):
        self.axis = axis
        self.n = n = lax.axis_size(axis)
        order = ring_order(n)
        self.ahead = [(order[i], order[(i + 1) % n]) for i in range(n)]
        self.behind = [(b, a) for a, b in self.ahead]
        half = n // 2
        table = np.zeros((n, 2 * n), np.int32)
        for i, device in enumerate(order):
            for slot in range(n):
                step = -((slot + 1) // 2) if slot % 2 and slot < n - 1 else slot // 2 if slot < n - 1 else half
                natural = order[(i + step) % n]
                table[device, natural], table[device, n + slot] = slot, natural
        self.table = jnp.asarray(table)

    def up(self, v):
        return lax.ppermute(v, self.axis, self.ahead)

    def down(self, v):
        return lax.ppermute(v, self.axis, self.behind)


class Gather:
    def __init__(self, ring, line, v):
        self.ring, self.line, self.d = ring, line, 1
        self.half = v.shape[0] // 2
        self.blocks = [v]
        self.flying = ring.up(v), ring.down(v)

    def step(self):
        got = self.line(lambda *v: v, *self.flying)
        self.blocks += got
        self.d += 1
        last = self.ring.n // 2
        if self.d < last:
            self.flying = self.ring.up(got[0]), self.ring.down(got[1])
        elif self.d == last:
            top, bottom = halves(*got)
            self.flying = self.ring.up(top), self.ring.down(bottom)
        return got


class Line:
    def __init__(self):
        self.last = ()

    def __call__(self, work, *given):
        given, _ = lax.optimization_barrier((given, self.last))
        out = work(*given)
        self.last = out
        return out


def swap(v, axis, bit):
    n = lax.axis_size(axis)
    return lax.ppermute(v, axis, [(i, i ^ bit) for i in range(n)])


def bits_of(n):
    return [1 << i for i in range(n.bit_length() - 1)]


def after(v, *others):
    return lax.optimization_barrier((v, *others))[0]


class Places:
    def __init__(self, model):
        u = functools.partial(jnp.asarray, dtype=jnp.uint32)
        seq, batch = lax.axis_index("seq").astype(jnp.uint32), lax.axis_index("batch").astype(jnp.uint32)
        core, y = batch % u(2), batch // u(2)
        self.seq = seq
        self.quarter = [batch ^ u(k) for k in range(4)]
        self.order = [(q % u(2)) * u(2) + q // u(2) for q in self.quarter]
        self.starts = {
            (name, size): which * u(size)
            for name, which in (("core", core), ("across", u(1) - core), ("y", y), ("other", u(1) - y))
            for size in (model // 2, model // 4)
        }
        for name in ("y", "other"):
            self.starts["mine " + name, model // 4] = (
                self.starts["core", model // 2] + self.starts[name, model // 4]
            )
        self.column_place = jnp.stack([(core * u(2) + y) ^ u(k) for k in range(4)]).astype(jnp.int32)
        self.row_place = jnp.stack([batch ^ u(k) for k in (0, 2, 1, 3)]).astype(jnp.int32)
        peers = [seq ^ u(k) for k in range(lax.axis_size("seq"))]
        self.peers = jnp.stack([batch, *peers]).astype(jnp.int32)

    def scalars(self):
        return [self.seq, *self.quarter, *self.order, *self.starts.values(), self.column_place, self.row_place, self.peers]

    def tied(self, scalars):
        self.seq, self.quarter, self.order = scalars[0], scalars[1:5], scalars[5:9]
        self.starts = dict(zip(self.starts, scalars[9:-3], strict=True))
        self.column_place, self.row_place, self.peers = scalars[-3:]

    def side(self, v, which, parts=2):
        size = v.shape[1] // parts
        return lax.dynamic_slice(v, (jnp.uint32(0), self.starts[which, size]), (v.shape[0], size))


def pick(v, index, axis):
    starts = [jnp.uint32(0)] * v.ndim
    starts[axis] = index
    sizes = list(v.shape)
    sizes[axis] = 1
    return lax.squeeze(lax.dynamic_slice(v, starts, sizes), (axis,))


def norm_parts(values, gain_vector, shift_vector):
    mean_value = jnp.mean(values, axis=-1, keepdims=True)
    centred = values - mean_value
    inverse = lax.rsqrt(jnp.mean(centred * centred, axis=-1, keepdims=True) + eps_norm)
    unit_value = centred * inverse
    return (unit_value * gain_vector + shift_vector, unit_value, inverse)


def norm_back(gradient, unit_value, inverse, gain_vector):
    scaled = gradient * gain_vector
    return inverse * (
        scaled
        - jnp.mean(scaled, axis=-1, keepdims=True)
        - unit_value * jnp.mean(scaled * unit_value, axis=-1, keepdims=True)
    )


def dot(a, b):
    return jnp.dot(a, b, preferred_element_type=f32)


def dot_rows(a, b):
    return lax.dot_general(a, b, (((0,), (0,)), ((), ())), preferred_element_type=f32)


def dot_last(a, b):
    return lax.dot_general(a, b, (((1,), (1,)), ((), ())), preferred_element_type=f32)


def rotary_waves(positions):
    half = ROT // 2
    frequency = theta_base ** (-(jnp.arange(half, dtype=f32) * 2.0 / ROT))
    angles = frequency[:, None] * positions
    return jnp.concatenate([jnp.cos(angles), jnp.sin(angles)], 0)


def fill_table(table_ref, waves_ref):
    half = ROT // 2
    for start in range(0, table_ref.shape[0], BLOCK):
        here = slice(start, start + BLOCK)
        cosine, sine = waves_ref[:half, here], waves_ref[half:, here]
        rest = jnp.zeros((HEAD_DIM - ROT, BLOCK), f32)
        table_ref[here, :] = jnp.concatenate([cosine, cosine, rest + 1.0, -sine, sine, rest], 0).T


def spread_table(table, width):
    own, other = table[:, :HEAD_DIM], table[:, HEAD_DIM:]
    return (jnp.concatenate([v] * (width // HEAD_DIM), 1) for v in (own, other))


def rotate_lanes(x, own, other):
    half = ROT // 2
    width = x.shape[1]
    lane = lax.broadcasted_iota(jnp.int32, x.shape, 1) % HEAD_DIM
    partner = jnp.where(lane < half, pltpu.roll(x, width - half, 1), pltpu.roll(x, half, 1))
    return x * own + partner * other


def visible_to(first_ref, start, keys, tile):
    key = lax.broadcasted_iota(jnp.int32, (keys, tile), 0)
    query = lax.broadcasted_iota(jnp.int32, (keys, tile), 1) + start
    return (key <= query) & (key >= first_ref[0:1, start : start + tile])


def head_rows(x, h):
    if x.shape[0] == HEAD_DIM:
        return x
    row = lax.broadcasted_iota(jnp.int32, x.shape, 0) // HEAD_DIM
    return jnp.where(row == h, x, jnp.zeros_like(x))


def head_lanes(x, h):
    if x.shape[1] == HEAD_DIM:
        return x
    lane = lax.broadcasted_iota(jnp.int32, x.shape, 1) // HEAD_DIM
    return jnp.where(lane == h, x, jnp.zeros_like(x))


def row_list(refs):
    return jnp.concatenate([ref[...] for ref in refs], 0)


def at_block(ref, index):
    return pl.ds(pl.multiple_of(ref[index] * BLOCK, BLOCK), BLOCK)


def grouped(refs, rows):
    groups, held, count = [], [], 0
    for ref in refs:
        held.append(ref)
        count += ref.shape[0]
        if count == rows:
            groups.append(held)
            held, count = [], 0
    return groups


def attend_kernel(blocks, maps_ref, *refs):
    block_refs, refs = refs[:blocks], refs[blocks:]
    piece_refs, refs = refs[:4], refs[4:]
    bias_ref, waves_ref, first_ref, all_ref, qkv_ref, mixed_ref, lse_ref, q_t, v_t, table_ref = refs
    fill_table(table_ref, waves_ref)
    length, width = mixed_ref.shape
    heads = width // HEAD_DIM
    blocks = length // BLOCK
    scale = HEAD_DIM ** (-0.5)
    tile = min(TILE, length)
    depth = piece_refs[0].shape[0]
    for i, group in enumerate(grouped(block_refs, tile)):
        rows = row_list(group)
        all_ref[i * tile : (i + 1) * tile, :] = rows
        x = bias_ref[...] + sum(dot(rows[:, g * depth : (g + 1) * depth], p[...]) for g, p in enumerate(piece_refs))
        for k in range(tile // BLOCK):
            here = at_block(maps_ref, blocks + i * (tile // BLOCK) + k)
            part = x[k * BLOCK : (k + 1) * BLOCK]
            own, other = spread_table(table_ref[here, :], width)
            q = rotate_lanes(part[:, :width], own, other).astype(bf16)
            v = part[:, 2 * width :].astype(bf16)
            qkv_ref[0, here, :] = q
            qkv_ref[1, here, :] = rotate_lanes(part[:, width : 2 * width], own, other).astype(bf16)
            qkv_ref[2, here, :] = v
            q_t[:, here] = (q.astype(f32) * scale).T.astype(bf16)
            v_t[:, here] = v.astype(f32).T.astype(bf16)
    lse_ref[...] = jnp.zeros_like(lse_ref)
    for start in range(0, length, tile):
        keys = start + tile
        seen = visible_to(first_ref, start, keys, tile)
        queries = q_t[:, start : start + tile]
        outs = []
        for h in range(heads):
            scores = dot(qkv_ref[1, :keys, :], head_rows(queries, h))
            scores = jnp.where(seen, scores, masked_score)
            top = jnp.max(scores, axis=0, keepdims=True)
            weights = jnp.exp(scores - top)
            total = jnp.sum(weights, axis=0, keepdims=True)
            lse_ref[h : h + 1, start : start + tile] = top + jnp.log(total)
            out = dot(v_t[h * HEAD_DIM : (h + 1) * HEAD_DIM, :keys], weights.astype(bf16))
            outs.append(out * (1.0 / total))
        out = jnp.concatenate(outs, 0).T.astype(bf16)
        for i in range(tile // BLOCK):
            mixed_ref[at_block(maps_ref, start // BLOCK + i), :] = out[i * BLOCK : (i + 1) * BLOCK]


def attend_back_kernel(blocks, maps_ref, *refs):
    block_refs, refs = refs[:blocks], refs[blocks:]
    w_ref, qkv_ref, mixed_ref, lse_ref, waves_ref, first_ref, out_ref, outer_ref = refs[:8]
    q_t, k_t, g_t, grads, delta, dk, dv, table_ref = refs[8:]
    fill_table(table_ref, waves_ref)
    length, width = mixed_ref.shape
    blocks = length // BLOCK
    heads = width // HEAD_DIM
    scale = HEAD_DIM ** (-0.5)
    tile = min(TILE, length)
    for i, group in enumerate(grouped(block_refs, tile)):
        rows = dot_last(row_list(group), w_ref[...]).astype(bf16)
        for k in range(tile // BLOCK):
            s = i * (tile // BLOCK) + k
            here = at_block(maps_ref, blocks + s)
            g = rows[k * BLOCK : (k + 1) * BLOCK]
            g_flip = g.astype(f32).T
            both = g_flip * mixed_ref[s * BLOCK : (s + 1) * BLOCK, :].astype(f32).T
            for h in range(heads):
                delta[h : h + 1, here] = jnp.sum(both[h * HEAD_DIM : (h + 1) * HEAD_DIM], axis=0, keepdims=True)
            grads[here, :] = g
            g_t[:, here] = g_flip.astype(bf16)
    for j in range(blocks):
        here = slice(j * BLOCK, (j + 1) * BLOCK)
        q_t[:, here] = (qkv_ref[0, here, :].astype(f32) * scale).T.astype(bf16)
        k_t[:, here] = qkv_ref[1, here, :].astype(f32).T.astype(bf16)
    dk[...] = jnp.zeros_like(dk)
    dv[...] = jnp.zeros_like(dv)
    for start in range(0, length, tile):
        keys = start + tile
        here = slice(start, keys)
        seen = visible_to(first_ref, start, keys, tile)
        q_tile, g_tile = q_t[:, here], g_t[:, here]
        q_rows, g_rows = qkv_ref[0, here, :], grads[here, :]
        dq, dk_sum, dv_sum = [], dk[:keys, :], dv[:keys, :]
        for h in range(heads):
            scores = dot(qkv_ref[1, :keys, :], head_rows(q_tile, h))
            prob = jnp.where(seen, jnp.exp(scores - lse_ref[h : h + 1, here]), 0.0)
            grad_prob = dot(qkv_ref[2, :keys, :], head_rows(g_tile, h))
            grad_score = (prob * (grad_prob - delta[h : h + 1, here])).astype(bf16)
            dv_sum += dot(prob.astype(bf16), head_lanes(g_rows, h))
            dk_sum += dot(grad_score, head_lanes(q_rows, h))
            dq.append(dot(k_t[h * HEAD_DIM : (h + 1) * HEAD_DIM, :keys], grad_score))
        dk[:keys, :] = dk_sum
        dv[:keys, :] = dv_sum
        dq = jnp.concatenate(dq, 0).T * scale
        for i in range(tile // BLOCK):
            at = slice(i * BLOCK, (i + 1) * BLOCK)
            place = slice(start + i * BLOCK, start + (i + 1) * BLOCK)
            own, other = spread_table(table_ref[place, :], width)
            turned = rotate_lanes(dq[at], own, -other)
            out_ref[at_block(maps_ref, start // BLOCK + i), :width] = turned.astype(bf16)
    for j in range(blocks):
        rows = at_block(maps_ref, j)
        here = slice(j * BLOCK, (j + 1) * BLOCK)
        own, other = spread_table(table_ref[here, :], width)
        turned = rotate_lanes(dk[here, :] * scale, own, -other)
        out_ref[rows, width : 2 * width] = turned.astype(bf16)
        out_ref[rows, 2 * width :] = dv[here, :].astype(bf16)
    for start in range(0, outer_ref.shape[1], 512):
        columns = slice(start, start + 512)
        outer_ref[:, columns] = sum(
            dot_rows(
                mixed_ref[i * tile : (i + 1) * tile, :], jnp.concatenate([ref[:, columns] for ref in group], 0)
            )
            for i, group in enumerate(grouped(block_refs, tile))
        )


def once(kernel, name, megabytes, out_shape, scratch, *given, maps=None):
    vmem = pl.BlockSpec(memory_space=pltpu.VMEM)
    many = isinstance(out_shape, (tuple, list))
    small = [] if maps is None else [maps]
    return pl.pallas_call(
        kernel,
        out_shape=out_shape,
        in_specs=[pl.BlockSpec(memory_space=pltpu.SMEM)] * len(small) + [vmem] * len(given),
        out_specs=[vmem] * len(out_shape) if many else vmem,
        scratch_shapes=scratch,
        compiler_params=pltpu.CompilerParams(vmem_limit_bytes=megabytes * 2**20),
        cost_estimate=BRIEF,
        name=name,
    )(*small, *given)


BRIEF = pl.CostEstimate(flops=1, bytes_accessed=1, transcendentals=0)


def attend(maps, blocks, pieces, bias, waves, first):
    length, width = waves.shape[1], pieces[0].shape[1] // 3
    return once(
        functools.partial(attend_kernel, len(blocks)),
        "attend",
        16 if length <= 1024 else 40,
        (
            jax.ShapeDtypeStruct((length, blocks[0].shape[1]), bf16),
            jax.ShapeDtypeStruct((3, length, width), bf16),
            jax.ShapeDtypeStruct((length, width), bf16),
            jax.ShapeDtypeStruct((max(8, width // HEAD_DIM), length), f32),
        ),
        [pltpu.VMEM((width, length), bf16), pltpu.VMEM((width, length), bf16), pltpu.VMEM((length, 2 * HEAD_DIM), f32)],
        *blocks,
        *pieces,
        bias,
        waves,
        first,
        maps=maps,
    )


def attend_back(maps, blocks, w_out, qkv, mixed, lse, waves, first):
    length, width = mixed.shape
    return once(
        functools.partial(attend_back_kernel, len(blocks)),
        "attend_back",
        16 if length <= 1024 else 40,
        (
            jax.ShapeDtypeStruct((length, 3 * width), bf16),
            jax.ShapeDtypeStruct((width, blocks[0].shape[1]), f32),
        ),
        [
            pltpu.VMEM((width, length), bf16),
            pltpu.VMEM((width, length), bf16),
            pltpu.VMEM((width, length), bf16),
            pltpu.VMEM((length, width), bf16),
            pltpu.VMEM((lse.shape[0], length), f32),
            pltpu.VMEM((length, width), f32),
            pltpu.VMEM((length, width), f32),
            pltpu.VMEM((length, 2 * HEAD_DIM), f32),
        ],
        *blocks,
        w_out,
        qkv,
        mixed,
        lse,
        waves,
        first,
        maps=maps,
    )


def products_kernel(items, *refs):
    out_ref, offset = refs[-1], 0
    rows = out_ref.shape[0]
    for (start, last), a, b in zip(items, refs[:-1:2], refs[1:-1:2], strict=True):
        width = b.shape[0 if last else 1]
        left = a[start : start + rows, :]
        for begin in range(0, width, 512):
            columns = slice(begin, begin + 512)
            term = dot_last(left, b[columns, :]) if last else dot(left, b[:, columns])
            out_ref[:, offset + begin : offset + begin + 512] = term.astype(out_ref.dtype)
        offset += width


def products(rows, items, *given, dtype=f32):
    width = sum(b.shape[0 if last else 1] for (_, last), b in zip(items, given[1::2], strict=True))
    out = jax.ShapeDtypeStruct((rows, width), dtype)
    return once(functools.partial(products_kernel, items), "products", 8, out, [], *given)


def hop_kernel(term_ref, first_ref, second_ref, ahead_ref, behind_ref):
    rows, half = ahead_ref.shape[0], first_ref.shape[0]
    ahead = term_ref[rows : rows + half, :].astype(f32) + first_ref[...].astype(f32)
    behind = term_ref[rows - half : rows, :].astype(f32) + second_ref[...].astype(f32)
    ahead_ref[:half, :] = ahead.astype(bf16)
    behind_ref[rows - half :, :] = behind.astype(bf16)
    if half < rows:
        ahead_ref[half:, :] = term_ref[rows + half :, :]
        behind_ref[: rows - half, :] = term_ref[: rows - half, :]


def hop(term, first, second):
    out = jax.ShapeDtypeStruct((term.shape[0] // 2, term.shape[1]), bf16)
    return once(hop_kernel, "hop", 8, (out, out), [], term, first, second)


def vectors_kernel(n, peers_ref, joined_ref, w_ref, local_ref, give_ref, shift_ref, gain_ref, two_ref, out_ref, turned):
    width = joined_ref.shape[1] // 3
    ones = jnp.ones((8, joined_ref.shape[0]), bf16)
    bias = dot(ones, joined_ref[...])[0:1]
    parts = []
    for _ in range(3):
        parts.append(bias.astype(bf16).astype(f32))
        bias = bias - parts[-1]
    shift = jnp.sum(dot_last(jnp.concatenate(parts, 0).astype(bf16), w_ref[...]), axis=0, keepdims=True)
    ones = jnp.ones((8, w_ref.shape[1]), bf16)
    half = w_ref.shape[0] // 2
    rows = []
    for start, ref in ((0, local_ref), (half, give_ref)):
        product = w_ref[start : start + half, :].astype(f32) * ref[...].astype(f32)
        upper = product.astype(bf16)
        lower = (product - upper.astype(f32)).astype(bf16)
        rows.append((dot_last(ones, upper) + dot_last(ones, lower))[0:1])
    both = jnp.concatenate([jnp.concatenate(rows, 1), shift], 0)
    for number in range(4):

        @pl.when(peers_ref[0] == number)
        def _(number=number):
            turned[...] = in_plain_order(both, number, n)

    out_ref[...] = jnp.zeros_like(out_ref)
    out_ref[0:1, :] = (turned[0:1, :] - shift_ref[...] * turned[1:2, :]) / gain_ref[...]
    out_ref[1:2, :] = turned[1:2, :]
    out_ref[2:4, :] = two_ref[...]
    total = sum(parts)
    for c in range(3):
        here = pl.ds(pl.multiple_of(peers_ref[1] * width, BLOCK), width)
        out_ref[4 + c : 5 + c, here] = total[:, c * width : (c + 1) * width]


def exchange(blocks):
    return [blocks[0]] + [swap(v, "seq", k) for k, v in enumerate(blocks) if k]


def local(kernel, name, out_shape, smem, given, anywhere=0, scratch=()):
    vmem = pl.BlockSpec(memory_space=pltpu.VMEM)
    many = isinstance(out_shape, (tuple, list))
    return pl.pallas_call(
        kernel,
        out_shape=out_shape,
        in_specs=[pl.BlockSpec(memory_space=pltpu.SMEM)]
        + [pl.BlockSpec(memory_space=pl.ANY)] * anywhere
        + [vmem] * (len(given) - anywhere),
        out_specs=[vmem] * len(out_shape) if many else vmem,
        scratch_shapes=list(scratch),
        compiler_params=pltpu.CompilerParams(vmem_limit_bytes=6 * 2**20),
        cost_estimate=BRIEF,
        name=name,
    )(smem, *given)


def cut_kernel(peers_ref, w_ref, place_ref, *refs):
    outs, semaphores = refs[:-1], refs[-1]
    extra, width = place_ref.shape[0], place_ref.shape[1] // 3
    share, model = outs[0].shape[0] - extra, w_ref.shape[1] // 3
    rows = pl.ds(pl.multiple_of(peers_ref[0] * share, share), share)
    copies = []
    for k, out in enumerate(outs):
        for c in range(3):
            columns = pl.ds(pl.multiple_of(c * model + peers_ref[1 + k] * width, BLOCK), width)
            copies.append(
                pltpu.make_async_copy(
                    w_ref.at[rows, columns],
                    out.at[pl.ds(0, share), pl.ds(c * width, width)],
                    semaphores.at[3 * k + c],
                )
            )
            copies[-1].start()
    for out in outs:
        out[share:, :] = place_ref[...]
    for copy in copies:
        copy.wait()


def cut(at, w, place, n):
    extra, columns = place.shape
    share, width = w.shape[0] // 4, columns // 3
    if width % BLOCK:
        mine = pick(w.reshape(4, share, 3 * width * n), at.quarter[0], 0).reshape(share, 3, n, width)
        mine = [pick(mine, at.seq ^ jnp.uint32(k), 2).reshape(share, columns) for k in range(n)]
        return [jnp.concatenate([v, place]) for v in mine]
    out = jax.ShapeDtypeStruct((share + extra, columns), bf16)
    return local(cut_kernel, "cut", [out] * n, at.peers, (w, place), 1, [pltpu.SemaphoreType.DMA((3 * n,))])


def stack_kernel(peers_ref, *refs):
    ins, (piece_ref, place_ref) = refs[:-2], refs[-2:]
    share = piece_ref.shape[0] // len(ins)
    tokens = place_ref.shape[1] // len(ins)
    for k, ref in enumerate(ins):
        peer = peers_ref[1 + k]
        piece_ref[pl.ds(pl.multiple_of(peer * share, share), share), :] = ref[:share, :]
        place = ref[share:, :tokens].astype(f32)
        place_ref[:, pl.ds(pl.multiple_of(peer * tokens, tokens), tokens)] = place[0:1] * 64.0 + place[1:2]


def stacked(at, blocks, extra, tokens):
    n, (rows, columns) = len(blocks), blocks[0].shape
    shapes = [
        jax.ShapeDtypeStruct((n * (rows - extra), columns), bf16),
        jax.ShapeDtypeStruct((1, n * tokens), f32),
    ]
    return local(stack_kernel, "stacked", shapes, at.peers, blocks)


def in_plain_order(x, number, n):
    share = x.shape[1] // (4 * n)
    order = [(q % 2) * 2 + q // 2 for q in (number ^ j for j in range(4))]
    starts = [order[j] * n * share + s * share for s in range(n) for j in range(4)]
    return jnp.concatenate([x[:, start : start + share] for start in starts], 1)


def last_back_kernel(
    n, peers_ref, term_ref, first_ref, second_ref, unit_ref, inverse_ref, gain_ref, grad_ref, middle_ref, out_ref, sum_ref
):
    total = term_ref[...] + first_ref[...].astype(f32) + second_ref[...].astype(f32)
    model = out_ref.shape[1]
    sum_ref[...] = (middle_ref[...] + total[:, model:]).astype(bf16)
    total = total[:, :model]
    for number in range(4):

        @pl.when(peers_ref[0] == number)
        def _(number=number):
            out_ref[...] = in_plain_order(total, number, n)

    out_ref[...] = grad_ref[...] + norm_back(out_ref[...], unit_ref[...], inverse_ref[...], gain_ref[...])


def beside_kernel(in_ref, out_ref):
    n, _, columns = in_ref.shape
    width = columns // 3
    for k in range(n):
        for c in range(3):
            start = (c * n + k) * width
            out_ref[:, start : start + width] = in_ref[k, :, c * width : (c + 1) * width]


def beside(v):
    n, rows, columns = v.shape
    return once(beside_kernel, "beside", 6, jax.ShapeDtypeStruct((rows, n * columns), bf16), [], v)


def halves_kernel(first_ref, second_ref, top_ref, bottom_ref):
    half = top_ref.shape[0]
    top_ref[...] = first_ref[:half, :]
    bottom_ref[...] = second_ref[half:, :]


def halves(first, second):
    half = jax.ShapeDtypeStruct((first.shape[0] // 2, first.shape[1]), first.dtype)
    vmem = pl.BlockSpec(memory_space=pltpu.VMEM)
    return pl.pallas_call(
        halves_kernel,
        out_shape=(half, half),
        in_specs=[vmem] * 2,
        out_specs=(vmem,) * 2,
        compiler_params=pltpu.CompilerParams(vmem_limit_bytes=4 * 2**20),
        cost_estimate=BRIEF,
        name="halves",
    )(first, second)


def hidden_kernel(at, tokens, cots, held, *refs):
    token_refs, refs = refs[:tokens], refs[tokens:]
    cot_refs, refs = refs[:cots], refs[cots:]
    gate_ref, up_ref, down_ref, refs = refs[0], refs[1], refs[2], refs[3 + held :]
    results, scratch, semaphores = refs[:5], refs[5:10], refs[10]
    rows = scratch[0].shape[0]
    copies = [
        pltpu.make_async_copy(v, out.at[pl.ds(at * rows, rows), :], semaphores.at[i])
        for i, (v, out) in enumerate(zip(scratch, results, strict=True))
    ]
    two, cot, hidden, grad_gate, grad_up = scratch
    two[...] = row_list(token_refs)
    copies[0].start()
    cot[...] = row_list(cot_refs)
    copies[1].start()
    units = gate_ref.shape[0]
    for start in range(0, units, TILE):
        here = slice(start, min(start + TILE, units))
        gate, up = dot_last(two[...], gate_ref[here, :]), dot_last(two[...], up_ref[here, :])
        grad_hidden = dot_last(cot[...], down_ref[here, :])
        sigmoid = 1.0 / (1.0 + jnp.exp(-gate))
        silu = gate * sigmoid
        hidden[:, here] = (silu * up).astype(bf16)
        grad_gate[:, here] = (grad_hidden * up * sigmoid * (1.0 + gate * (1.0 - sigmoid))).astype(bf16)
        grad_up[:, here] = (grad_hidden * silu).astype(bf16)
    for copy in copies[2:]:
        copy.start()
    for copy in copies:
        copy.wait()


def hidden_pair(at, pairs, tokens, cots, gate_rows, up_rows, w_down, held):
    rows = sum(b.shape[0] for b in tokens)
    units, model = gate_rows.shape
    widths = (model, model, units, units, units)
    first = len(tokens) + len(cots) + 3
    hbm = pl.BlockSpec(memory_space=pltpu.HBM)
    return pl.pallas_call(
        functools.partial(hidden_kernel, at, len(tokens), len(cots), len(held)),
        out_shape=[jax.ShapeDtypeStruct((rows * pairs, w), bf16) for w in widths],
        in_specs=[pl.BlockSpec(memory_space=pltpu.VMEM)] * first + [hbm] * len(held),
        out_specs=[hbm] * 5,
        scratch_shapes=[pltpu.VMEM((rows, w), bf16) for w in widths] + [pltpu.SemaphoreType.DMA((5,))],
        input_output_aliases={first + i: i for i in range(len(held))},
        compiler_params=pltpu.CompilerParams(vmem_limit_bytes=12 * 2**20),
        cost_estimate=BRIEF,
        name="hidden_pair",
    )(*tokens, *cots, gate_rows, up_rows, w_down, *held)


def place_kernel(at_ref, *refs):
    out_ref = refs[-1]
    for i, ref in enumerate(refs[:-1]):

        @pl.when(pl.program_id(0) == i)
        def _(ref=ref):
            out_ref[...] = ref[...].astype(f32)


def placed(at, pieces, axis):
    shape = list(pieces[0].shape)
    total = list(shape)
    total[axis] *= len(pieces)
    return pl.pallas_call(
        place_kernel,
        out_shape=jax.ShapeDtypeStruct(tuple(total), f32),
        grid_spec=pltpu.PrefetchScalarGridSpec(
            num_scalar_prefetch=1,
            grid=(len(pieces),),
            in_specs=[pl.BlockSpec(tuple(shape), lambda i, at: (0, 0)) for _ in pieces],
            out_specs=pl.BlockSpec(tuple(shape), lambda i, at: (0, at[i]) if axis else (at[i], 0)),
        ),
        compiler_params=pltpu.CompilerParams(vmem_limit_bytes=16 * 2**20),
        cost_estimate=BRIEF,
        name="placed",
    )(at, *pieces)


def on_device(
    inputs, positions, ln1_gain, ln1_bias, w_qkv, qkv_bias, w_out, ln2_gain, ln2_bias, w_gate, w_up, w_down, cotangent
):
    n = lax.axis_size("seq")
    ring = Ring("seq")
    line = Line()
    tokens, model = inputs.shape[0], inputs.shape[2]
    length = tokens * n
    pairs = n // 2
    width = model // n
    depth = w_qkv.shape[0]
    share = depth // 4
    x = inputs.reshape(tokens, model).astype(f32)
    cot = cotangent.reshape(tokens, model)
    gate_rows, up_rows = w_gate.T, w_up.T
    others = (0, 2, 1, 3)
    at = Places(model)
    at.tied(line(lambda *v: v, *at.scalars()))

    def other_y(v):
        return swap(v, "batch", 2)

    def other_core(v):
        return swap(v, "batch", 1)

    place = positions.reshape(tokens)
    extra = 16
    place = jnp.stack([place // 64, place % 64]).astype(bf16)
    place = jnp.pad(place, ((0, extra - 2), (0, 3 * width - tokens)))
    fetched = exchange(line(lambda w, place: cut(at, w, place, n), w_qkv, place))
    bias_heads = line(lambda v: pick(v.reshape(3, n, width), at.seq, 1).reshape(1, 3 * width), qkv_bias)

    def first_norm(x):
        normed, unit, inverse = norm_parts(x, ln1_gain, ln1_bias)
        normed = normed.astype(bf16).reshape(tokens, n, 4, share)
        normed = [pick(normed, at.quarter[k], 2).reshape(tokens, -1) for k in others]
        return jnp.concatenate(normed, 1), unit, inverse

    normed, unit_one, inverse_one = line(first_norm, x)
    normed_blocks = Gather(ring, line, after(normed, fetched[1]))

    piece, places = line(lambda *v: stacked(at, v, extra, tokens), *fetched)
    piece_y, piece_core = other_y(piece), other_core(piece)
    normed_blocks.step()

    def take(places, maps):
        maps = pick(maps, at.seq, 0)
        first = jnp.arange(length, dtype=jnp.int32)[None] - places.astype(jnp.int32)
        return maps, rotary_waves(places), first

    normed_blocks.step()
    ring.maps, waves, seen_from = line(take, places, ring.table)
    piece_core = line(lambda v: v, piece_core)
    for _ in range(pairs - 3):
        normed_blocks.step()
    piece_y = line(lambda v: v, piece_y)
    piece_both = other_core(piece_y)
    normed_blocks.step()
    cot_blocks = Gather(ring, line, cot)
    pieces = [piece, piece_y, piece_core, piece_both]
    all_normed, qkv, mixed, lse = line(
        lambda pieces: attend(ring.maps, normed_blocks.blocks, pieces, bias_heads, waves, seen_from), pieces
    )

    def block(v, i):
        return v[i * tokens : (i + 1) * tokens]

    class Scatter:
        def __init__(self, given, far, pair, own, fused=False):
            self.given, self.pair, self.own, self.fused = given, pair, own, fused
            top, bottom = line(lambda *v: halves(*[far(*v).astype(bf16)] * 2), *given)
            self.first, self.second = ring.up(top), ring.down(bottom)
            self.d = pairs - 1
            self.term = line(lambda *v: pair(self.d, *v), *given)

        def step(self):
            half = tokens // 2

            def add(term, first, second):
                first, second = first.astype(f32), second.astype(f32)
                if self.d == pairs - 1:
                    first = jnp.pad(first, ((0, half), (0, 0)))
                    second = jnp.pad(second, ((half, 0), (0, 0)))
                return (term[tokens:] + first).astype(bf16), (term[:tokens] + second).astype(bf16)

            if self.fused:
                first, second = line(hop, self.term, self.first, self.second)
            else:
                first, second = line(add, self.term, self.first, self.second)
            self.first, self.second = ring.up(first), ring.down(second)
            self.d -= 1
            self.term = line(lambda *v: self.pair(self.d, *v) if self.d else self.own(*v), *self.given)

        def parts(self):
            return self.term, self.first, self.second

        def finish(self):
            return line(lambda a, b, c: a + b.astype(f32) + c.astype(f32), *self.parts())

    def scattered(given, far, pair, own, fill, whole=True, fused=False):
        going = Scatter(given, far, pair, own, fused)
        for k in range(pairs):
            for work in fill[k] if k < len(fill) else ():
                work()
            if k < pairs - 1:
                going.step()
        return going.finish() if whole else going.parts()

    def pair_rows(v, d):
        return v[(2 * d - 1) * tokens : (2 * d + 1) * tokens]

    heads = {}

    def join_heads():
        heads["w"] = line(lambda *p: jnp.concatenate(p), *pieces)

    cot_step = cot_blocks.step
    branch = scattered(
        (mixed, w_out),
        lambda v, w: dot(block(v, n - 1), w),
        lambda d, v, w: dot(pair_rows(v, d), w),
        lambda v, w: dot(block(v, 0), w),
        [(cot_step,), (cot_step,), (cot_step,), (join_heads,)],
    )

    def second_norm(x, branch):
        middle = x + branch
        normed, unit, inverse = norm_parts(middle, ln2_gain, ln2_bias)
        return normed.astype(bf16), middle, unit, inverse

    normed_two, middle, unit_two, inverse_two = line(second_norm, x, branch)
    two_blocks = Gather(ring, line, normed_two)
    while len(cot_blocks.blocks) < n + 1:
        cot_blocks.step()
    held = []
    for d in range(1, pairs + 1):
        two_blocks.step()
        first, second = (v.blocks[2 * d - 1 : 2 * d + 1] for v in (two_blocks, cot_blocks))
        if d == pairs:
            first, second = [normed_two, *first], [cot, *second]
        held = line(
            lambda t, held, c=second, d=d: hidden_pair(d - 1, pairs, t, c, gate_rows, up_rows, w_down, held), first, held
        )
    all_two, all_cot, all_hidden, all_gate, all_up = held

    def last(v):
        return v[(n - 2) * tokens :]

    def ffn_rows(v, d):
        return v[2 * (d - 1) * tokens : 2 * d * tokens]

    def both(gate, up, gate_rows, up_rows):
        return dot(gate, gate_rows) + dot(up, up_rows)

    def quarter_one(units, rows, got):
        return (dot_rows(units, at.side(rows, "mine other", 4)) + at.side(got, "other").astype(f32)).astype(bf16)

    def quarter_two(units, rows, got, got_y):
        return (dot_rows(units, at.side(rows, "mine y", 4)) + at.side(got, "y").astype(f32) + got_y.astype(f32)).astype(bf16)

    class Reduced:
        def __init__(self, units, rows):
            self.units, self.rows = units, rows

        def one(self):
            self.got = other_core(line(lambda u, r: dot_rows(u, at.side(r, "across")).astype(bf16), self.units, self.rows))

        def two(self):
            self.got_y = other_y(line(quarter_one, self.units, self.rows, self.got))

        def three(self):
            piece = line(quarter_two, self.units, self.rows, self.got, self.got_y)
            self.pieces = [piece, other_y(piece), other_core(piece)]

        def four(self):
            self.pieces[1] = line(lambda v: v, self.pieces[1])
            self.pieces.append(other_core(self.pieces[1]))

        def five(self):
            self.out = line(lambda *p: placed(at.column_place, p, 1), *self.pieces)

    down, gate, up = Reduced(all_hidden, all_cot), Reduced(all_gate, all_two), Reduced(all_up, all_two)
    last_term = line(lambda g, u, *w: both(last(g), last(u), *w), all_gate, all_up, gate_rows, up_rows)
    grad_two = scattered(
        (last_term, all_gate, all_up, gate_rows, up_rows),
        lambda v, *_: v[tokens:],
        lambda d, _, g, u, *w: both(ffn_rows(g, d), ffn_rows(u, d), *w),
        lambda v, *_: v[:tokens],
        [(down.one, gate.one), (down.two,), (gate.two, up.one), (down.three,)],
    )

    def second_back(grad_two):
        grad_middle = cot.astype(f32) + norm_back(grad_two, unit_two, inverse_two, ln2_gain)
        sums = jnp.stack([jnp.sum(grad_two * unit_two, axis=0), jnp.sum(grad_two, axis=0)])
        return grad_middle, grad_middle.astype(bf16), sums

    grad_middle, grad_branch, two_grads = line(second_back, grad_two)

    branch_blocks = Gather(ring, line, grad_branch)
    fill = [(), (gate.three, down.four), (up.two,), (gate.four, down.five)]
    for k in range(pairs):
        for work in fill[k] if k < len(fill) else ():
            work()
        branch_blocks.step()
    grad_joined, outer = line(
        lambda w: attend_back(ring.maps, branch_blocks.blocks, w, qkv, mixed, lse, waves, seen_from), w_out
    )

    grad_w_out = {}

    def out_one():
        grad_w_out["mine"], give = line(lambda v: (at.side(v, "core"), at.side(v, "across").astype(bf16)), outer)
        grad_w_out["got"] = other_core(give)

    def out_two():
        def work(v, got):
            v = v + got.astype(f32)
            return at.side(v, "y"), at.side(v, "other").astype(bf16)

        grad_w_out["mine"], give = line(work, grad_w_out["mine"], grad_w_out["got"])
        grad_w_out["got"] = other_y(give)

    def out_three():
        v = line(lambda v, got: (v + got.astype(f32)).astype(bf16), grad_w_out["mine"], grad_w_out["got"])
        grad_w_out["pieces"] = [v, other_y(v), other_core(v)]

    qkv_grad = {}

    def qkv_one():
        give = line(lambda a, b: dot_rows(a[:, model // 2 :], b).astype(bf16), all_normed, grad_joined)
        qkv_grad["give"], qkv_grad["got"] = give, other_core(give)

    def qkv_local():
        qkv_grad["local"] = line(lambda a, b: dot_rows(a[:, : model // 2], b), all_normed, grad_joined)

    def qkv_two():
        def work(v, got):
            return (v[model // 4 :] + got[model // 4 :].astype(f32)).astype(bf16)

        qkv_grad["got_y"] = other_y(line(work, qkv_grad["local"], qkv_grad["got"]))

    def qkv_three():
        def work(v, got, got_y):
            return (v[: model // 4] + got[: model // 4].astype(f32) + got_y.astype(f32)).astype(bf16)

        piece = line(work, qkv_grad["local"], qkv_grad["got"], qkv_grad["got_y"])
        piece = piece.reshape(n, share, 3 * width)
        qkv_grad["back"] = lax.all_to_all(piece, "seq", split_axis=0, concat_axis=0, tiled=True)

    def to_rows():
        back = line(beside, qkv_grad["back"])
        qkv_grad["rows"], qkv_grad["back_y"], qkv_grad["back_core"] = back, other_y(back), other_core(back)

    def natural(v):
        v = v.reshape(-1, 4, n, share)
        v = [pick(v, at.order[j], 1) for j in range(4)]
        return jnp.stack(v, 2).reshape(-1, model)

    vectors = {}

    def sum_vectors():
        def plain(joined, w, local, give):
            bias = jnp.sum(joined.astype(f32), axis=0)
            w = w.astype(f32)
            shift = natural(jnp.sum(w * bias, axis=1))[0]
            rows = jnp.concatenate([local, give.astype(f32)])
            gain = (natural(jnp.sum(w * rows, axis=1))[0] - ln1_bias * shift) / ln1_gain
            bias_all = jnp.zeros((3, n, width), f32)
            start = (jnp.uint32(0), at.seq, jnp.uint32(0))
            bias_all = lax.dynamic_update_slice(bias_all, bias.reshape(3, 1, width), start).reshape(3, model)
            return jnp.concatenate([jnp.stack([gain, shift]), two_grads, bias_all, jnp.zeros((1, model), f32)])

        def work(*v):
            if share % HEAD_DIM:
                return plain(*v)
            out = jax.ShapeDtypeStruct((8, model), f32)
            kernel = functools.partial(vectors_kernel, n)
            scratch = [pltpu.VMEM((2, model), f32)]
            return once(kernel, "vectors", 16, out, scratch, *v, ln1_bias[None], ln1_gain[None], two_grads, maps=at.peers)

        v = line(work, grad_joined, heads["w"], qkv_grad["local"], qkv_grad["give"])
        vectors["sum"] = v
        vectors["hops"] = [[("batch", 1)], [("batch", 2)], [("seq", k) for k in (1, 2, 3) if k < n]]
        vectors["hops"] += [[("seq", bit)] for bit in bits_of(n)[2:]]
        vectors["other"] = [swap(v, *k) for k in vectors["hops"][0]]

    def vector_step():
        v = line(lambda a, *b: sum_in_order(a, b), vectors["sum"], *vectors["other"])
        vectors["sum"] = v
        vectors["hops"].pop(0)
        if vectors["hops"]:
            vectors["other"] = [swap(v, *k) for k in vectors["hops"][0]]

    def sum_in_order(a, b):
        if len(b) == 1:
            return a + b[0]
        return (a + b[0]) + (b[1] + b[2]) if len(b) == 3 else functools.reduce(jnp.add, b, a)

    def up_back():
        up.got_y = line(lambda v: v, up.got_y)

    def back_done():
        qkv_grad["back_y"] = line(lambda v: v, qkv_grad["back_y"])
        qkv_grad["back_both"] = other_core(qkv_grad["back_y"])

    def out_done():
        v = grad_w_out["pieces"]
        v[1] = line(lambda v: v, v[1])
        v.append(other_core(v[1]))

    def qkv_done():
        parts = (qkv_grad[k] for k in ("rows", "back_y", "back_core", "back_both"))
        qkv_grad["out"] = line(lambda *p: placed(at.row_place, p, 0), *parts)

    up_back()
    qkv_one()
    last = (n - 1) * tokens
    summed = scattered(
        (grad_joined, heads["w"], all_hidden, w_down),
        lambda *v: products(tokens, ((last, True), (last, False)), *v),
        lambda d, *v: products(
            2 * tokens, (((2 * d - 1) * tokens, True), (2 * (d - 1) * tokens, False)), *v, dtype=bf16
        ),
        lambda *v: products(tokens, ((0, True), (last - tokens, False)), *v),
        [
            (qkv_local, qkv_two, sum_vectors, up.three, gate.five, vector_step),
            (qkv_three, up.four, vector_step, out_one),
            (out_two, to_rows, out_three, up.five),
            (back_done, qkv_done),
        ],
        whole=False,
        fused=True,
    )

    def last_back(term, first, second):
        if share % HEAD_DIM:
            total = term + first.astype(f32) + second.astype(f32)
            back = grad_middle + norm_back(natural(total[:, :model]), unit_one, inverse_one, ln1_gain)
            return back, (middle + total[:, model:]).astype(bf16)
        given = term, first, second, unit_one, inverse_one, ln1_gain[None], grad_middle, middle
        out = jax.ShapeDtypeStruct((tokens, model), f32), jax.ShapeDtypeStruct((tokens, model), bf16)
        return once(functools.partial(last_back_kernel, n), "last_back", 10, out, [], *given, maps=at.peers)

    grad_input, output = line(last_back, *summed)
    vector_step()
    out_done()
    while vectors["hops"]:
        vector_step()
    grad_w_out = line(lambda *p: placed(at.column_place, p, 1), *grad_w_out["pieces"])
    gain_one_sum, bias_one_sum, gain_two_sum, bias_two_sum = (vectors["sum"][i] for i in range(4))
    qkv_bias_sum = vectors["sum"][4:7].reshape(-1)
    return (
        output.reshape(tokens, 1, model),
        grad_input.reshape(tokens, 1, model),
        gain_one_sum,
        bias_one_sum,
        qkv_grad["out"],
        qkv_bias_sum,
        grad_w_out,
        gain_two_sum,
        bias_two_sum,
        gate.out.T,
        up.out.T,
        down.out,
    )


def solution(mesh):
    token, shard, column, whole = P("seq", "batch", None), P("seq", None), P(None, "seq"), P()
    in_specs = (
        token, P("seq", "batch"), whole, whole, shard, whole, shard, whole, whole, column, column, shard, token
    )
    out_specs = (token, token, whole, whole, shard, whole, shard, whole, whole, column, column, shard)
    return jax.shard_map(on_device, mesh=mesh, in_specs=in_specs, out_specs=out_specs, check_vma=False)
```
